32 devices in a mesh: br: 2 (over x), seq: 8 (over z, y), ch: 2 (over core).
Axes of the slice: x: 2, y: 2, z: 4, core: 2. Of those that a mesh axis runs over, the one named last changes fastest.
Arguments:
- inputs: float32 [8192, 2048], P('seq'), may hold values from -6 to 6
- lengths: int32 [6], replicated, may hold values from 1 to 7168, as said below
- norm_gain1: bfloat16 [2048], P('seq'), may hold values from 0.5 to 1.5
- in_weight: bfloat16 [2, 2048, 2560], P('br', 'seq', 'ch'), may hold values from -0.125 to 0.125
- conv_weight: bfloat16 [4, 2, 2, 640], P(None, 'ch', 'br', 'seq'), may hold values from -3 to 3
- conv_bias: bfloat16 [2, 2, 640], P('ch', 'br', 'seq'), may hold values from -3 to 3
- gate_weight: bfloat16 [2, 2, 2, 4, 160, 160], P(None, 'ch', 'br', None, 'seq'), may hold values from -0.5 to 0.5
- gate_bias: bfloat16 [2, 2, 2, 640], P(None, 'ch', 'br', 'seq'), may hold values from -4 to 4
- decay_param: bfloat16 [2, 2, 640], P('ch', 'br', 'seq'), may hold values from 3 to 11
- out_weight: bfloat16 [2, 2, 640, 2048], P('ch', 'br', None, 'seq'), may hold values from -0.25 to 0.25
- norm_gain2: bfloat16 [2048], P('seq'), may hold values from 0.5 to 1.5
- mlp_in: bfloat16 [2, 2048, 6144], P(None, 'seq', ('br', 'ch')), may hold values from -0.125 to 0.125
- mlp_down: bfloat16 [6144, 2048], P(('br', 'ch'), 'seq'), may hold values from -0.15625 to 0.15625
- cotangent: float32 [8192, 2048], P('seq'), may hold values from -6 to 6
Outputs:
- output: float32 [8192, 2048], P('seq', ('br', 'ch'))
- inputs_grad: float32 [8192, 2048], P('seq')
- norm_gain1_grad: float32 [2048], P('seq')
- in_weight_grad: float32 [2, 2048, 2560], P('br', 'seq', 'ch')
- conv_weight_grad: float32 [4, 2, 2, 640], P(None, 'ch', 'br', 'seq')
- conv_bias_grad: float32 [2, 2, 640], P('ch', 'br', 'seq')
- gate_weight_grad: float32 [2, 2, 2, 4, 160, 160], P(None, 'ch', 'br', None, 'seq')
- gate_bias_grad: float32 [2, 2, 2, 640], P(None, 'ch', 'br', 'seq')
- decay_param_grad: float32 [2, 2, 640], P('ch', 'br', 'seq')
- out_weight_grad: float32 [2, 2, 640, 2048], P('ch', 'br', None, 'seq')
- norm_gain2_grad: float32 [2048], P('seq')
- mlp_in_grad: float32 [2, 2048, 6144], P(None, 'seq', ('br', 'ch'))
- mlp_down_grad: float32 [6144, 2048], P(('br', 'ch'), 'seq')
- decay_mean: float32 [2, 2, 640], P('ch', 'br', 'seq')
The draws below stay inside these ranges and needn't reach their ends.
Inputs may be any that keep to these rules, and one draw needn't show every extreme that they name: 6 positive lengths summing to 8192; one of them, neither the first nor the last, equals 7168.
All inputs are finite; a program needn't handle non-finite values.
Results may differ from the reference program's by a relative error of at most 0.011.
Values may be sent and summed in bfloat16 or wider, within the bound.
No kernel may reach another device: no remote copies, remote signals or barrier semaphores. Data moves between devices by JAX's collectives and lax.ppermute only.
A program may use at most 320 MiB of HBM per device.

```python
from functools import partial
import jax
import jax.numpy as jnp
from jax import lax

D = 2048
R = 2560
HEADS = 16
FF = 6144
CONV = 4
TOK_DEV = 1024
NDOC = 6
TOKENS = 8192
BLOCK = 160
CHD = 640
HD = 4
N_BR = 2
N_CH = 2


def draw_lengths(key, part):
    key = jax.random.fold_in(key, 7)
    cut_key, place_key = jax.random.split(key)
    shuffled = jax.random.permutation(cut_key, TOK_DEV - 1) + 1
    cut_points = jnp.sort(shuffled[:NDOC - 2]).astype(jnp.int32)
    boundaries = jnp.concatenate([jnp.zeros((1,), jnp.int32), cut_points, jnp.full((1,), TOK_DEV, jnp.int32)])
    short_lengths = boundaries[1:] - boundaries[:-1]
    long_index = jax.random.randint(place_key, (), 1, NDOC - 1)
    slot_index = jnp.arange(NDOC)
    before_len = short_lengths[jnp.minimum(slot_index, NDOC - 2)]
    after_len = short_lengths[jnp.maximum(slot_index - 1, 0)]
    long_length = TOKENS - TOK_DEV
    return jnp.where(slot_index < long_index, before_len, jnp.where(slot_index == long_index, long_length, after_len)).astype(jnp.int32)


def levels(own_key, extent, cuts, smallest, top_value):
    loudness = 1.0
    for dim, parts in cuts:
        draws = jax.random.uniform(jax.random.fold_in(jax.random.fold_in(own_key, 6), dim), (parts,), jnp.float32, smallest / len(cuts), top_value / len(cuts))
        loudness = loudness * jnp.repeat(jnp.exp(draws), extent[dim] // parts).reshape((-1,) + (1,) * (len(extent) - 1 - dim))
    return loudness


def centred(key, shape, scale, bound, cuts=(), kind=jnp.bfloat16):
    level = levels(key, shape, cuts, -0.22, 0.18) if cuts else 1.0
    array = jax.random.normal(key, shape, jnp.float32) * scale * level
    return jnp.minimum(jnp.maximum(array, -bound), bound).astype(kind)


def setup_inputs(seed: int = 0) -> dict:
    keys = jax.random.split(jax.random.key(seed), 15)
    return {
        "inputs": centred(keys[0], (TOKENS, D), 1.0, 6.0, ((0, 8),), jnp.float32),
        "lengths": draw_lengths(jax.random.fold_in(keys[14], 71), 0),
        "norm_gain1": jnp.clip(1.0 + 0.1 * jax.random.normal(keys[2], (D,), jnp.float32), 0.5, 1.5).astype(jnp.bfloat16),
        "in_weight": centred(keys[3], (2, D, R), D ** -0.5, 0.125, ((0, 2), (1, 8), (2, 2))),
        "conv_weight": centred(keys[4], (CONV, N_CH, N_BR, CHD), CONV ** -0.5, 3.0, ((1, 2), (2, 2), (3, 8))),
        "conv_bias": centred(keys[5], (N_CH, N_BR, CHD), 0.5, 3.0, ((0, 2), (1, 2), (2, 8))),
        "gate_weight": centred(keys[6], (2, N_CH, N_BR, HD, BLOCK, BLOCK), BLOCK ** -0.5, 0.5, ((1, 2), (2, 2), (4, 8))),
        "gate_bias": centred(keys[7], (2, N_CH, N_BR, CHD), 1.0, 4.0, ((1, 2), (2, 2), (3, 8))),
        "decay_param": jnp.clip(3.0 + 8.0 * jax.random.uniform(keys[8], (N_CH, N_BR, CHD), jnp.float32) ** levels(keys[8], (N_CH, N_BR, CHD), ((0, 2), (1, 2), (2, 8)), -0.2, 0.2), 3.0, 11.0).astype(jnp.bfloat16),
        "out_weight": centred(keys[9], (N_CH, N_BR, CHD, D), (R // 4) ** -0.5, 0.25, ((0, 2), (1, 2), (3, 8))),
        "norm_gain2": jnp.clip(1.0 + 0.1 * jax.random.normal(keys[10], (D,), jnp.float32), 0.5, 1.5).astype(jnp.bfloat16),
        "mlp_in": centred(keys[11], (2, D, FF), D ** -0.5, 0.125, ((1, 8), (2, 4))),
        "mlp_down": centred(keys[12], (FF, D), (FF // 4) ** -0.5, 0.15625, ((0, 4), (1, 8))),
        "cotangent": centred(keys[13], (TOKENS, D), 1.0, 6.0, ((0, 8),), jnp.float32),
    }


NORM_EPS = 1e-06
DECAY_SCALE = 8.0

@jax.custom_vjp
def low(v):
    return lax.optimization_barrier(v.astype(jnp.bfloat16)).astype(jnp.float32)

@jax.custom_vjp
def low_back(v):
    return v

def low_keep(v):
    return (low(v), None)

def low_pass(kept, grad):
    return (grad,)

def back_keep(v):
    return (v, None)

def back_low(kept, grad):
    return (low(grad),)
low.defvjp(low_keep, low_pass)
low_back.defvjp(back_keep, back_low)

def matmul_high(left, right):
    return jnp.dot(left, right, precision=lax.Precision.HIGHEST, preferred_element_type=jnp.float32)

def rms_normed(values):
    return values * lax.rsqrt(lax.optimization_barrier(jnp.mean(values * values, axis=1, keepdims=True)) + NORM_EPS)

def linear_combine(earlier, later):
    return (earlier[0] * later[0], later[0] * earlier[1] + later[1])

def gated_input(gate_pre, unit_val, decay_rate, at_reset):
    rec_gate = jax.nn.sigmoid(gate_pre[0])
    in_gate = jax.nn.sigmoid(gate_pre[1])
    log_decay = -DECAY_SCALE * rec_gate * jax.nn.softplus(-decay_rate)
    keep_val = jnp.where(at_reset, jnp.float32(0.0), jnp.exp(log_decay))
    norm_scale = jnp.where(at_reset, jnp.float32(1.0), jnp.sqrt(-jnp.expm1(2.0 * log_decay)))
    return (keep_val, norm_scale * in_gate * unit_val)

def block_forward(inputs, gain_one, in_weight, conv_weight, conv_bias, gate_weight, gate_bias, decay_param, out_weight, gain_two, mlp_in, mlp_down, doc_ids, at_reset):
    row_count = inputs.shape[0]
    conv_span = CONV - 1
    block_size = R // HEADS
    h_one = low(rms_normed(inputs) * gain_one)
    z_gate = low_back(low(matmul_high(h_one, in_weight[0])))
    z_rec = low_back(low(matmul_high(h_one, in_weight[1])))
    conv_w = conv_weight.reshape(CONV, R)
    padded = jnp.pad(z_rec, ((conv_span, 0), (0, 0)))
    doc_pad = jnp.pad(doc_ids, (conv_span, 0), constant_values=-1)
    conv_sum = jnp.broadcast_to(conv_bias.reshape(R), (row_count, R))
    for lag_index in range(CONV):
        lo_row = conv_span - lag_index
        lag_valid = (doc_pad[lo_row:lo_row + row_count] == doc_ids).astype(jnp.float32)[:, None]
        conv_sum = conv_sum + conv_w[lag_index] * padded[lo_row:lo_row + row_count] * lag_valid
    unit_val = low(conv_sum)
    gate_pre = jnp.einsum('thi,ghij->gthj', unit_val.reshape(row_count, HEADS, block_size), gate_weight.reshape(2, HEADS, block_size, block_size), precision=lax.Precision.HIGHEST).reshape(2, row_count, R) + gate_bias.reshape(2, 1, R)
    gate_pre = low_back(gate_pre)
    decay_rate = decay_param.reshape(R)
    carry_keep, drive_term = gated_input(gate_pre, unit_val, decay_rate, at_reset)
    keep_prod, state_val = lax.associative_scan(linear_combine, (carry_keep, drive_term), axis=0)
    decay_mean = lax.optimization_barrier(jnp.mean(jnp.exp(-DECAY_SCALE * jax.nn.sigmoid(gate_pre[0]) * jax.nn.softplus(-decay_rate)), axis=0))
    mixed_low = low(jax.nn.gelu(z_gate) * state_val)
    resid_one = inputs + low_back(matmul_high(mixed_low, out_weight.reshape(R, D)))
    h_two = low(rms_normed(resid_one) * gain_two)
    gate_val = low_back(matmul_high(h_two, mlp_in[0]))
    up_val = low_back(matmul_high(h_two, mlp_in[1]))
    hidden_low = low(jax.nn.gelu(gate_val) * up_val)
    output = resid_one + low_back(matmul_high(hidden_low, mlp_down))
    return (output, decay_mean.reshape(N_CH, N_BR, R // (N_CH * N_BR)))

def reference(inputs, lengths, norm_gain1, in_weight, conv_weight, conv_bias, gate_weight, gate_bias, decay_param, out_weight, norm_gain2, mlp_in, mlp_down, cotangent):
    doc_starts = (jnp.cumsum(lengths) - lengths).astype(jnp.int32)
    positions = jnp.arange(inputs.shape[0], dtype=jnp.int32)
    doc_ids = lax.optimization_barrier(jnp.sum((positions[:, None] >= doc_starts[None, 1:]).astype(jnp.int32), axis=1)).astype(jnp.int32)
    at_reset = jnp.any(positions[:, None] == doc_starts[None, :], axis=1)[:, None]
    params = tuple((param_arg.astype(jnp.float32) for param_arg in (norm_gain1, in_weight, conv_weight, conv_bias, gate_weight, gate_bias, decay_param, out_weight, norm_gain2, mlp_in, mlp_down)))
    forward_part = partial(block_forward, doc_ids=doc_ids, at_reset=at_reset)
    output, pull_back, decay_mean = jax.vjp(forward_part, inputs, *params, has_aux=True)
    grads = pull_back(cotangent)
    return (output, grads[0], grads[1], grads[2], grads[3], grads[4], grads[5], grads[6], grads[7], grads[8], grads[9], grads[10], grads[11], decay_mean)
```

```python
import functools

import jax
import jax.numpy as jnp
from jax import lax
from jax.experimental import pallas as pl
from jax.experimental.pallas import tpu as pltpu
from jax.sharding import PartitionSpec as P

NORM_EPS = 1e-06
DECAY_SCALE = 8.0
GELU_C = 0.7978845608028654
GELU_K = 0.044715
LANES = 128
ROWS = 128
SWAP = [(0, 1), (1, 0)]
F32 = jnp.float32
BF16 = jnp.bfloat16


def ring_order(count):
    return list(range(0, count, 2)) + list(range(count - 1, 0, -2))


def ring_place(index, count):
    half = index // 2
    return jnp.where(index % 2 == 0, half, count - 1 - half)


class Ring:
    def __init__(self, count, depth=2):
        order = ring_order(count)
        self.count = count
        self.pairs = {
            1: [(order[i], order[(i + 1) % count]) for i in range(count)],
            -1: [(order[(i + 1) % count], order[i]) for i in range(count)],
        }
        self.done = {1: [], -1: []}
        self.depth = depth

    def hop(self, x, way):
        done = self.done[way]
        if len(done) >= self.depth:
            x, _ = lax.optimization_barrier((x, done[-self.depth]))
        got = lax.ppermute(x, "seq", self.pairs[way])
        done.append(got)
        return got

    def gather(self, x):
        n = self.count
        parts = [None] * n
        parts[0] = x
        ahead = behind = x
        for step in range(1, n // 2):
            ahead = self.hop(ahead, 1)
            behind = self.hop(behind, -1)
            parts[n - step] = ahead
            parts[step] = behind
        cut = x.shape[0] // 2
        far = [self.hop(ahead[:cut], 1), self.hop(behind[cut:], -1)]
        parts[n // 2] = jnp.concatenate(far, axis=0)
        return parts

    def scatter(self, part):
        n = self.count
        half = n // 2
        far = part(half)
        cut = far.shape[0] // 2
        ahead = self.hop(far[:cut].astype(BF16), 1)
        behind = self.hop(far[cut:].astype(BF16), -1)
        for step in range(1, half):
            up, down = part(half - step), part(half + step)
            if step == 1:
                up = jnp.concatenate([up[:cut] + ahead.astype(F32), up[cut:]], axis=0)
                down = jnp.concatenate([down[:cut], down[cut:] + behind.astype(F32)], axis=0)
            else:
                up = up + ahead.astype(F32)
                down = down + behind.astype(F32)
            ahead = self.hop(up.astype(BF16), 1)
            behind = self.hop(down.astype(BF16), -1)
        return part(0) + (ahead.astype(F32) + behind.astype(F32))


def group_sum(part):
    half = part.shape[0] // 2
    core = lax.axis_index("ch")
    mine = lax.dynamic_slice_in_dim(part, core * half, half, 0)
    theirs = lax.dynamic_slice_in_dim(part, (1 - core) * half, half, 0)
    chip = (mine.astype(F32) + lax.ppermute(theirs, "ch", SWAP).astype(F32)).astype(BF16)
    both = (chip.astype(F32) + lax.ppermute(chip, "br", SWAP).astype(F32)).astype(BF16)
    other = lax.ppermute(both, "ch", SWAP)
    first = core == 0
    return jnp.concatenate([jnp.where(first, both, other), jnp.where(first, other, both)], axis=0)


def tiny_group_sum(x):
    x = x + lax.ppermute(x, "ch", SWAP)
    return x + lax.ppermute(x, "br", SWAP)


def entering(pair, reverse):
    count, index = lax.axis_size("seq"), lax.axis_index("seq")
    spread = jnp.broadcast_to(pair[None], (count,) + pair.shape)
    every = lax.all_to_all(spread, "seq", 0, 0, tiled=True)
    value = jnp.zeros(pair.shape[1:], F32)
    for k in range(count):
        at = count - 1 - k if reverse else k
        new = every[at, 1] + every[at, 0] * value
        value = jnp.where((at > index) if reverse else (at < index), new, value)
    return value


def gelu_both(x):
    square = x * x
    bent = jnp.tanh(GELU_C * (x + GELU_K * (x * square)))
    half = 0.5 * (1.0 + bent)
    slope = half + 0.5 * x * (1.0 - bent * bent) * (GELU_C * (1.0 + 3.0 * GELU_K * square))
    return x * half, slope


def minus_expm1(x, exp_x):
    series = 1.0 + x * (1.0 / 6.0)
    for k in (5.0, 4.0, 3.0, 2.0):
        series = 1.0 + x * (1.0 / k) * series
    return jnp.where(x > -0.2, -x * series, 1.0 - exp_x)


def scan_rows(keep, add, reverse):
    rows = keep.shape[0]
    at = lax.broadcasted_iota(jnp.int32, keep.shape, 0)
    step = 1
    while step < rows:
        shift = rows - step if reverse else step
        inside = (at < rows - step) if reverse else (at >= step)
        far_add = jnp.where(inside, pltpu.roll(add, shift, 0), 0.0)
        add = add + keep * far_add
        keep = keep * jnp.where(inside, pltpu.roll(keep, shift, 0), 1.0)
        step *= 2
    return keep, add


def forward_kernel(
    z_ref, rim_ref, mask_ref, conv_ref, wide_ref, bias_ref, rate_ref,
    unit_ref, gate_ref, loc_ref, prod_ref, last_ref, total_ref, ext,
):
    block = pl.program_id(0)
    rows, channels = z_ref.shape
    span = conv_ref.shape[0] - 2

    @pl.when(block == 0)
    def _():
        ext[0:8] = rim_ref[...]
        last_ref[0:1] = jnp.ones((1, channels), F32)
        last_ref[1:8] = jnp.zeros((7, channels), F32)
        total_ref[...] = jnp.zeros_like(total_ref)

    @pl.when(block > 0)
    def _():
        ext[0:8] = ext[rows : rows + 8]

    ext[8 : rows + 8] = z_ref[...].astype(F32)
    conv = jnp.broadcast_to(conv_ref[span + 1 : span + 2], (rows, channels))
    for lag in range(span + 1):
        conv = conv + conv_ref[lag : lag + 1] * ext[8 - lag : 8 - lag + rows] * mask_ref[:, lag : lag + 1]
    unit_ref[...] = conv.astype(BF16)
    pre = jnp.dot(unit_ref[...], wide_ref[...], preferred_element_type=F32) + bias_ref[...]
    gate_ref[...] = jax.nn.sigmoid(pre)
    reset = mask_ref[:, span + 1 : span + 2] > 0.5
    for lane in range(0, channels, LANES):
        own = slice(lane, lane + LANES)
        in_gate = gate_ref[:, channels + lane : channels + lane + LANES]
        log_decay = gate_ref[:, own] * rate_ref[0:1, own]
        decay = jnp.exp(log_decay)
        scale = jnp.sqrt(minus_expm1(2.0 * log_decay, decay * decay))
        total_ref[0:1, own] += jnp.sum(decay, axis=0, keepdims=True)
        keep = jnp.where(reset, 0.0, decay)
        drive = jnp.where(reset, 1.0, scale) * in_gate * unit_ref[:, own].astype(F32)
        prod, loc = scan_rows(keep, drive, False)
        loc = loc + prod * last_ref[1:2, own]
        prod = prod * last_ref[0:1, own]
        loc_ref[:, own] = loc
        prod_ref[:, own] = prod
        last_ref[0:1, own] = prod[rows - 1 :]
        last_ref[1:2, own] = loc[rows - 1 :]


def adjoint_kernel(
    dmix_ref, zg_ref, loc_ref, prod_ref, gate_ref, mask_ref, enter_ref, rate_ref,
    adj_ref, tail_ref, dzg_ref, head_ref, after,
):
    step = pl.program_id(0)
    rows, channels = zg_ref.shape
    reset_col = mask_ref.shape[1] - 1

    @pl.when(step == 0)
    def _():
        head_ref[0:1] = jnp.ones((1, channels), F32)
        head_ref[1:8] = jnp.zeros((7, channels), F32)
        after[0:2] = jnp.ones((2, channels), F32)
        after[2:8] = jnp.zeros((6, channels), F32)

    reset = mask_ref[:, 4:5] > 0.5
    for lane in range(0, channels, LANES):
        own = slice(lane, lane + LANES)
        state = loc_ref[:, own] + prod_ref[:, own] * enter_ref[0:1, own]
        act, slope = gelu_both(zg_ref[:, own].astype(F32))
        dmix = dmix_ref[:, own].astype(F32)
        dzg_ref[:, own] = (dmix * state * slope).astype(BF16)
        keep = jnp.where(reset, 0.0, jnp.exp(gate_ref[:, own] * rate_ref[0:1, own]))
        at = lax.broadcasted_iota(jnp.int32, keep.shape, 0)
        nxt = jnp.where(at == rows - 1, after[0:1, own], pltpu.roll(keep, rows - 1, 0))
        tail, adj = scan_rows(nxt, dmix * act, True)
        adj = adj + tail * after[2:3, own]
        tail = tail * after[1:2, own]
        adj_ref[:, own] = adj
        tail_ref[:, own] = tail
        after[0:1, own] = keep[0:1]
        after[1:2, own] = tail[0:1]
        after[2:3, own] = adj[0:1]
        head_ref[0:1, own] = keep[0:1] * tail[0:1]
        head_ref[1:2, own] = keep[0:1] * adj[0:1]


def backward_kernel(
    adj_ref, tail_ref, arrive_ref, loc_ref, prod_ref, loc0_ref, prod0_ref, enter_ref, gate_ref,
    unit_ref, mask_ref, z_ref, z0_ref, rim_ref, conv_ref, wide_ref, rate_ref,
    dz_ref, gw_ref, sums_ref, edge_ref, dpre, ddir, zext, moved,
):
    step = pl.program_id(0)
    block = pl.num_programs(0) - 1 - step
    rows, channels = z_ref.shape
    span = conv_ref.shape[0] - 2

    @pl.when(step == 0)
    def _():
        gw_ref[...] = jnp.zeros_like(gw_ref)
        sums_ref[...] = jnp.zeros_like(sums_ref)
        moved[...] = jnp.zeros_like(moved)

    @pl.when(step > 0)
    def _():
        for lag in range(1, span + 1):
            moved[lag - 1, rows : rows + 8] = moved[lag - 1, 0:8]

    zext[8 : rows + 8] = z_ref[...].astype(F32)

    @pl.when(block == 0)
    def _():
        zext[0:8] = rim_ref[...]

    @pl.when(block > 0)
    def _():
        zext[0:8] = z0_ref[8:16].astype(F32)

    reset = mask_ref[:, 4:5] > 0.5
    for lane in range(0, channels, LANES):
        own = slice(lane, lane + LANES)
        two = slice(channels + lane, channels + lane + LANES)
        enter = enter_ref[0:1, own]
        adj = adj_ref[:, own] + tail_ref[:, own] * arrive_ref[0:1, own]
        state = loc_ref[:, own] + prod_ref[:, own] * enter
        before = jnp.where(block == 0, enter, loc0_ref[7:8, own] + prod0_ref[7:8, own] * enter)
        at = lax.broadcasted_iota(jnp.int32, state.shape, 0)
        previous = jnp.where(at == 0, before, pltpu.roll(state, 1, 0))
        rec_gate, in_gate = gate_ref[:, own], gate_ref[:, two]
        unit = unit_ref[:, own].astype(F32)
        rate = rate_ref[0:1, own]
        log_decay = rec_gate * rate
        decay = jnp.exp(log_decay)
        scale = jnp.sqrt(minus_expm1(2.0 * log_decay, decay * decay))
        dlog = decay * (adj * previous - adj * in_gate * unit * (decay / scale))
        dlog = jnp.where(reset, 0.0, dlog)
        sums_ref[0:1, own] += jnp.sum(dlog * rec_gate, axis=0, keepdims=True)
        scale = jnp.where(reset, 1.0, scale)
        dpre[:, own] = (dlog * rate * (rec_gate * (1.0 - rec_gate))).astype(BF16)
        through = adj * scale
        dpre[:, two] = (through * unit * (in_gate * (1.0 - in_gate))).astype(BF16)
        ddir[:, own] = through * in_gate

    gw_ref[...] += lax.dot_general(
        unit_ref[...], dpre[...], (((0,), (0,)), ((), ())), preferred_element_type=F32
    )
    dconv_all = ddir[...] + lax.dot_general(
        dpre[...], wide_ref[...], (((1,), (1,)), ((), ())), preferred_element_type=F32
    )
    ddir[...] = dconv_all
    for lane in range(0, channels, LANES):
        own = slice(lane, lane + LANES)
        two = slice(channels + lane, channels + lane + LANES)
        dconv = ddir[:, own]
        sums_ref[1:2, own] += jnp.sum(dpre[:, own].astype(F32), axis=0, keepdims=True)
        sums_ref[2:3, own] += jnp.sum(dpre[:, two].astype(F32), axis=0, keepdims=True)
        sums_ref[3:4, own] += jnp.sum(dconv, axis=0, keepdims=True)
        sums_ref[4:5, own] += jnp.sum(dconv * zext[8 : 8 + rows, own], axis=0, keepdims=True)
        dz = dconv * conv_ref[0:1, own]
        edge = jnp.zeros((8, LANES), F32)
        at8 = lax.broadcasted_iota(jnp.int32, edge.shape, 0)
        for lag in range(1, span + 1):
            kept = dconv * mask_ref[:, lag : lag + 1]
            sums_ref[4 + lag : 5 + lag, own] += jnp.sum(
                kept * zext[8 - lag : 8 - lag + rows, own], axis=0, keepdims=True
            )
            moved[lag - 1, 0:rows, own] = kept * conv_ref[lag : lag + 1, own]
            dz = dz + moved[lag - 1, lag : lag + rows, own]
            edge = edge + jnp.where(
                at8 >= 8 - lag, pltpu.roll(moved[lag - 1, 0:8, own], 8 - lag, 0), 0.0
            )
        dz_ref[:, own] = dz.astype(BF16)
        edge_ref[0:8, own] = edge

        @pl.when(step == 0)
        def _():
            edge_ref[8:16, own] = dz[rows - 8 :]


def kernel_params():
    return pltpu.CompilerParams(
        dimension_semantics=("arbitrary",), vmem_limit_bytes=48 * 1024 * 1024
    )


def forward_local(z, rim, mask, conv, wide, bias, rate):
    tokens, channels = z.shape[0], rate.shape[1]
    rows = min(ROWS, tokens)
    spec = lambda shape, index: pl.BlockSpec(shape, index)
    whole = lambda x: pl.BlockSpec(x.shape, lambda i: (0,) * x.ndim)
    time = lambda width, at=0: pl.BlockSpec((rows, width), lambda i: (i, at))
    fixed = pl.BlockSpec((8, channels), lambda i: (0, 0))
    return pl.pallas_call(
        forward_kernel,
        grid=(tokens // rows,),
        in_specs=[time(channels, 1), whole(rim), time(mask.shape[1]), whole(conv), whole(wide), whole(bias), whole(rate)],
        out_specs=[time(channels), time(2 * channels), time(channels), time(channels), fixed, fixed],
        out_shape=[
            jax.ShapeDtypeStruct((tokens, channels), BF16),
            jax.ShapeDtypeStruct((tokens, 2 * channels), F32),
            jax.ShapeDtypeStruct((tokens, channels), F32),
            jax.ShapeDtypeStruct((tokens, channels), F32),
            jax.ShapeDtypeStruct((8, channels), F32),
            jax.ShapeDtypeStruct((8, channels), F32),
        ],
        scratch_shapes=[pltpu.VMEM((rows + 8, channels), F32)],
        compiler_params=kernel_params(),
    )(z, rim, mask, conv, wide, bias, rate)


def adjoint_local(dmix, z, loc, prod, gate, mask, enter, rate):
    tokens, channels = loc.shape
    rows = min(ROWS, tokens)
    last = tokens // rows - 1
    whole = lambda x: pl.BlockSpec(x.shape, lambda i: (0,) * x.ndim)
    time = lambda width: pl.BlockSpec((rows, width), lambda i: (last - i, 0))
    return pl.pallas_call(
        adjoint_kernel,
        grid=(tokens // rows,),
        in_specs=[time(channels)] * 5 + [time(mask.shape[1]), whole(enter), whole(rate)],
        out_specs=[time(channels)] * 3 + [pl.BlockSpec((8, channels), lambda i: (0, 0))],
        out_shape=[
            jax.ShapeDtypeStruct((tokens, channels), F32),
            jax.ShapeDtypeStruct((tokens, channels), F32),
            jax.ShapeDtypeStruct((tokens, channels), BF16),
            jax.ShapeDtypeStruct((8, channels), F32),
        ],
        scratch_shapes=[pltpu.VMEM((8, channels), F32)],
        compiler_params=kernel_params(),
    )(dmix, z, loc, prod, gate, mask, enter, rate)


def backward_local(adj, tail, arrive, loc, prod, enter, gate, unit, mask, z, rim, conv, wide, rate):
    tokens, channels = loc.shape
    rows = min(ROWS, tokens)
    last = tokens // rows - 1
    whole = lambda x: pl.BlockSpec(x.shape, lambda i: (0,) * x.ndim)
    time = lambda width, at=0: pl.BlockSpec((rows, width), lambda i: (last - i, at))
    ahead = lambda size, at=0: pl.BlockSpec(
        (size, channels), lambda i: (jnp.maximum((last - i) * (rows // size) - 1, 0), at)
    )
    fixed = lambda size, width: pl.BlockSpec((size, width), lambda i: (0, 0))
    span = conv.shape[0] - 2
    return pl.pallas_call(
        backward_kernel,
        grid=(tokens // rows,),
        in_specs=[
            time(channels), time(channels), whole(arrive), time(channels), time(channels), ahead(8), ahead(8),
            whole(enter), time(2 * channels), time(channels), time(mask.shape[1]), time(channels, 1), ahead(16, 1),
            whole(rim), whole(conv), whole(wide), whole(rate),
        ],
        out_specs=[time(channels), fixed(channels, 2 * channels), fixed(16, channels), fixed(16, channels)],
        out_shape=[
            jax.ShapeDtypeStruct((tokens, channels), BF16),
            jax.ShapeDtypeStruct((channels, 2 * channels), F32),
            jax.ShapeDtypeStruct((16, channels), F32),
            jax.ShapeDtypeStruct((16, channels), F32),
        ],
        scratch_shapes=[
            pltpu.VMEM((rows, 2 * channels), BF16),
            pltpu.VMEM((rows, channels), F32),
            pltpu.VMEM((rows + 8, channels), F32),
            pltpu.VMEM((span, rows + 8, channels), F32),
        ],
        compiler_params=kernel_params(),
    )(adj, tail, arrive, loc, prod, loc, prod, enter, gate, unit, mask, z, z, rim, conv, wide, rate)


def pad_rows(x, rows, before=False):
    extra = rows - x.shape[0]
    return jnp.pad(x, ((extra, 0) if before else (0, extra), (0, 0)))


def per_device(
    inputs,
    lengths,
    norm_gain1,
    in_weight,
    conv_weight,
    conv_bias,
    gate_weight,
    gate_bias,
    decay_param,
    out_weight,
    norm_gain2,
    mlp_in,
    mlp_down,
    cotangent,
):
    tokens, width = inputs.shape
    count, index = lax.axis_size("seq"), lax.axis_index("seq")
    br, ch = lax.axis_index("br"), lax.axis_index("ch")
    place = ring_place(index, count)
    order = jnp.asarray(ring_order(count), jnp.int32)
    cols = width // count
    taps = conv_weight.shape[0]
    span = taps - 1
    part_ch = conv_weight.shape[3]
    channels = part_ch * count
    heads, part_in, block = gate_weight.shape[3], gate_weight.shape[4], gate_weight.shape[5]
    true_of = [order[(place + k) % count] for k in range(count)]
    ring_of = [(ring_place(jnp.int32(s), count) - place) % count for s in range(count)]

    def to_ring(x):
        return jnp.concatenate(
            [lax.dynamic_slice_in_dim(x, true_of[k] * cols, cols, 1) for k in range(count)], axis=1
        )

    def from_ring(x):
        return jnp.concatenate(
            [lax.dynamic_slice_in_dim(x, ring_of[s] * cols, cols, 1) for s in range(count)], axis=1
        )

    ring = Ring(count)

    small = jnp.concatenate(
        [
            norm_gain1,
            norm_gain2,
            conv_weight.reshape(-1),
            conv_bias.reshape(-1),
            gate_bias.reshape(-1),
            decay_param.reshape(-1),
        ]
    )
    fold = 2 * block
    small_rows = -(-small.shape[0] // fold)
    small = jnp.pad(small, (0, small_rows * fold - small.shape[0])).reshape(small_rows, fold)
    gate_rows = heads * part_in
    packed = jnp.concatenate(
        [gate_weight[:, 0, 0].transpose(1, 2, 0, 3).reshape(gate_rows, fold), small], axis=0
    )
    packed = pad_rows(packed, -(-packed.shape[0] // 32) * 32)
    packed_all = ring.gather(packed)

    own_cols = lax.dynamic_slice_in_dim(in_weight[0], br * channels, channels, 1)
    far_cols = lax.ppermute(
        lax.dynamic_slice_in_dim(in_weight[0], (1 - br) * channels, channels, 1), "br", SWAP
    )
    w_in_own = jnp.concatenate(
        [jnp.where(br == 0, own_cols, far_cols), jnp.where(br == 0, far_cols, own_cols)], axis=1
    )
    w_in = ring.gather(w_in_own)
    w_out = ring.gather(out_weight[0, 0])
    w_mlp = ring.gather(mlp_in)
    w_down = ring.gather(mlp_down)

    doc_starts = jnp.cumsum(lengths) - lengths
    positions = jnp.arange(tokens + span, dtype=jnp.int32) + index * tokens - span
    doc_ext = jnp.sum((positions[:, None] >= doc_starts[None, 1:]).astype(jnp.int32), axis=1)
    lags = [
        (doc_ext[span - lag : span - lag + tokens] == doc_ext[span:]).astype(F32) for lag in range(taps)
    ]
    reset = jnp.any(positions[span:, None] == doc_starts[None, :], axis=1).astype(F32)
    mask = jnp.stack(lags + [reset], axis=1)

    small_all = jnp.stack([part[gate_rows : gate_rows + small_rows].reshape(-1) for part in packed_all])
    gain_one = small_all[:, :cols].astype(F32).reshape(1, width)
    gain_two = small_all[:, cols : 2 * cols].astype(F32).reshape(1, width)
    ring_index = jnp.stack(ring_of)
    place_hot = (ring_index[:, None] == jnp.arange(count)[None, :]).astype(BF16)
    chan = jnp.dot(place_hot, small_all[:, 2 * cols :], preferred_element_type=F32)
    chan = chan[:, : (taps + 4) * part_ch].reshape(count, taps + 4, part_ch)
    chan = chan.transpose(1, 0, 2).reshape(taps + 4, channels)
    conv = chan[: taps + 1]
    gate_bias_all = chan[taps + 1 : taps + 3].reshape(1, 2 * channels)
    decay_rate = chan[taps + 3 : taps + 4]
    rate = -DECAY_SCALE * jax.nn.softplus(-decay_rate)

    stacked = jnp.concatenate([part[:gate_rows] for part in packed_all], axis=0)
    row = jnp.arange(channels)
    row_head, row_in = row // block, row % block
    source = ring_index[row_in // part_in] * gate_rows + row_head * part_in + row_in % part_in
    row_hot = (source[:, None] == jnp.arange(channels)[None, :]).astype(BF16)
    wide_col = jnp.arange(2 * channels)
    wide_gate, wide_head, wide_out = (
        wide_col // channels,
        (wide_col % channels) // block,
        wide_col % block,
    )
    spread_hot = (jnp.arange(fold)[:, None] == (wide_gate * block + wide_out)[None, :]).astype(BF16)
    on_block = (row_head[:, None] == wide_head[None, :]).astype(BF16)
    compact = jnp.dot(row_hot, stacked, preferred_element_type=F32).astype(BF16)
    wide = jnp.dot(compact, spread_hot, preferred_element_type=F32).astype(BF16) * on_block

    x_in = to_ring(inputs)
    rstd_one = lax.rsqrt(jnp.mean(x_in * x_in, axis=1, keepdims=True) + NORM_EPS)
    h_one = (x_in * rstd_one * gain_one).astype(BF16)
    z = jnp.dot(h_one, jnp.concatenate(w_in, axis=0), preferred_element_type=F32).astype(BF16)

    forward_pairs = [(i, i + 1) for i in range(count - 1)]
    rim = lax.ppermute(z[tokens - 8 :, channels:], "seq", forward_pairs).astype(F32)
    unit, gates, loc, prod, last, total = forward_local(z, rim, mask, conv, wide, gate_bias_all, rate)
    enter = entering(last[:2], False)[None]
    act = jax.nn.gelu(z[:, :channels].astype(F32))
    mixed = (act * (loc + prod * enter)).astype(BF16)

    w_out_all = jnp.concatenate(w_out, axis=1)
    attn = group_sum(jnp.dot(mixed, w_out_all, preferred_element_type=F32).astype(BF16))
    resid = x_in + attn.astype(F32)
    rstd_two = lax.rsqrt(jnp.mean(resid * resid, axis=1, keepdims=True) + NORM_EPS)
    h_two = (resid * rstd_two * gain_two).astype(BF16)

    w_mlp_all = jnp.concatenate(w_mlp, axis=1)
    gate_up = jnp.einsum("td,gdf->gtf", h_two, w_mlp_all, preferred_element_type=F32)
    act_gate, act_slope = gelu_both(gate_up[0])
    hidden = (act_gate * gate_up[1]).astype(BF16)
    cot = to_ring(cotangent)
    d_mlp = cot.astype(BF16)

    def chunk(x, k):
        return x[:, k * cols : (k + 1) * cols]

    g_down = ring.scatter(
        lambda k: lax.dot_general(
            hidden, chunk(d_mlp, k), (((0,), (0,)), ((), ())), preferred_element_type=F32
        )
    )
    w_down_all = jnp.concatenate(w_down, axis=1)
    d_hidden = jnp.einsum("td,fd->tf", d_mlp, w_down_all, preferred_element_type=F32)
    d_gate_up = jnp.stack([d_hidden * gate_up[1] * act_slope, d_hidden * act_gate]).astype(BF16)
    g_mlp = ring.scatter(
        lambda k: jnp.einsum("td,gtf->gdf", chunk(h_two, k), d_gate_up, preferred_element_type=F32)
    )
    d_h_two = group_sum(
        jnp.einsum("gtf,gdf->td", d_gate_up, w_mlp_all, preferred_element_type=F32).astype(BF16)
    ).astype(F32)

    mlp_part = jnp.dot(hidden, w_down_all, preferred_element_type=F32).astype(BF16)
    per = width // 4 // cols

    def columns(x, b, c):
        first = (b * 2 + c) * per
        at = [(ring_place(first + j, count) - place) % count for j in range(per)]
        return jnp.concatenate([lax.dynamic_slice_in_dim(x, a * cols, cols, 1) for a in at], axis=1)

    mine = jnp.concatenate([columns(mlp_part, b, ch) for b in range(2)], axis=1)
    theirs = jnp.concatenate([columns(mlp_part, b, 1 - ch) for b in range(2)], axis=1)
    chip = mine.astype(F32) + lax.ppermute(theirs, "ch", SWAP).astype(F32)
    own = lax.dynamic_slice_in_dim(chip, br * (width // 4), width // 4, 1)
    far = lax.dynamic_slice_in_dim(chip, (1 - br) * (width // 4), width // 4, 1).astype(BF16)
    output = columns(resid, br, ch) + own + lax.ppermute(far, "br", SWAP).astype(F32)

    normed_two = resid * rstd_two
    g_gain_two = jnp.sum(d_h_two * normed_two, axis=0)
    d_normed = d_h_two * gain_two
    d_resid = cot + rstd_two * (d_normed - normed_two * jnp.mean(d_normed * normed_two, axis=1, keepdims=True))
    d_attn = d_resid.astype(BF16)
    g_out = ring.scatter(
        lambda k: lax.dot_general(
            mixed, chunk(d_attn, k), (((0,), (0,)), ((), ())), preferred_element_type=F32
        )
    )
    d_mixed = jnp.einsum("td,kd->tk", d_attn, w_out_all, preferred_element_type=F32)

    adj, tail, d_z_gate, head = adjoint_local(d_mixed, z, loc, prod, gates, mask, enter, rate)
    arrive = entering(head[:2], True)[None]
    d_z_rec, g_wide, sums, edge = backward_local(
        adj, tail, arrive, loc, prod, enter, gates, unit, mask, z, rim, conv, wide, rate
    )
    backward_pairs = [(i + 1, i) for i in range(count - 1)]
    from_next = lax.ppermute(edge[:8], "seq", backward_pairs)
    fixed = (edge[8:] + from_next).astype(BF16)
    d_z_rec = jnp.concatenate([d_z_rec[: tokens - 8], fixed], axis=0)
    d_z = jnp.concatenate([d_z_gate, d_z_rec], axis=1)

    w_in_all = jnp.concatenate(w_in, axis=0)
    g_in = ring.scatter(
        lambda k: lax.dot_general(
            chunk(h_one, k), d_z, (((0,), (0,)), ((), ())), preferred_element_type=F32
        )
    )
    keep_half = lax.dynamic_slice_in_dim(g_in, br * channels, channels, 1)
    send_half = lax.dynamic_slice_in_dim(g_in, (1 - br) * channels, channels, 1).astype(BF16)
    got_half = lax.ppermute(send_half, "br", SWAP).astype(F32)
    g_in = jnp.concatenate(
        [jnp.where(br == 0, keep_half, got_half), jnp.where(br == 0, got_half, keep_half)], axis=1
    )
    d_h_part = lax.dot_general(d_z, w_in_all, (((1,), (1,)), ((), ())), preferred_element_type=F32)
    d_h_one = group_sum(d_h_part.astype(BF16)).astype(F32)
    normed_one = x_in * rstd_one
    g_gain_one = jnp.sum(d_h_one * normed_one, axis=0)
    d_normed = d_h_one * gain_one
    inputs_grad = from_ring(
        d_resid + rstd_one * (d_normed - normed_one * jnp.mean(d_normed * normed_one, axis=1, keepdims=True))
    )

    g_compact = lax.dot_general(
        (g_wide * on_block.astype(F32)).astype(BF16),
        spread_hot,
        (((1,), (1,)), ((), ())),
        preferred_element_type=F32,
    ).astype(BF16)
    g_gates = lax.dot_general(row_hot, g_compact, (((0,), (0,)), ((), ())), preferred_element_type=F32)
    g_decay = sums[0:1] * -DECAY_SCALE * -jax.nn.sigmoid(-decay_rate)
    g_chan = jnp.concatenate([sums[4 : 4 + taps], sums[3:4], sums[1:3], g_decay, total[0:1]], axis=0)
    g_chan = g_chan.reshape(taps + 5, count, part_ch).transpose(1, 0, 2).reshape(count, -1)
    g_chan = lax.dot_general(
        place_hot.astype(F32), g_chan, (((0,), (0,)), ((), ())), precision=lax.Precision.HIGHEST
    )
    g_small = jnp.concatenate(
        [g_gain_one.reshape(count, cols), g_gain_two.reshape(count, cols), g_chan], axis=1
    )
    g_rows = -(-g_small.shape[1] // fold)
    g_small = jnp.pad(g_small, ((0, 0), (0, g_rows * fold - g_small.shape[1]))).reshape(count, g_rows, fold)
    g_packed = jnp.concatenate([g_gates.reshape(count, gate_rows, fold), g_small], axis=1)
    total_rows = -(-g_packed.shape[1] // 32) * 32
    g_packed = jnp.pad(g_packed, ((0, 0), (0, total_rows - g_packed.shape[1]), (0, 0)))
    g_own = ring.scatter(lambda k: g_packed[k])
    g_gate_w = g_own[:gate_rows].reshape(heads, part_in, 2, block).transpose(2, 0, 1, 3)[:, None, None]
    g_flat = g_own[gate_rows : gate_rows + g_rows].reshape(-1)
    g_gain_one, g_gain_two = g_flat[:cols], g_flat[cols : 2 * cols]
    g_chan = g_flat[2 * cols : 2 * cols + (taps + 5) * part_ch].reshape(taps + 5, part_ch)
    return (
        output,
        inputs_grad,
        g_gain_one,
        g_in[None],
        g_chan[:taps][:, None, None],
        g_chan[taps][None, None],
        g_gate_w,
        g_chan[taps + 1 : taps + 3][:, None, None],
        g_chan[taps + 3][None, None],
        g_out[None, None],
        g_gain_two,
        g_mlp,
        g_down,
        g_chan[taps + 4][None, None] / (tokens * count),
    )


def solution(mesh):
    placed = (
        P("seq", None),
        P(),
        P("seq"),
        P("br", "seq", "ch"),
        P(None, "ch", "br", "seq"),
        P("ch", "br", "seq"),
        P(None, "ch", "br", None, "seq", None),
        P(None, "ch", "br", "seq"),
        P("ch", "br", "seq"),
        P("ch", "br", None, "seq"),
        P("seq"),
        P(None, "seq", ("br", "ch")),
        P(("br", "ch"), "seq"),
        P("seq", None),
    )
    return jax.shard_map(
        per_device,
        mesh=mesh,
        in_specs=placed,
        out_specs=(
            P("seq", ("br", "ch")),
            P("seq", None),
            P("seq"),
            P("br", "seq", "ch"),
            P(None, "ch", "br", "seq"),
            P("ch", "br", "seq"),
            P(None, "ch", "br", None, "seq", None),
            P(None, "ch", "br", "seq"),
            P("ch", "br", "seq"),
            P("ch", "br", None, "seq"),
            P("seq"),
            P(None, "seq", ("br", "ch")),
            P(("br", "ch"), "seq"),
            P("ch", "br", "seq"),
        ),
        check_vma=False,
    )
```

```python
import functools

import jax
import jax.numpy as jnp
from jax import lax
from jax.experimental import pallas as pl
from jax.experimental.pallas import tpu as pltpu
from jax.sharding import PartitionSpec as P

NORM_EPS = 1e-06
DECAY_SCALE = 8.0
GELU_C = 0.7978845608028654
GELU_K = 0.044715
LANES = 128
ROWS = 128
SWAP = [(0, 1), (1, 0)]
F32 = jnp.float32
BF16 = jnp.bfloat16
COST = pl.CostEstimate(flops=0, bytes_accessed=0, transcendentals=0)


def after(x, *others):
    if not others:
        return x
    return lax.optimization_barrier((x,) + others)[0]


def ring_order(count):
    return list(range(0, count, 2)) + list(range(count - 1, 0, -2))


def ring_place(index, count):
    half = index // 2
    return jnp.where(index % 2 == 0, half, count - 1 - half)


class Ring:
    def __init__(self, count, depth=3):
        order = ring_order(count)
        self.count = count
        self.half = count // 2
        self.reps = max(1, self.half // 4)
        self.pairs = {
            1: [(order[i], order[(i + 1) % count]) for i in range(count)],
            -1: [(order[(i + 1) % count], order[i]) for i in range(count)],
        }
        self.done = {1: [], -1: []}
        self.depth = depth
        self.mark = ()

    def hop(self, x, way, free=False):
        if not free:
            held = self.done[way]
            others = self.mark + tuple(held[-self.depth :][:1] if len(held) >= self.depth else ())
            if others:
                x = after(x, *others)
        got = lax.ppermute(x, "seq", self.pairs[way])
        if not free:
            self.done[way].append(got)
        return got


class Gather:
    def __init__(self, ring, x, free=False):
        self.ring, self.free = ring, free
        self.parts = [None] * ring.count
        self.parts[0] = x
        self.last = (x, x)
        self.step = 0

    def pieces(self):
        far = self.ring.half
        every = [(part, k, None) for k, part in enumerate(self.parts) if k != far]
        return every + [(self.last[0], far, 0), (self.last[1], far, 1)]

    def hop(self):
        ring = self.ring
        for _ in range(ring.reps):
            self.step += 1
            ahead, behind = self.last
            if self.step < ring.half:
                self.last = (ring.hop(ahead, 1, self.free), ring.hop(behind, -1, self.free))
                self.parts[ring.count - self.step], self.parts[self.step] = self.last
            else:
                cut = ahead.shape[0] // 2
                self.last = (
                    ring.hop(ahead[:cut], 1, self.free),
                    ring.hop(behind[cut:], -1, self.free),
                )
                self.parts[ring.half] = jnp.concatenate(self.last, axis=0)


class Scatter:
    def __init__(self, ring, part, free=False):
        self.ring, self.part, self.free = ring, part, free
        self.last = None
        self.step = 0

    def hop(self):
        ring = self.ring
        for _ in range(ring.reps):
            self.step += 1
            mark = () if self.free else ring.mark
            if self.step == 1:
                far = self.part(ring.half, *mark)
                self.cut = cut = far.shape[0] // 2
                up, down = far[:cut], far[cut:]
            else:
                ahead, behind = (x.astype(F32) for x in self.last)
                cut, at = self.cut, self.step - 1
                up = self.part(ring.half - at, *mark, self.last[0])
                down = self.part(ring.half + at, *mark, self.last[1])
                if at == 1:
                    up = jnp.concatenate([up[:cut] + ahead, up[cut:]], axis=0)
                    down = jnp.concatenate([down[:cut], down[cut:] + behind], axis=0)
                else:
                    up, down = up + ahead, down + behind
            self.last = (
                ring.hop(up.astype(BF16), 1, self.free),
                ring.hop(down.astype(BF16), -1, self.free),
            )

    def result(self):
        return self.part(0, *self.last) + (self.last[0].astype(F32) + self.last[1].astype(F32))


class TokenSum:
    def second(self, mine, others):
        got = lax.ppermute(others, "ch", SWAP)
        self.chip = (mine.astype(F32) + got.astype(F32)).astype(BF16)

    def cross(self, *others):
        self.far = lax.ppermute(after(self.chip, *others), "br", SWAP)

    def first(self, mine, others):
        self.own = mine
        self.core = lax.ppermute(others, "ch", SWAP)


class TokenGather:
    def __init__(self, own):
        self.own = own
        self.far = lax.ppermute(own, "br", SWAP)
        self.core = lax.ppermute(own, "ch", SWAP)
        self.far_core = lax.ppermute(self.far, "ch", SWAP)

    def parts(self):
        return [self.own, self.core, self.far, self.far_core]


def tiny_group_sum(x):
    x = x + lax.ppermute(x, "ch", SWAP)
    return x + lax.ppermute(x, "br", SWAP)


def entering(pair, reverse):
    count, index = lax.axis_size("seq"), lax.axis_index("seq")
    spread = jnp.broadcast_to(pair[None], (count,) + pair.shape)
    every = lax.all_to_all(spread, "seq", 0, 0, tiled=True)
    value = jnp.zeros(pair.shape[1:], F32)
    for k in range(count):
        at = count - 1 - k if reverse else k
        new = every[at, 1] + every[at, 0] * value
        value = jnp.where((at > index) if reverse else (at < index), new, value)
    return value


def gelu_both(x):
    square = x * x
    bent = jnp.tanh(GELU_C * (x + GELU_K * (x * square)))
    half = 0.5 * (1.0 + bent)
    slope = half + 0.5 * x * (1.0 - bent * bent) * (GELU_C * (1.0 + 3.0 * GELU_K * square))
    return x * half, slope


def minus_expm1(x, exp_x):
    series = 1.0 + x * (1.0 / 6.0)
    for k in (5.0, 4.0, 3.0, 2.0):
        series = 1.0 + x * (1.0 / k) * series
    return jnp.where(x > -0.2, -x * series, 1.0 - exp_x)


def scan_rows(keep, add, reverse):
    rows = keep.shape[0]
    at = lax.broadcasted_iota(jnp.int32, keep.shape, 0)
    step = 1
    while step < rows:
        shift = rows - step if reverse else step
        inside = (at < rows - step) if reverse else (at >= step)
        far_add = jnp.where(inside, pltpu.roll(add, shift, 0), 0.0)
        add = add + keep * far_add
        keep = keep * jnp.where(inside, pltpu.roll(keep, shift, 0), 1.0)
        step *= 2
    return keep, add


def forward_kernel(
    z_ref, rim_ref, mask_ref, conv_ref, wide_ref, bias_ref, rate_ref,
    unit_ref, gate_ref, loc_ref, prod_ref, last_ref, total_ref, ext,
):
    block = pl.program_id(0)
    rows, channels = z_ref.shape
    span = conv_ref.shape[0] - 2

    @pl.when(block == 0)
    def _():
        ext[0:8] = rim_ref[...]
        last_ref[0:1] = jnp.ones((1, channels), F32)
        last_ref[1:8] = jnp.zeros((7, channels), F32)
        total_ref[...] = jnp.zeros_like(total_ref)

    @pl.when(block > 0)
    def _():
        ext[0:8] = ext[rows : rows + 8]

    ext[8 : rows + 8] = z_ref[...].astype(F32)
    conv = jnp.broadcast_to(conv_ref[span + 1 : span + 2], (rows, channels))
    for lag in range(span + 1):
        conv = conv + conv_ref[lag : lag + 1] * ext[8 - lag : 8 - lag + rows] * mask_ref[:, lag : lag + 1]
    unit_ref[...] = conv.astype(BF16)
    pre = jnp.dot(unit_ref[...], wide_ref[...], preferred_element_type=F32) + bias_ref[...]
    gate_ref[...] = jax.nn.sigmoid(pre)
    reset = mask_ref[:, span + 1 : span + 2] > 0.5
    for lane in range(0, channels, LANES):
        own = slice(lane, lane + LANES)
        in_gate = gate_ref[:, channels + lane : channels + lane + LANES]
        log_decay = gate_ref[:, own] * rate_ref[0:1, own]
        decay = jnp.exp(log_decay)
        scale = jnp.sqrt(minus_expm1(2.0 * log_decay, decay * decay))
        total_ref[0:1, own] += jnp.sum(decay, axis=0, keepdims=True)
        keep = jnp.where(reset, 0.0, decay)
        drive = jnp.where(reset, 1.0, scale) * in_gate * unit_ref[:, own].astype(F32)
        prod, loc = scan_rows(keep, drive, False)
        loc = loc + prod * last_ref[1:2, own]
        prod = prod * last_ref[0:1, own]
        loc_ref[:, own] = loc
        prod_ref[:, own] = prod
        last_ref[0:1, own] = prod[rows - 1 :]
        last_ref[1:2, own] = loc[rows - 1 :]


def adjoint_body(
    where, weight, d_ref, z_ref, loc_ref, prod_ref, gate_ref, mask_ref, enter_ref, rate_ref,
    adj_ref, tail_ref, dzg_ref, head_ref, dmix_ref, after,
):
    step = pl.program_id(0)
    rows, channels = loc_ref.shape
    dmix_ref[...] = lax.dot_general(d_ref[...], weight[...], NT, preferred_element_type=F32)

    @pl.when(step == 0)
    def _():
        head_ref[0:1] = jnp.ones((1, channels), F32)
        head_ref[1:8] = jnp.zeros((7, channels), F32)
        after[0:2] = jnp.ones((2, channels), F32)
        after[2:8] = jnp.zeros((6, channels), F32)

    reset = mask_ref[:, 4:5] > 0.5
    for lane in range(0, channels, LANES):
        own = slice(lane, lane + LANES)
        state = loc_ref[:, own] + prod_ref[:, own] * enter_ref[0:1, own]
        act, slope = gelu_both(z_ref[:, own].astype(F32))
        dmix = dmix_ref[:, own]
        dzg_ref[:, own] = (dmix * state * slope).astype(BF16)
        keep = jnp.where(reset, 0.0, jnp.exp(gate_ref[:, own] * rate_ref[0:1, own]))
        at = lax.broadcasted_iota(jnp.int32, keep.shape, 0)
        nxt = jnp.where(at == rows - 1, after[0:1, own], pltpu.roll(keep, rows - 1, 0))
        tail, adj = scan_rows(nxt, dmix * act, True)
        adj = adj + tail * after[2:3, own]
        tail = tail * after[1:2, own]
        adj_ref[:, own] = adj
        tail_ref[:, own] = tail
        after[0:1, own] = keep[0:1]
        after[1:2, own] = tail[0:1]
        after[2:3, own] = adj[0:1]
        head_ref[0:1, own] = keep[0:1] * tail[0:1]
        head_ref[1:2, own] = keep[0:1] * adj[0:1]


def backward_kernel(
    adj_ref, tail_ref, arrive_ref, loc_ref, prod_ref, loc0_ref, prod0_ref, enter_ref, gate_ref,
    unit_ref, mask_ref, z_ref, z0_ref, rim_ref, conv_ref, wide_ref, rate_ref,
    dz_ref, gw_ref, sums_ref, edge_ref, dpre, ddir, zext, moved,
):
    step = pl.program_id(0)
    block = pl.num_programs(0) - 1 - step
    rows, channels = z_ref.shape
    span = conv_ref.shape[0] - 2

    @pl.when(step == 0)
    def _():
        gw_ref[...] = jnp.zeros_like(gw_ref)
        sums_ref[...] = jnp.zeros_like(sums_ref)
        moved[...] = jnp.zeros_like(moved)

    @pl.when(step > 0)
    def _():
        for lag in range(1, span + 1):
            moved[lag - 1, rows : rows + 8] = moved[lag - 1, 0:8]

    zext[8 : rows + 8] = z_ref[...].astype(F32)

    @pl.when(block == 0)
    def _():
        zext[0:8] = rim_ref[...]

    @pl.when(block > 0)
    def _():
        zext[0:8] = z0_ref[8:16].astype(F32)

    reset = mask_ref[:, 4:5] > 0.5
    for lane in range(0, channels, LANES):
        own = slice(lane, lane + LANES)
        two = slice(channels + lane, channels + lane + LANES)
        enter = enter_ref[0:1, own]
        adj = adj_ref[:, own] + tail_ref[:, own] * arrive_ref[0:1, own]
        state = loc_ref[:, own] + prod_ref[:, own] * enter
        before = jnp.where(block == 0, enter, loc0_ref[7:8, own] + prod0_ref[7:8, own] * enter)
        at = lax.broadcasted_iota(jnp.int32, state.shape, 0)
        previous = jnp.where(at == 0, before, pltpu.roll(state, 1, 0))
        rec_gate, in_gate = gate_ref[:, own], gate_ref[:, two]
        unit = unit_ref[:, own].astype(F32)
        rate = rate_ref[0:1, own]
        log_decay = rec_gate * rate
        decay = jnp.exp(log_decay)
        scale = jnp.sqrt(minus_expm1(2.0 * log_decay, decay * decay))
        dlog = decay * (adj * previous - adj * in_gate * unit * (decay / scale))
        dlog = jnp.where(reset, 0.0, dlog)
        sums_ref[0:1, own] += jnp.sum(dlog * rec_gate, axis=0, keepdims=True)
        scale = jnp.where(reset, 1.0, scale)
        dpre[:, own] = (dlog * rate * (rec_gate * (1.0 - rec_gate))).astype(BF16)
        through = adj * scale
        dpre[:, two] = (through * unit * (in_gate * (1.0 - in_gate))).astype(BF16)
        ddir[:, own] = through * in_gate

    gw_ref[...] += lax.dot_general(
        unit_ref[...], dpre[...], (((0,), (0,)), ((), ())), preferred_element_type=F32
    )
    dconv_all = ddir[...] + lax.dot_general(
        dpre[...], wide_ref[...], (((1,), (1,)), ((), ())), preferred_element_type=F32
    )
    ddir[...] = dconv_all
    for lane in range(0, channels, LANES):
        own = slice(lane, lane + LANES)
        two = slice(channels + lane, channels + lane + LANES)
        dconv = ddir[:, own]
        sums_ref[1:2, own] += jnp.sum(dpre[:, own].astype(F32), axis=0, keepdims=True)
        sums_ref[2:3, own] += jnp.sum(dpre[:, two].astype(F32), axis=0, keepdims=True)
        sums_ref[3:4, own] += jnp.sum(dconv, axis=0, keepdims=True)
        sums_ref[4:5, own] += jnp.sum(dconv * zext[8 : 8 + rows, own], axis=0, keepdims=True)
        dz = dconv * conv_ref[0:1, own]
        edge = jnp.zeros((8, LANES), F32)
        at8 = lax.broadcasted_iota(jnp.int32, edge.shape, 0)
        for lag in range(1, span + 1):
            kept = dconv * mask_ref[:, lag : lag + 1]
            sums_ref[4 + lag : 5 + lag, own] += jnp.sum(
                kept * zext[8 - lag : 8 - lag + rows, own], axis=0, keepdims=True
            )
            moved[lag - 1, 0:rows, own] = kept * conv_ref[lag : lag + 1, own]
            dz = dz + moved[lag - 1, lag : lag + rows, own]
            edge = edge + jnp.where(
                at8 >= 8 - lag, pltpu.roll(moved[lag - 1, 0:8, own], 8 - lag, 0), 0.0
            )
        dz_ref[:, own] = dz.astype(BF16)
        edge_ref[0:8, own] = edge

        @pl.when(step == 0)
        def _():
            edge_ref[8:16, own] = dz[rows - 8 :]


def kernel_params():
    return pltpu.CompilerParams(
        dimension_semantics=("arbitrary",), vmem_limit_bytes=48 * 1024 * 1024
    )


def forward_local(z, rim, mask, conv, wide, bias, rate):
    tokens, channels = z.shape[0], rate.shape[1]
    rows = min(ROWS, tokens)
    spec = lambda shape, index: pl.BlockSpec(shape, index)
    whole = lambda x: pl.BlockSpec(x.shape, lambda i: (0,) * x.ndim)
    time = lambda width, at=0: pl.BlockSpec((rows, width), lambda i: (i, at))
    fixed = pl.BlockSpec((8, channels), lambda i: (0, 0))
    return pl.pallas_call(
        forward_kernel,
        grid=(tokens // rows,),
        in_specs=[time(channels, 1), whole(rim), time(mask.shape[1]), whole(conv), whole(wide), whole(bias), whole(rate)],
        out_specs=[time(channels), time(2 * channels), time(channels), time(channels), fixed, fixed],
        out_shape=[
            jax.ShapeDtypeStruct((tokens, channels), BF16),
            jax.ShapeDtypeStruct((tokens, 2 * channels), F32),
            jax.ShapeDtypeStruct((tokens, channels), F32),
            jax.ShapeDtypeStruct((tokens, channels), F32),
            jax.ShapeDtypeStruct((8, channels), F32),
            jax.ShapeDtypeStruct((8, channels), F32),
        ],
        scratch_shapes=[pltpu.VMEM((rows + 8, channels), F32)],
        compiler_params=kernel_params(),
        cost_estimate=COST,
    )(z, rim, mask, conv, wide, bias, rate)


def backward_local(adj, tail, arrive, loc, prod, enter, gate, unit, mask, z, rim, conv, wide, rate):
    tokens, channels = loc.shape
    rows = min(ROWS, tokens)
    last = tokens // rows - 1
    whole = lambda x: pl.BlockSpec(x.shape, lambda i: (0,) * x.ndim)
    time = lambda width, at=0: pl.BlockSpec((rows, width), lambda i: (last - i, at))
    ahead = lambda size, at=0: pl.BlockSpec(
        (size, channels), lambda i: (jnp.maximum((last - i) * (rows // size) - 1, 0), at)
    )
    fixed = lambda size, width: pl.BlockSpec((size, width), lambda i: (0, 0))
    span = conv.shape[0] - 2
    return pl.pallas_call(
        backward_kernel,
        grid=(tokens // rows,),
        in_specs=[
            time(channels), time(channels), whole(arrive), time(channels), time(channels), ahead(8), ahead(8),
            whole(enter), time(2 * channels), time(channels), time(mask.shape[1]), time(channels, 1), ahead(16, 1),
            whole(rim), whole(conv), whole(wide), whole(rate),
        ],
        out_specs=[time(channels), fixed(channels, 2 * channels), fixed(16, channels), fixed(16, channels)],
        out_shape=[
            jax.ShapeDtypeStruct((tokens, channels), BF16),
            jax.ShapeDtypeStruct((channels, 2 * channels), F32),
            jax.ShapeDtypeStruct((16, channels), F32),
            jax.ShapeDtypeStruct((16, channels), F32),
        ],
        scratch_shapes=[
            pltpu.VMEM((rows, 2 * channels), BF16),
            pltpu.VMEM((rows, channels), F32),
            pltpu.VMEM((rows + 8, channels), F32),
            pltpu.VMEM((span, rows + 8, channels), F32),
        ],
        compiler_params=kernel_params(),
        cost_estimate=COST,
    )(adj, tail, arrive, loc, prod, loc, prod, enter, gate, unit, mask, z, z, rim, conv, wide, rate)


def pad_rows(x, rows, before=False):
    extra = rows - x.shape[0]
    return jnp.pad(x, ((extra, 0) if before else (0, extra), (0, 0)))


def pieces_of(width, where, count):
    cols = width // count
    for k in range(count):
        true = pl.ds(pl.multiple_of(where[k] * cols, LANES), cols) if count > 1 else slice(0, width)
        yield slice(k * cols, (k + 1) * cols), true


def norm_one_kernel(count, where, x_ref, gain_ref, h_ref):
    width = x_ref.shape[1]
    x = x_ref[...]
    rstd = lax.rsqrt(jnp.sum(x * x, axis=1, keepdims=True) * (1.0 / width) + NORM_EPS)
    for own, true in pieces_of(width, where, count):
        h_ref[:, own] = (x_ref[:, true] * rstd * gain_ref[:, own]).astype(BF16)


def low_kernel(count, where, x_ref, low_ref, true_ref):
    true_ref[...] = x_ref[...].astype(BF16)
    for own, true in pieces_of(x_ref.shape[1], where, count):
        low_ref[:, own] = true_ref[:, true]


def summed(refs, own):
    return sum(ref[:, own].astype(F32) for ref in refs[1:]) + refs[0][:, own].astype(F32)


def norm_two_kernel(count, where, x_ref, a_ref, b_ref, c_ref, gain_ref, resid_ref, h_ref):
    width = x_ref.shape[1]
    square = 0.0
    for own, true in pieces_of(width, where, count):
        resid = x_ref[:, true] + summed((a_ref, b_ref, c_ref), own)
        resid_ref[:, own] = resid
        square = square + jnp.sum(resid * resid, axis=1, keepdims=True)
    rstd = lax.rsqrt(square * (1.0 / width) + NORM_EPS)
    h_ref[...] = (resid_ref[...] * rstd * gain_ref[...]).astype(BF16)


def norm_two_back_kernel(count, where, cot_ref, a_ref, b_ref, c_ref, gain_ref, resid_ref, d_resid_ref, low_ref):
    width = cot_ref.shape[1]
    resid = resid_ref[...]
    rstd = lax.rsqrt(jnp.sum(resid * resid, axis=1, keepdims=True) * (1.0 / width) + NORM_EPS)
    along = 0.0
    for own, _ in pieces_of(width, where, count):
        d_normed = summed((a_ref, b_ref, c_ref), own) * gain_ref[:, own]
        d_resid_ref[:, own] = d_normed
        along = along + jnp.sum(d_normed * resid_ref[:, own], axis=1, keepdims=True)
    along = along * rstd * (1.0 / width)
    for own, true in pieces_of(width, where, count):
        d_resid = cot_ref[:, true] + rstd * (d_resid_ref[:, own] - resid_ref[:, own] * rstd * along)
        d_resid_ref[:, own] = d_resid
        low_ref[:, own] = d_resid.astype(BF16)


def norm_one_back_kernel(count, where, x_ref, a_ref, b_ref, c_ref, gain_ref, d_resid_ref, out_ref, kept):
    width = x_ref.shape[1]
    x = x_ref[...]
    rstd = lax.rsqrt(jnp.sum(x * x, axis=1, keepdims=True) * (1.0 / width) + NORM_EPS)
    along = 0.0
    for own, true in pieces_of(width, where, count):
        d_normed = summed((a_ref, b_ref, c_ref), own) * gain_ref[:, own]
        kept[:, own] = d_normed
        along = along + jnp.sum(d_normed * x_ref[:, true], axis=1, keepdims=True)
    along = along * rstd * (1.0 / width)
    for own, true in pieces_of(width, where, count):
        out = d_resid_ref[:, own] + rstd * (kept[:, own] - x_ref[:, true] * rstd * along)
        out_ref[:, true] = out.astype(BF16)


def spread_kernel(count, where, a_ref, b_ref, c_ref, d_ref, out_ref):
    for slot, ref in enumerate((a_ref, b_ref, c_ref, d_ref)):

        @pl.when(where[count + 4 + pl.program_id(0)] == slot)
        def _():
            out_ref[...] = ref[...].astype(F32)


def norm_call(kernel, count, where, x, gain, outputs=1, slots=False):
    tokens, width = x.shape
    rows = min(ROWS, tokens // 4)
    per = tokens // 4 // rows
    time = pl.BlockSpec((rows, width), lambda i, w: (i, 0))
    moved = pl.BlockSpec((rows, width), lambda i, w: (w[count + i // per] * per + i % per, 0))
    args = (x,) if gain is None else (x, gain)
    return pl.pallas_call(
        functools.partial(kernel, count),
        grid_spec=pltpu.PrefetchScalarGridSpec(
            num_scalar_prefetch=1,
            grid=(tokens // rows,),
            in_specs=[moved if slots else time] + [pl.BlockSpec(a.shape, lambda i, w: (0, 0)) for a in args[1:]],
            out_specs=[time] * outputs,
        ),
        out_shape=[jax.ShapeDtypeStruct((tokens, width), BF16)] * outputs,
        compiler_params=kernel_params(),
        cost_estimate=COST,
    )(where, *args)


def own_call(kernel, count, where, x, total, gain, extra, out_types, scratch=False):
    tokens, width = x.shape
    rows = min(64, tokens // 4)
    per = tokens // 4 // rows
    time = pl.BlockSpec((rows, width), lambda i, w: (i, 0))
    true = pl.BlockSpec((rows, width), lambda i, w: (w[count] * per + i, 0))
    args = (x, total.own, total.core, total.far, gain) + extra
    return pl.pallas_call(
        functools.partial(kernel, count),
        grid_spec=pltpu.PrefetchScalarGridSpec(
            num_scalar_prefetch=1,
            grid=(per,),
            in_specs=[true, time, time, time, pl.BlockSpec(gain.shape, lambda i, w: (0, 0))] + [time] * len(extra),
            out_specs=[time] * len(out_types),
            scratch_shapes=[pltpu.VMEM((rows, width), F32)] if scratch else [],
        ),
        out_shape=[jax.ShapeDtypeStruct((tokens // 4, width), t) for t in out_types],
        compiler_params=kernel_params(),
        cost_estimate=COST,
    )(where, *args)


def spread_call(count, where, parts):
    rows, width = parts[0].shape
    whole = pl.BlockSpec((rows, width), lambda i, w: (0, 0))
    return pl.pallas_call(
        functools.partial(spread_kernel, count),
        grid_spec=pltpu.PrefetchScalarGridSpec(
            num_scalar_prefetch=1,
            grid=(4,),
            in_specs=[whole] * 4,
            out_specs=pl.BlockSpec((rows, width), lambda i, w: (i, 0)),
        ),
        out_shape=jax.ShapeDtypeStruct((4 * rows, width), F32),
        compiler_params=kernel_params(),
        cost_estimate=COST,
    )(where, *parts)


def weight_call(
    body, pieces, target, rows, inputs, fixed, outputs, scalars, scratch=(), steps=None, spots=None, earlier=()
):
    tokens = inputs[0].shape[0]
    steps = tokens // rows if steps is None else steps
    same = lambda i, s: i
    read, write = spots if spots else (None, same)
    read = read or [same] * len(inputs)
    count = len(pieces)

    def kernel(scalar_ref, *refs):
        shard_refs, refs = refs[:count], refs[count:]
        weight, sem = refs[-2:]

        @pl.when(pl.program_id(0) == 0)
        def _():
            copies = []
            for n, (ref, (_, place)) in enumerate(zip(shard_refs, pieces)):
                for m, (source, to) in enumerate(place(scalar_ref)):
                    copies.append(pltpu.make_async_copy(ref.at[source], weight.at[to], sem.at[n, m]))
            for copy in copies:
                copy.start()
            for copy in copies:
                copy.wait()

        skip = len(inputs) + len(fixed)
        body(scalar_ref, weight, *refs[:skip], *refs[skip + len(earlier) : -2])

    whole = lambda x: pl.BlockSpec(x.shape, lambda i, s: (0,) * x.ndim)
    in_specs = [pl.BlockSpec(memory_space=pl.ANY)] * count
    for x, at in zip(inputs, read):
        in_specs.append(pl.BlockSpec((rows, x.shape[1]), lambda i, s, at=at: (at(i, s), 0)))
    in_specs += [whole(x) for x in fixed] + [pl.BlockSpec(memory_space=pl.ANY)] * len(earlier)
    out_specs, out_shape = [], []
    for o in outputs:
        if len(o) == 2:
            out_specs.append(pl.BlockSpec((rows, o[0]), lambda i, s: (write(i, s), 0)))
            out_shape.append(jax.ShapeDtypeStruct((tokens, o[0]), o[1]))
        else:
            out_specs.append(pl.BlockSpec(o[:2], lambda i, s: (0, 0)))
            out_shape.append(jax.ShapeDtypeStruct(o[:2], o[2]))
    first = 1 + count + len(inputs) + len(fixed)
    return pl.pallas_call(
        kernel,
        grid_spec=pltpu.PrefetchScalarGridSpec(
            num_scalar_prefetch=1,
            grid=(steps,),
            in_specs=in_specs,
            out_specs=out_specs,
            scratch_shapes=list(scratch) + [pltpu.VMEM(target, BF16), pltpu.SemaphoreType.DMA((count, 16))],
        ),
        out_shape=out_shape,
        input_output_aliases={first + i: i for i in range(len(earlier))},
        compiler_params=kernel_params(),
        cost_estimate=COST,
    )(scalars, *[array for array, _ in pieces], *inputs, *fixed, *earlier)


def row_pieces(ring_gather, cols, lane=lambda s: slice(None)):
    out = []
    for array, k, half in ring_gather.pieces():
        first = array.shape[0] if half == 1 else 0
        size = min(array.shape[0], cols - first)
        if size > 0:
            place = lambda s, start=k * cols + first, size=size: [
                ((pl.ds(0, size),), (pl.ds(start, size), lane(s)))
            ]
            out.append((array, place))
    return out


def col_pieces(ring_gather, cols):
    if cols % LANES:
        return [(jnp.concatenate(ring_gather.parts, axis=1), lambda s: [((slice(None),), (slice(None),))])]
    out = []
    for array, k, half in ring_gather.pieces():
        size = array.shape[0]
        start = size if half == 1 else 0
        out.append(
            (
                array,
                lambda s, start=start, size=size, k=k: [
                    ((slice(None),), (pl.ds(start, size), pl.ds(k * cols, cols)))
                ],
            )
        )
    return out


NT = (((1,), (1,)), ((), ()))


def product_body(where, weight, x_ref, out_ref):
    out_ref[...] = jnp.dot(x_ref[...], weight[...], preferred_element_type=F32).astype(BF16)


def to_quarter(slot, refs, value):
    for s, ref in enumerate(refs):

        @pl.when(slot == s)
        def _():
            ref[...] = value.astype(BF16)


def product_nt_body(where, weight, x_ref, *out_refs):
    part = lax.dot_general(x_ref[...], weight[...], NT, preferred_element_type=F32)
    to_quarter(pl.program_id(0), out_refs, part)


def output_body(count, where, weight, hidden_ref, *refs):
    attn_refs, out_ref, part = refs[:4], refs[4], refs[5]
    part[...] = jnp.dot(hidden_ref[...], weight[...], preferred_element_type=F32)
    width = part.shape[1]
    for slot, ref in enumerate(attn_refs):

        @pl.when(pl.program_id(0) == slot)
        def _():
            part[...] += ref[...].astype(F32)

    cols = width // count
    for k in range(count):
        own = slice(k * cols, (k + 1) * cols)
        to = pl.ds(pl.multiple_of(where[count + 8 + k] * cols, LANES), cols) if count > 1 else own
        out_ref[:, to] = part[:, own].astype(BF16)


def mixed_body(count, where, weight, z_ref, loc_ref, prod_ref, enter_ref, mixed_ref, *out_refs):
    channels = loc_ref.shape[1]
    act, _ = gelu_both(z_ref[:, :channels].astype(F32))
    mixed_ref[...] = (act * (loc_ref[...] + prod_ref[...] * enter_ref[...])).astype(BF16)
    part = jnp.dot(mixed_ref[...], weight[...], preferred_element_type=F32)
    to_quarter(where[count + 4 + pl.program_id(0)], out_refs, part)


def gate_up_body(where, weight, h_ref, hidden_ref, act_ref, slope_ref, both):
    units = hidden_ref.shape[1]
    both[...] = jnp.dot(h_ref[...], weight[...], preferred_element_type=F32)
    for lane in range(0, units, LANES):
        own = slice(lane, lane + LANES)
        act, slope = gelu_both(both[:, own])
        up = both[:, units + lane : units + lane + LANES]
        hidden_ref[:, own] = (act * up).astype(BF16)
        act_ref[:, own] = act.astype(BF16)
        slope_ref[:, own] = (slope * up).astype(BF16)


def d_hidden_body(where, weight, d_ref, act_ref, slope_ref, out_ref):
    units = act_ref.shape[1]
    d_hidden = lax.dot_general(d_ref[...], weight[...], NT, preferred_element_type=F32)
    out_ref[:, :units] = (d_hidden * slope_ref[...].astype(F32)).astype(BF16)
    out_ref[:, units:] = (d_hidden * act_ref[...].astype(F32)).astype(BF16)


def d_h_one_body(where, weight, dzg_ref, dzr_ref, *out_refs):
    channels = dzg_ref.shape[1]
    gate = lax.dot_general(dzg_ref[...], weight[:, :channels], NT, preferred_element_type=F32)
    rec = lax.dot_general(dzr_ref[...], weight[:, channels:], NT, preferred_element_type=F32)
    to_quarter(pl.program_id(0), out_refs, gate + rec)


def per_device(
    inputs,
    lengths,
    norm_gain1,
    in_weight,
    conv_weight,
    conv_bias,
    gate_weight,
    gate_bias,
    decay_param,
    out_weight,
    norm_gain2,
    mlp_in,
    mlp_down,
    cotangent,
):
    tokens, width = inputs.shape
    count, index = lax.axis_size("seq"), lax.axis_index("seq")
    br, ch = lax.axis_index("br"), lax.axis_index("ch")
    place = ring_place(index, count)
    cols = width // count
    taps = conv_weight.shape[0]
    span = taps - 1
    part_ch = conv_weight.shape[3]
    channels = part_ch * count
    hidden_units = mlp_down.shape[0]
    heads, part_in, block = gate_weight.shape[3], gate_weight.shape[4], gate_weight.shape[5]
    ahead = (place + jnp.arange(count, dtype=jnp.int32)) % count
    true_all = jnp.where(ahead < count // 2, 2 * ahead, 2 * (count - 1 - ahead) + 1)
    ring_index = (ring_place(jnp.arange(count, dtype=jnp.int32), count) - place) % count
    true_of = [true_all[k] for k in range(count)]
    ring_of = [ring_index[k] for k in range(count)]
    aligned = cols % LANES == 0

    def move(x, at):
        return jnp.concatenate(
            [lax.dynamic_slice_in_dim(x, a * cols, cols, 1) for a in at], axis=1
        )

    quarter = tokens // 4
    me = ch * 2 + br
    quarters = me ^ jnp.asarray([0, 2, 1, 3], jnp.int32)
    slots = me ^ jnp.arange(4, dtype=jnp.int32)
    slots = (slots % 2) * 2 + slots // 2
    per_device_cols = count // 4
    to = true_all // per_device_cols
    dealt = (((to % 2) ^ ch) * 2 + ((to // 2) ^ br)) * per_device_cols + true_all % per_device_cols
    whole_inputs = inputs
    if aligned:
        n_pieces = count
        where = jnp.concatenate([true_all, quarters, slots, dealt, br[None]]).astype(jnp.int32)
    else:
        n_pieces = 1
        zero = jnp.zeros((1,), jnp.int32)
        where = jnp.concatenate([zero, quarters, slots, zero, br[None]]).astype(jnp.int32)
        inputs, cotangent = move(inputs, true_of), move(cotangent, true_of)

    ring = Ring(count)

    small = jnp.concatenate(
        [
            norm_gain1,
            norm_gain2,
            conv_weight.reshape(-1),
            conv_bias.reshape(-1),
            gate_bias.reshape(-1),
            decay_param.reshape(-1),
        ]
    )
    fold = 2 * block
    small_rows = -(-small.shape[0] // fold)
    small = jnp.pad(small, (0, small_rows * fold - small.shape[0])).reshape(small_rows, fold)
    gate_rows = heads * part_in
    packed = jnp.concatenate(
        [gate_weight[:, 0, 0].transpose(1, 2, 0, 3).reshape(gate_rows, fold), small], axis=0
    )
    packed = pad_rows(packed, -(-packed.shape[0] // 32) * 32)
    packed_rows = packed.shape[0] * fold // channels
    packed_shape = packed.shape

    own_cols = lax.dynamic_slice_in_dim(in_weight[0], br * channels, channels, 1)
    far_cols = lax.ppermute(
        lax.dynamic_slice_in_dim(in_weight[0], (1 - br) * channels, channels, 1), "br", SWAP
    )
    extra_rows = -(-(cols + packed_rows) // 32) * 32 - cols - packed_rows
    own_and_packed = jnp.concatenate(
        [own_cols, packed.reshape(packed_rows, channels), jnp.zeros((extra_rows, channels), BF16)], axis=0
    )
    in_own, in_far = Gather(ring, own_and_packed), Gather(ring, far_cols)
    out_ring = Gather(ring, out_weight[0, 0])
    down_ring = Gather(ring, mlp_down)
    in_own.hop()
    in_far.hop()
    own_first, far_first = in_own.last, in_far.last
    in_own.hop()
    in_far.hop()
    own_second, far_second = in_own.last, in_far.last
    in_own.hop()
    in_far.hop()
    mlp_all = lax.all_gather(after(mlp_in, *in_far.last), "seq", axis=1, tiled=True)
    in_own.hop()
    in_far.hop()
    out_ring.hop()

    doc_starts = jnp.cumsum(lengths) - lengths
    positions = jnp.arange(tokens + span, dtype=jnp.int32) + index * tokens - span
    doc_ext = jnp.sum((positions[:, None] >= doc_starts[None, 1:]).astype(jnp.int32), axis=1)
    lags = [
        (doc_ext[span - lag : span - lag + tokens] == doc_ext[span:]).astype(F32) for lag in range(taps)
    ]
    reset = jnp.any(positions[span:, None] == doc_starts[None, :], axis=1).astype(F32)
    mask = jnp.stack(lags + [reset], axis=1)

    packed_all = [part[cols : cols + packed_rows].reshape(packed_shape) for part in in_own.parts]
    small_all = jnp.stack([part[gate_rows : gate_rows + small_rows].reshape(-1) for part in packed_all])
    gain_one = small_all[:, :cols].astype(F32).reshape(1, width)
    gain_two = small_all[:, cols : 2 * cols].astype(F32).reshape(1, width)
    place_hot = (ring_index[:, None] == jnp.arange(count)[None, :]).astype(BF16)
    chan = jnp.dot(place_hot, small_all[:, 2 * cols :], preferred_element_type=F32)
    chan = chan[:, : (taps + 4) * part_ch].reshape(count, taps + 4, part_ch)
    chan = chan.transpose(1, 0, 2).reshape(taps + 4, channels)
    conv = chan[: taps + 1]
    gate_bias_all = chan[taps + 1 : taps + 3].reshape(1, 2 * channels)
    decay_rate = chan[taps + 3 : taps + 4]
    rate = -DECAY_SCALE * jax.nn.softplus(-decay_rate)

    stacked = jnp.concatenate([part[:gate_rows] for part in packed_all], axis=0)
    row = jnp.arange(channels)
    row_head, row_in = row // block, row % block
    source = ring_index[row_in // part_in] * gate_rows + row_head * part_in + row_in % part_in
    row_hot = (source[:, None] == jnp.arange(channels)[None, :]).astype(BF16)
    wide_col = jnp.arange(2 * channels)
    wide_gate, wide_head, wide_out = (
        wide_col // channels,
        (wide_col % channels) // block,
        wide_col % block,
    )
    spread_hot = (jnp.arange(fold)[:, None] == (wide_gate * block + wide_out)[None, :]).astype(BF16)
    on_block = (row_head[:, None] == wide_head[None, :]).astype(BF16)
    compact = jnp.dot(row_hot, stacked, preferred_element_type=F32).astype(BF16)
    wide = jnp.dot(compact, spread_hot, preferred_element_type=F32).astype(BF16) * on_block

    (h_one,) = norm_call(norm_one_kernel, n_pieces, where, inputs, gain_one)
    scalars = where
    last_at = where.shape[0] - 1
    in_pieces = row_pieces(in_own, cols, lambda s: pl.ds(pl.multiple_of(s[last_at] * channels, LANES), channels))
    in_pieces += row_pieces(
        in_far, cols, lambda s: pl.ds(pl.multiple_of((1 - s[last_at]) * channels, LANES), channels)
    )
    in_shape = (width, 2 * channels)
    (z_last,) = weight_call(
        product_body, in_pieces, in_shape, 16, (h_one[tokens - 16 :],), (), [(2 * channels, BF16)], scalars
    )
    forward_pairs = [(i, i + 1) for i in range(count - 1)]
    rim = lax.ppermute(z_last[8:, channels:], "seq", forward_pairs).astype(F32)
    (z,) = weight_call(
        product_body, in_pieces, in_shape, quarter, (after(h_one, z_last),), (), [(2 * channels, BF16)], scalars
    )
    ring.mark = (z, rim)
    out_first = out_ring.last
    out_ring.hop()

    unit, gates, loc, prod, last, total = forward_local(
        after(z, *out_first), rim, mask, conv, wide, gate_bias_all, rate
    )
    ring.mark = (last,)
    out_second = out_ring.last
    out_ring.hop()
    enter = entering(after(last[:2], *out_second), False)[None]
    ring.mark = (enter,)
    out_third = out_ring.last
    out_ring.hop()
    down_ring.hop()

    to_slot = lambda i, s: s[n_pieces + 4 + i]
    from_slot = lambda i, s: s[n_pieces + i]
    out_pieces = col_pieces(out_ring, cols)
    out_shape = (channels, width)
    one_quarter = (quarter, width, BF16)
    mixed, *attn_parts = weight_call(
        functools.partial(mixed_body, n_pieces), out_pieces, out_shape, quarter, (z, loc, prod),
        (after(enter, *out_third),), [(channels, BF16)] + [one_quarter] * 4, scalars, spots=(None, to_slot),
    )
    attn = TokenSum()
    attn.second(*attn_parts[2:])
    attn.cross()
    attn.first(*attn_parts[:2])
    down_first = down_ring.last
    ring.mark = (attn.chip,)
    down_ring.hop()
    d_mlp, slot_cot = norm_call(low_kernel, n_pieces, where, after(cotangent, attn.chip), None, 2, slots=True)
    if not aligned:
        slot_cot = move(slot_cot, ring_of)

    resid, h_own = own_call(
        norm_two_kernel, n_pieces, where, inputs, attn, after(gain_two, d_mlp, *down_first), (), (F32, BF16)
    )
    h_two = TokenGather(h_own)
    down_second = down_ring.last
    ring.mark = (h_own,)
    down_ring.hop()
    h_two = after(jnp.concatenate(h_two.parts(), axis=0), *down_second)
    down_third = down_ring.last
    ring.mark = (h_two,)
    down_ring.hop()


    def mlp_place(s):
        out = []
        for k in range(count):
            rows = pl.ds(pl.multiple_of(s[k] * cols, 8), cols)
            for g in range(2):
                out.append(
                    ((g, rows), (pl.ds(k * cols, cols), pl.ds(g * hidden_units, hidden_units)))
                )
        return out

    if aligned:
        mlp_pieces = [(mlp_all, mlp_place)]
    else:
        moved = [lax.dynamic_slice_in_dim(mlp_all, a * cols, cols, 1) for a in true_of]
        mlp_pieces = [
            (
                jnp.concatenate(moved, axis=1),
                lambda s: [
                    ((g,), (slice(None), pl.ds(g * hidden_units, hidden_units))) for g in range(2)
                ],
            )
        ]
    mlp_shape = (width, 2 * hidden_units)
    hidden, act, slope = weight_call(
        gate_up_body, mlp_pieces, mlp_shape, quarter, (after(h_two, *down_third),), (),
        [(hidden_units, BF16)] * 3, scalars, scratch=(pltpu.VMEM((quarter, 2 * hidden_units), F32),),
    )

    def chunk(x, k):
        return x[:, k * cols : (k + 1) * cols]

    def outer(left, right):
        return lax.dot_general(left, right, (((0,), (0,)), ((), ())), preferred_element_type=F32)

    down_pieces = col_pieces(down_ring, cols)
    down_shape = (hidden_units, width)
    (d_gate_up,) = weight_call(
        d_hidden_body, down_pieces, down_shape, quarter, (after(d_mlp, hidden), act, slope), (),
        [(2 * hidden_units, BF16)], scalars,
    )
    ring.mark = (d_gate_up,)
    g_mlp = Scatter(ring, lambda k, *t: outer(chunk(h_two, k), after(d_gate_up, *t)))
    g_mlp.hop()
    mlp_hop = [g_mlp.last]
    upper, lower = lambda i, s: i + 2, lambda i, s: i
    part = weight_call(
        product_nt_body, mlp_pieces, mlp_shape, quarter, (d_gate_up,), (), [one_quarter] * 2, scalars,
        steps=2, spots=([upper], upper),
    )
    d_h_two = TokenSum()
    d_h_two.second(*part)
    d_h_two.cross()
    part = weight_call(
        product_nt_body, mlp_pieces, mlp_shape, quarter, (after(d_gate_up, d_h_two.chip),), (), [one_quarter] * 2,
        scalars, steps=2, spots=([lower], lower),
    )
    d_h_two.first(*part)
    ring.mark = (part[0],)
    g_mlp.hop()
    mlp_hop.append(g_mlp.last)
    g_down_part = outer(after(hidden, part[0], *g_mlp.last), slot_cot).astype(BF16)
    g_down = lax.psum_scatter(g_down_part, "seq", scatter_dimension=1, tiled=True)
    d_resid, d_attn = own_call(
        norm_two_back_kernel, n_pieces, where, cotangent, d_h_two, gain_two, (resid,), (F32, BF16)
    )
    d_attn = TokenGather(d_attn)

    (o_part,) = weight_call(
        functools.partial(output_body, n_pieces), down_pieces, down_shape, quarter,
        (after(hidden, d_attn.own),), tuple(attn_parts), [(width, BF16)], scalars, spots=(None, from_slot),
        scratch=(pltpu.VMEM((quarter, width), F32),),
    )
    if not aligned:
        at = jnp.arange(count)
        o_part = move(o_part, [jnp.sum(jnp.where(dealt == k, at, 0)) for k in range(count)])
    o_cols = width // 4
    swapped = lax.ppermute(o_part[:, 2 * o_cols :], "ch", SWAP).astype(F32)
    o_far = lax.ppermute((o_part[:, o_cols : 2 * o_cols].astype(F32) + swapped[:, o_cols:]).astype(BF16), "br", SWAP)
    o_inputs = lax.dynamic_slice_in_dim(whole_inputs, (br * 2 + ch) * o_cols, o_cols, 1)
    output = o_inputs + o_part[:, :o_cols].astype(F32) + swapped[:, :o_cols] + o_far.astype(F32)

    ring.mark = (d_attn.own,)
    mlp_first = mlp_hop[1]
    g_mlp.hop()
    mlp_hop.append(g_mlp.last)
    d_attn = jnp.concatenate(d_attn.parts(), axis=0)
    rows = min(ROWS, quarter)
    per = quarter // rows
    last_step = tokens // rows - 1
    back = lambda i, s: last_step - i
    back_slot = lambda i, s: s[n_pieces + 4 + (last_step - i) // per] * per + (last_step - i) % per
    adj, tail, d_z_gate, head = weight_call(
        adjoint_body, out_pieces, out_shape, rows, (d_attn, z, loc, prod, gates, mask), (enter, rate),
        [(channels, F32), (channels, F32), (channels, BF16), (8, channels, F32)], scalars,
        scratch=(pltpu.VMEM((rows, channels), F32), pltpu.VMEM((8, channels), F32)),
        spots=([back_slot] + [back] * 5, back),
    )
    ring.mark = (head,)
    g_out = Scatter(ring, lambda k, *t: outer(after(mixed, *t), chunk(d_attn, k)))
    g_out.hop()
    out_hop = [g_out.last]
    arrive = entering(after(head[:2], *mlp_hop[2]), True)[None]
    g_mlp.hop()
    mlp_hop.append(g_mlp.last)
    d_z_rec, g_wide, sums, edge = backward_local(
        adj, tail, after(arrive, *out_hop[0]), loc, prod, enter, gates, unit, mask, z, rim, conv, wide, rate
    )
    ring.mark = (edge,)
    backward_pairs = [(i + 1, i) for i in range(count - 1)]
    from_next = lax.ppermute(edge[:8], "seq", backward_pairs)
    g_out.hop()
    out_hop.append(g_out.last)
    fixed = (edge[8:] + from_next).astype(BF16)
    d_z_rec = d_z_rec.at[tokens - 8 :].set(fixed)

    d_z = jnp.concatenate([d_z_gate, d_z_rec], axis=1)
    d_h_one = TokenSum()
    for first in (2, 0):
        read = lambda i, s, first=first: s[n_pieces + i + first]
        rec = after(d_z_rec, *out_hop[1]) if first else after(d_z_rec, d_h_one.chip, *mlp_hop[3])
        part = weight_call(
            d_h_one_body, in_pieces, in_shape, quarter, (d_z_gate, rec), (), [one_quarter] * 2, scalars,
            steps=2, spots=([read, read], None),
        )
        if first:
            d_h_one.second(*part)
            d_h_one.cross()
        else:
            d_h_one.first(*part)
    ring.mark = (part[0], d_z)
    g_in_ring = Scatter(ring, lambda k, *t: outer(chunk(h_one, k), after(d_z, *t)))
    g_in_ring.hop()
    in_hop = [g_in_ring.last]
    g_out.hop()
    out_hop.append(g_out.last)

    g_compact = lax.dot_general(
        (after(g_wide, d_h_one.chip) * on_block.astype(F32)).astype(BF16),
        spread_hot,
        (((1,), (1,)), ((), ())),
        preferred_element_type=F32,
    ).astype(BF16)
    g_gates = lax.dot_general(row_hot, g_compact, (((0,), (0,)), ((), ())), preferred_element_type=F32)
    g_decay = sums[0:1] * -DECAY_SCALE * -jax.nn.sigmoid(-decay_rate)
    g_chan = jnp.concatenate([sums[4 : 4 + taps], sums[3:4], sums[1:3], g_decay, total[0:1]], axis=0)
    g_chan = g_chan.reshape(taps + 5, count, part_ch).transpose(1, 0, 2).reshape(count, -1)
    g_small = lax.dot_general(
        place_hot.astype(F32), g_chan, (((0,), (0,)), ((), ())), precision=lax.Precision.HIGHEST
    )
    g_rows = -(-g_small.shape[1] // fold)
    g_small = jnp.pad(g_small, ((0, 0), (0, g_rows * fold - g_small.shape[1]))).reshape(count, g_rows, fold)
    g_packed = jnp.concatenate([g_gates.reshape(count, gate_rows, fold), g_small], axis=1)
    total_rows = -(-g_packed.shape[1] // 32) * 32
    g_packed = jnp.pad(g_packed, ((0, 0), (0, total_rows - g_packed.shape[1]), (0, 0)))
    g_packed_ring = Scatter(ring, lambda k, *t: g_packed[k], free=True)
    for _ in range(4):
        g_packed_ring.hop()
    (grad_own,) = own_call(
        norm_one_back_kernel, n_pieces, where, inputs, d_h_one, after(gain_one, *in_hop[0]), (d_resid,), (BF16,),
        scratch=True,
    )
    grad_parts = TokenGather(grad_own).parts()
    ring.mark = (grad_own,)
    g_in_ring.hop()
    in_hop.append(g_in_ring.last)
    g_out.hop()
    ring.mark = g_packed_ring.last
    g_in_ring.hop()
    in_hop.append(g_in_ring.last)
    inputs_grad = spread_call(n_pieces, where, [after(grad_parts[0], *in_hop[1])] + grad_parts[1:])
    if not aligned:
        inputs_grad = move(inputs_grad, ring_of)
    g_in_ring.hop()

    g_in_own = g_in_ring.result()
    g_in_gate, g_in_rec = g_in_own[:, :channels], g_in_own[:, channels:]
    keep_half = jnp.where(br == 0, g_in_gate, g_in_rec)
    send_half = jnp.where(br == 0, g_in_rec, g_in_gate).astype(BF16)
    got_half = lax.ppermute(send_half, "br", SWAP).astype(F32)
    g_in = jnp.concatenate(
        [jnp.where(br == 0, keep_half, got_half), jnp.where(br == 0, got_half, keep_half)], axis=1
    )
    g_mlp_own = g_mlp.result()
    g_gate_own, g_up_own = g_mlp_own[:, :hidden_units], g_mlp_own[:, hidden_units:]
    w_gate = jnp.where(br == 0, own_cols, far_cols).astype(F32)
    w_rec = jnp.where(br == 0, far_cols, own_cols).astype(F32)
    gains = jnp.stack(
        [
            jnp.sum(g_in_gate * w_gate, axis=1) + jnp.sum(g_in_rec * w_rec, axis=1),
            jnp.sum(g_gate_own * mlp_in[0].astype(F32), axis=1)
            + jnp.sum(g_up_own * mlp_in[1].astype(F32), axis=1),
        ]
    )
    gains = tiny_group_sum(gains)
    g_own = g_packed_ring.result()
    g_gate_w = g_own[:gate_rows].reshape(heads, part_in, 2, block).transpose(2, 0, 1, 3)[:, None, None]
    g_flat = g_own[gate_rows : gate_rows + g_rows].reshape(-1)
    g_chan = g_flat[: (taps + 5) * part_ch].reshape(taps + 5, part_ch)
    return (
        output,
        inputs_grad,
        gains[0] / norm_gain1.astype(F32),
        g_in[None],
        g_chan[:taps][:, None, None],
        g_chan[taps][None, None],
        g_gate_w,
        g_chan[taps + 1 : taps + 3][:, None, None],
        g_chan[taps + 3][None, None],
        g_out.result()[None, None],
        gains[1] / norm_gain2.astype(F32),
        jnp.stack([g_gate_own, g_up_own]),
        g_down.astype(F32),
        g_chan[taps + 4][None, None] / (tokens * count),
    )


def solution(mesh):
    placed = (
        P("seq", None),
        P(),
        P("seq"),
        P("br", "seq", "ch"),
        P(None, "ch", "br", "seq"),
        P("ch", "br", "seq"),
        P(None, "ch", "br", None, "seq", None),
        P(None, "ch", "br", "seq"),
        P("ch", "br", "seq"),
        P("ch", "br", None, "seq"),
        P("seq"),
        P(None, "seq", ("br", "ch")),
        P(("br", "ch"), "seq"),
        P("seq", None),
    )
    return jax.shard_map(
        per_device,
        mesh=mesh,
        in_specs=placed,
        out_specs=(
            P("seq", ("br", "ch")),
            P("seq", None),
            P("seq"),
            P("br", "seq", "ch"),
            P(None, "ch", "br", "seq"),
            P("ch", "br", "seq"),
            P(None, "ch", "br", None, "seq", None),
            P(None, "ch", "br", "seq"),
            P("ch", "br", "seq"),
            P("ch", "br", None, "seq"),
            P("seq"),
            P(None, "seq", ("br", "ch")),
            P(("br", "ch"), "seq"),
            P("ch", "br", "seq"),
        ),
        check_vma=False,
    )
```

```python
import functools

import jax
import jax.numpy as jnp
import numpy as np
from jax import lax
from jax.experimental import pallas as pl
from jax.experimental.pallas import tpu as pltpu
from jax.sharding import PartitionSpec as P

NORM_EPS = 1e-06
DECAY_SCALE = 8.0
GELU_C = 0.7978845608028654
GELU_K = 0.044715
LANES = 128
ROWS = 128
SWAP = [(0, 1), (1, 0)]
F32 = jnp.float32
BF16 = jnp.bfloat16
COST = pl.CostEstimate(flops=0, bytes_accessed=0, transcendentals=0)


def after(x, *others):
    if not others:
        return x
    return lax.optimization_barrier((x,) + others)[0]


def ring_order(count):
    return list(range(0, count, 2)) + list(range(count - 1, 0, -2))


def ring_place(index, count):
    half = index // 2
    return jnp.where(index % 2 == 0, half, count - 1 - half)


class Ring:
    def __init__(self, count, depth=3):
        order = ring_order(count)
        self.count = count
        self.half = count // 2
        self.reps = max(1, self.half // 4)
        self.pairs = {
            1: [(order[i], order[(i + 1) % count]) for i in range(count)],
            -1: [(order[(i + 1) % count], order[i]) for i in range(count)],
        }
        self.done = {1: [], -1: []}
        self.depth = depth
        self.mark = ()

    def hop(self, x, way, free=False):
        if not free:
            held = self.done[way]
            others = self.mark + tuple(held[-self.depth :][:1] if len(held) >= self.depth else ())
            if others:
                x = after(x, *others)
        got = lax.ppermute(x, "seq", self.pairs[way])
        if not free:
            self.done[way].append(got)
        return got


class Gather:
    def __init__(self, ring, x, free=False):
        self.ring, self.free = ring, free
        self.parts = [None] * ring.count
        self.parts[0] = x
        self.last = (x, x)
        self.step = 0

    def pieces(self):
        far = self.ring.half
        every = [(part, k, None) for k, part in enumerate(self.parts) if k != far]
        return every + [(self.last[0], far, 0), (self.last[1], far, 1)]

    def hop(self):
        ring = self.ring
        for _ in range(ring.reps):
            self.step += 1
            ahead, behind = self.last
            if self.step < ring.half:
                self.last = (ring.hop(ahead, 1, self.free), ring.hop(behind, -1, self.free))
                self.parts[ring.count - self.step], self.parts[self.step] = self.last
            else:
                cut = ahead.shape[0] // 2
                self.last = (
                    ring.hop(ahead[:cut], 1, self.free),
                    ring.hop(behind[cut:], -1, self.free),
                )
                self.parts[ring.half] = jnp.concatenate(self.last, axis=0)


class Scatter:
    def __init__(self, ring, part, free=False):
        self.ring, self.part, self.free = ring, part, free
        self.last = None
        self.step = 0

    def hop(self):
        ring = self.ring
        for _ in range(ring.reps):
            self.step += 1
            mark = () if self.free else ring.mark
            if self.step == 1:
                far = self.part(ring.half, *mark)
                self.cut = cut = far.shape[0] // 2
                up, down = far[:cut], far[cut:]
            else:
                ahead, behind = (x.astype(F32) for x in self.last)
                cut, at = self.cut, self.step - 1
                up = self.part(ring.half - at, *mark, self.last[0])
                down = self.part(ring.half + at, *mark, self.last[1])
                if at == 1:
                    up = jnp.concatenate([up[:cut] + ahead, up[cut:]], axis=0)
                    down = jnp.concatenate([down[:cut], down[cut:] + behind], axis=0)
                else:
                    up, down = up + ahead, down + behind
            self.last = (
                ring.hop(up.astype(BF16), 1, self.free),
                ring.hop(down.astype(BF16), -1, self.free),
            )

    def result(self):
        return self.part(0, *self.last) + (self.last[0].astype(F32) + self.last[1].astype(F32))


class TokenSum:
    def second(self, mine, others):
        got = lax.ppermute(others, "ch", SWAP)
        self.chip = (mine.astype(F32) + got.astype(F32)).astype(BF16)

    def cross(self, *others):
        self.far = lax.ppermute(after(self.chip, *others), "br", SWAP)

    def first(self, mine, others):
        self.own = mine
        self.core = lax.ppermute(others, "ch", SWAP)


class GroupSum:
    def __init__(self, part):
        self.half = part.shape[0] // 2
        core = lax.axis_index("ch")
        self.own = lax.dynamic_slice_in_dim(part, core * self.half, self.half, 0)
        theirs = lax.dynamic_slice_in_dim(part, (1 - core) * self.half, self.half, 0)
        self.got = lax.ppermute(theirs, "ch", SWAP)

    def chip(self, *others):
        got = after(self.got, *others) if others else self.got
        self.chip_sum = (self.own.astype(F32) + got.astype(F32)).astype(BF16)
        return self.chip_sum

    def cross(self, *others):
        x = after(self.chip_sum, *others) if others else self.chip_sum
        self.far = lax.ppermute(x, "br", SWAP)

    def total(self, *others):
        far = after(self.far, *others) if others else self.far
        self.mine = (self.chip_sum.astype(F32) + far.astype(F32)).astype(BF16)
        self.other = lax.ppermute(self.mine, "ch", SWAP)
        return self.mine


class TokenGather:
    def __init__(self, own):
        self.own = own
        self.far = lax.ppermute(own, "br", SWAP)
        self.core = lax.ppermute(own, "ch", SWAP)
        self.far_core = lax.ppermute(self.far, "ch", SWAP)

    def parts(self):
        return [self.own, self.core, self.far, self.far_core]


def tiny_group_sum(x):
    x = x + lax.ppermute(x, "ch", SWAP)
    return x + lax.ppermute(x, "br", SWAP)


def entering(pair, reverse):
    count, index = lax.axis_size("seq"), lax.axis_index("seq")
    spread = jnp.broadcast_to(pair[None], (count,) + pair.shape)
    every = lax.all_to_all(spread, "seq", 0, 0, tiled=True)
    value = jnp.zeros(pair.shape[1:], F32)
    for k in range(count):
        at = count - 1 - k if reverse else k
        new = every[at, 1] + every[at, 0] * value
        value = jnp.where((at > index) if reverse else (at < index), new, value)
    return value


def gelu_both(x):
    square = x * x
    bent = jnp.tanh(GELU_C * (x + GELU_K * (x * square)))
    half = 0.5 * (1.0 + bent)
    slope = half + 0.5 * x * (1.0 - bent * bent) * (GELU_C * (1.0 + 3.0 * GELU_K * square))
    return x * half, slope


def minus_expm1(x, exp_x):
    series = 1.0 + x * (1.0 / 6.0)
    for k in (5.0, 4.0, 3.0, 2.0):
        series = 1.0 + x * (1.0 / k) * series
    return jnp.where(x > -0.2, -x * series, 1.0 - exp_x)


def scan_rows(keep, add, reverse):
    rows = keep.shape[0]
    at = lax.broadcasted_iota(jnp.int32, keep.shape, 0)
    step = 1
    while step < rows:
        shift = rows - step if reverse else step
        inside = (at < rows - step) if reverse else (at >= step)
        far_add = jnp.where(inside, pltpu.roll(add, shift, 0), 0.0)
        add = add + keep * far_add
        keep = keep * jnp.where(inside, pltpu.roll(keep, shift, 0), 1.0)
        step *= 2
    return keep, add


def forward_kernel(
    z_ref, rim_ref, mask_ref, conv_ref, wide_ref, bias_ref, rate_ref,
    unit_ref, gate_ref, loc_ref, prod_ref, last_ref, total_ref, ext,
):
    block = pl.program_id(0)
    rows, channels = z_ref.shape
    span = conv_ref.shape[0] - 2

    @pl.when(block == 0)
    def _():
        ext[0:8] = rim_ref[...]
        last_ref[0:1] = jnp.ones((1, channels), F32)
        last_ref[1:8] = jnp.zeros((7, channels), F32)
        total_ref[...] = jnp.zeros_like(total_ref)

    @pl.when(block > 0)
    def _():
        ext[0:8] = ext[rows : rows + 8]

    ext[8 : rows + 8] = z_ref[...].astype(F32)
    conv = jnp.broadcast_to(conv_ref[span + 1 : span + 2], (rows, channels))
    for lag in range(span + 1):
        conv = conv + conv_ref[lag : lag + 1] * ext[8 - lag : 8 - lag + rows] * mask_ref[:, lag : lag + 1]
    unit_ref[...] = conv.astype(BF16)
    pre = jnp.dot(unit_ref[...], wide_ref[...], preferred_element_type=F32) + bias_ref[...]
    gate_ref[...] = jax.nn.sigmoid(pre)
    reset = mask_ref[:, span + 1 : span + 2] > 0.5
    for lane in range(0, channels, LANES):
        own = slice(lane, lane + LANES)
        in_gate = gate_ref[:, channels + lane : channels + lane + LANES]
        log_decay = gate_ref[:, own] * rate_ref[0:1, own]
        decay = jnp.exp(log_decay)
        scale = jnp.sqrt(minus_expm1(2.0 * log_decay, decay * decay))
        total_ref[0:1, own] += jnp.sum(decay, axis=0, keepdims=True)
        keep = jnp.where(reset, 0.0, decay)
        drive = jnp.where(reset, 1.0, scale) * in_gate * unit_ref[:, own].astype(F32)
        prod, loc = scan_rows(keep, drive, False)
        loc = loc + prod * last_ref[1:2, own]
        prod = prod * last_ref[0:1, own]
        loc_ref[:, own] = loc
        prod_ref[:, own] = prod
        last_ref[0:1, own] = prod[rows - 1 :]
        last_ref[1:2, own] = loc[rows - 1 :]


def adjoint_body(
    where, weight, d_ref, z_ref, loc_ref, prod_ref, gate_ref, mask_ref, enter_ref, rate_ref,
    adj_ref, tail_ref, dzg_ref, head_ref, dmix_ref, after,
):
    step = pl.program_id(0)
    rows, channels = loc_ref.shape
    dmix_ref[...] = lax.dot_general(d_ref[...], weight[...], NT, preferred_element_type=F32)

    @pl.when(step == 0)
    def _():
        head_ref[0:1] = jnp.ones((1, channels), F32)
        head_ref[1:8] = jnp.zeros((7, channels), F32)
        after[0:2] = jnp.ones((2, channels), F32)
        after[2:8] = jnp.zeros((6, channels), F32)

    reset = mask_ref[:, 4:5] > 0.5
    for lane in range(0, channels, LANES):
        own = slice(lane, lane + LANES)
        state = loc_ref[:, own] + prod_ref[:, own] * enter_ref[0:1, own]
        act, slope = gelu_both(z_ref[:, own].astype(F32))
        dmix = dmix_ref[:, own]
        dzg_ref[:, own] = (dmix * state * slope).astype(BF16)
        keep = jnp.where(reset, 0.0, jnp.exp(gate_ref[:, own] * rate_ref[0:1, own]))
        at = lax.broadcasted_iota(jnp.int32, keep.shape, 0)
        nxt = jnp.where(at == rows - 1, after[0:1, own], pltpu.roll(keep, rows - 1, 0))
        tail, adj = scan_rows(nxt, dmix * act, True)
        adj = adj + tail * after[2:3, own]
        tail = tail * after[1:2, own]
        adj_ref[:, own] = adj
        tail_ref[:, own] = tail
        after[0:1, own] = keep[0:1]
        after[1:2, own] = tail[0:1]
        after[2:3, own] = adj[0:1]
        head_ref[0:1, own] = keep[0:1] * tail[0:1]
        head_ref[1:2, own] = keep[0:1] * adj[0:1]


def backward_kernel(
    adj_ref, tail_ref, arrive_ref, loc_ref, prod_ref, loc0_ref, prod0_ref, enter_ref, gate_ref,
    unit_ref, mask_ref, z_ref, z0_ref, rim_ref, conv_ref, wide_ref, rate_ref,
    dz_ref, gw_ref, sums_ref, edge_ref, dpre, ddir, zext, moved,
):
    step = pl.program_id(0)
    block = pl.num_programs(0) - 1 - step
    rows, channels = z_ref.shape
    span = conv_ref.shape[0] - 2

    @pl.when(step == 0)
    def _():
        gw_ref[...] = jnp.zeros_like(gw_ref)
        sums_ref[...] = jnp.zeros_like(sums_ref)
        moved[...] = jnp.zeros_like(moved)

    @pl.when(step > 0)
    def _():
        for lag in range(1, span + 1):
            moved[lag - 1, rows : rows + 8] = moved[lag - 1, 0:8]

    zext[8 : rows + 8] = z_ref[...].astype(F32)

    @pl.when(block == 0)
    def _():
        zext[0:8] = rim_ref[...]

    @pl.when(block > 0)
    def _():
        zext[0:8] = z0_ref[8:16].astype(F32)

    reset = mask_ref[:, 4:5] > 0.5
    for lane in range(0, channels, LANES):
        own = slice(lane, lane + LANES)
        two = slice(channels + lane, channels + lane + LANES)
        enter = enter_ref[0:1, own]
        adj = adj_ref[:, own] + tail_ref[:, own] * arrive_ref[0:1, own]
        state = loc_ref[:, own] + prod_ref[:, own] * enter
        before = jnp.where(block == 0, enter, loc0_ref[7:8, own] + prod0_ref[7:8, own] * enter)
        at = lax.broadcasted_iota(jnp.int32, state.shape, 0)
        previous = jnp.where(at == 0, before, pltpu.roll(state, 1, 0))
        rec_gate, in_gate = gate_ref[:, own], gate_ref[:, two]
        unit = unit_ref[:, own].astype(F32)
        rate = rate_ref[0:1, own]
        log_decay = rec_gate * rate
        decay = jnp.exp(log_decay)
        scale = jnp.sqrt(minus_expm1(2.0 * log_decay, decay * decay))
        dlog = decay * (adj * previous - adj * in_gate * unit * (decay / scale))
        dlog = jnp.where(reset, 0.0, dlog)
        sums_ref[0:1, own] += jnp.sum(dlog * rec_gate, axis=0, keepdims=True)
        scale = jnp.where(reset, 1.0, scale)
        dpre[:, own] = (dlog * rate * (rec_gate * (1.0 - rec_gate))).astype(BF16)
        through = adj * scale
        dpre[:, two] = (through * unit * (in_gate * (1.0 - in_gate))).astype(BF16)
        ddir[:, own] = through * in_gate

    gw_ref[...] += lax.dot_general(
        unit_ref[...], dpre[...], (((0,), (0,)), ((), ())), preferred_element_type=F32
    )
    dconv_all = ddir[...] + lax.dot_general(
        dpre[...], wide_ref[...], (((1,), (1,)), ((), ())), preferred_element_type=F32
    )
    ddir[...] = dconv_all
    for lane in range(0, channels, LANES):
        own = slice(lane, lane + LANES)
        two = slice(channels + lane, channels + lane + LANES)
        dconv = ddir[:, own]
        sums_ref[1:2, own] += jnp.sum(dpre[:, own].astype(F32), axis=0, keepdims=True)
        sums_ref[2:3, own] += jnp.sum(dpre[:, two].astype(F32), axis=0, keepdims=True)
        sums_ref[3:4, own] += jnp.sum(dconv, axis=0, keepdims=True)
        sums_ref[4:5, own] += jnp.sum(dconv * zext[8 : 8 + rows, own], axis=0, keepdims=True)
        dz = dconv * conv_ref[0:1, own]
        edge = jnp.zeros((8, LANES), F32)
        at8 = lax.broadcasted_iota(jnp.int32, edge.shape, 0)
        for lag in range(1, span + 1):
            kept = dconv * mask_ref[:, lag : lag + 1]
            sums_ref[4 + lag : 5 + lag, own] += jnp.sum(
                kept * zext[8 - lag : 8 - lag + rows, own], axis=0, keepdims=True
            )
            moved[lag - 1, 0:rows, own] = kept * conv_ref[lag : lag + 1, own]
            dz = dz + moved[lag - 1, lag : lag + rows, own]
            edge = edge + jnp.where(
                at8 >= 8 - lag, pltpu.roll(moved[lag - 1, 0:8, own], 8 - lag, 0), 0.0
            )
        dz_ref[:, own] = dz.astype(BF16)
        edge_ref[0:8, own] = edge

        @pl.when(step == 0)
        def _():
            edge_ref[8:16, own] = dz[rows - 8 :]


def kernel_params(mib=48):
    return pltpu.CompilerParams(dimension_semantics=("arbitrary",), vmem_limit_bytes=mib * 1024 * 1024)


def forward_local(z, rim, mask, conv, wide, bias, rate):
    tokens, channels = z.shape[0], rate.shape[1]
    rows = min(ROWS, tokens)
    spec = lambda shape, index: pl.BlockSpec(shape, index)
    whole = lambda x: pl.BlockSpec(x.shape, lambda i: (0,) * x.ndim)
    time = lambda width, at=0: pl.BlockSpec((rows, width), lambda i: (i, at))
    fixed = pl.BlockSpec((8, channels), lambda i: (0, 0))
    return pl.pallas_call(
        forward_kernel,
        grid=(tokens // rows,),
        in_specs=[time(channels, 1), whole(rim), time(mask.shape[1]), whole(conv), whole(wide), whole(bias), whole(rate)],
        out_specs=[time(channels), time(2 * channels), time(channels), time(channels), fixed, fixed],
        out_shape=[
            jax.ShapeDtypeStruct((tokens, channels), BF16),
            jax.ShapeDtypeStruct((tokens, 2 * channels), F32),
            jax.ShapeDtypeStruct((tokens, channels), F32),
            jax.ShapeDtypeStruct((tokens, channels), F32),
            jax.ShapeDtypeStruct((8, channels), F32),
            jax.ShapeDtypeStruct((8, channels), F32),
        ],
        scratch_shapes=[pltpu.VMEM((rows + 8, channels), F32)],
        compiler_params=kernel_params(),
        cost_estimate=COST,
    )(z, rim, mask, conv, wide, bias, rate)


def backward_local(adj, tail, arrive, loc, prod, enter, gate, unit, mask, z, rim, conv, wide, rate, first_rows=0):
    tokens, channels = loc.shape
    rows = first_rows or min(ROWS, tokens)
    tokens = first_rows or tokens
    last = tokens // rows - 1
    whole = lambda x: pl.BlockSpec(x.shape, lambda i: (0,) * x.ndim)
    time = lambda width, at=0: pl.BlockSpec((rows, width), lambda i: (last - i, at))
    ahead = lambda size, at=0: pl.BlockSpec(
        (size, channels), lambda i: (jnp.maximum((last - i) * (rows // size) - 1, 0), at)
    )
    fixed = lambda size, width: pl.BlockSpec((size, width), lambda i: (0, 0))
    span = conv.shape[0] - 2
    return pl.pallas_call(
        backward_kernel,
        grid=(tokens // rows,),
        in_specs=[
            time(channels), time(channels), whole(arrive), time(channels), time(channels), ahead(8), ahead(8),
            whole(enter), time(2 * channels), time(channels), time(mask.shape[1]), time(channels, 1), ahead(16, 1),
            whole(rim), whole(conv), whole(wide), whole(rate),
        ],
        out_specs=[time(channels), fixed(channels, 2 * channels), fixed(16, channels), fixed(16, channels)],
        out_shape=[
            jax.ShapeDtypeStruct((tokens, channels), BF16),
            jax.ShapeDtypeStruct((channels, 2 * channels), F32),
            jax.ShapeDtypeStruct((16, channels), F32),
            jax.ShapeDtypeStruct((16, channels), F32),
        ],
        scratch_shapes=[
            pltpu.VMEM((rows, 2 * channels), BF16),
            pltpu.VMEM((rows, channels), F32),
            pltpu.VMEM((rows + 8, channels), F32),
            pltpu.VMEM((span, rows + 8, channels), F32),
        ],
        compiler_params=kernel_params(),
        cost_estimate=COST,
    )(adj, tail, arrive, loc, prod, loc, prod, enter, gate, unit, mask, z, z, rim, conv, wide, rate)


def pad_rows(x, rows, before=False):
    extra = rows - x.shape[0]
    return jnp.pad(x, ((extra, 0) if before else (0, extra), (0, 0)))


def pieces_of(width, where, count):
    cols = width // count
    for k in range(count):
        true = pl.ds(pl.multiple_of(where[k] * cols, LANES), cols) if count > 1 else slice(0, width)
        yield slice(k * cols, (k + 1) * cols), true


def norm_one_kernel(count, where, x_ref, gain_ref, h_ref):
    width = x_ref.shape[1]
    x = x_ref[...]
    rstd = lax.rsqrt(jnp.sum(x * x, axis=1, keepdims=True) * (1.0 / width) + NORM_EPS)
    for own, true in pieces_of(width, where, count):
        h_ref[:, own] = (x_ref[:, true] * rstd * gain_ref[:, own]).astype(BF16)


def first_norm_kernel(count, row, where, x_ref, *refs):
    parts, h_ref, gain_ref = refs[:count], refs[count], refs[count + 1]
    width = x_ref.shape[1]
    cols = width // count
    x = x_ref[...]
    rstd = lax.rsqrt(jnp.sum(x * x, axis=1, keepdims=True) * (1.0 / width) + NORM_EPS)
    for part, (own, true) in zip(parts, pieces_of(width, where, count)):
        gain = part[row : row + 1, 0:cols].astype(F32)
        h_ref[:, own] = (x_ref[:, true] * rstd * gain).astype(BF16)
        gain_ref[0:1, own] = gain
        gain_ref[1:2, own] = part[row : row + 1, cols : 2 * cols].astype(F32)


def first_norm_call(count, where, x, parts, part_rows, row):
    tokens, width = x.shape
    rows = min(ROWS, tokens)
    time = pl.BlockSpec((rows, width), lambda i, w: (i, 0))
    fixed = lambda shape: pl.BlockSpec(shape, lambda i, w: (0, 0))
    return pl.pallas_call(
        functools.partial(first_norm_kernel, count, row),
        grid_spec=pltpu.PrefetchScalarGridSpec(
            num_scalar_prefetch=1,
            grid=(tokens // rows,),
            in_specs=[time] + [fixed((part_rows, p.shape[1])) for p in parts],
            out_specs=[time, fixed((8, width))],
        ),
        out_shape=[jax.ShapeDtypeStruct((tokens, width), BF16), jax.ShapeDtypeStruct((8, width), F32)],
        compiler_params=kernel_params(),
        cost_estimate=COST,
    )(where, x, *parts)


def prepare_kernel(count, gates, part_ch, taps, cols, *refs):
    parts, (row_ref, head_ref, code_ref, col_ref, hot_ref, wide_ref, chan_ref, small) = refs[:count], refs[count:]
    channels = wide_ref.shape[0]
    stacked = jnp.concatenate([p[0:gates].astype(F32) for p in parts], axis=0).astype(BF16)
    inside = head_ref[...] == col_ref[0:1]
    for g in range(2):
        hot = (row_ref[...] == code_ref[g : g + 1]).astype(F32).astype(BF16)
        placed = jnp.dot(hot, stacked, preferred_element_type=F32)
        wide_ref[:, g * channels : (g + 1) * channels] = jnp.where(inside, placed, 0.0).astype(BF16)
    for k, part in enumerate(parts):
        small[k : k + 1] = part[gates : gates + 1].astype(F32)
        small[count + k : count + k + 1] = part[gates + 1 : gates + 2].astype(F32)
    ordered = [
        jnp.dot(hot_ref[...], small[s * count : (s + 1) * count].astype(BF16), preferred_element_type=F32).astype(BF16)
        for s in range(2)
    ]
    lane = lax.broadcasted_iota(jnp.int32, (channels, channels), 0)
    seq = lax.broadcasted_iota(jnp.int32, (count, channels), 0)
    wanted = [(1, y * part_ch) for y in range(taps + 3)] + [(0, 2 * cols)]
    for y, (s, offset) in enumerate(wanted):
        hot = (lane == col_ref[1:2] + offset).astype(F32).astype(BF16)
        spread = jnp.dot(ordered[s], hot, preferred_element_type=F32)
        chan_ref[y : y + 1] = jnp.sum(jnp.where(seq == col_ref[2:3], spread, 0.0), axis=0, keepdims=True)


def prepare_call(parts, true_all, place_hot, part_rows, part_in, block, part_ch, taps, cols):
    count = len(parts)
    channels = parts[0].shape[1]
    gates = 2 * part_in
    at = np.arange(channels)
    row_code = jnp.asarray((at % block // part_in * part_in + at % part_in)[:, None], jnp.int32)
    row_head = jnp.asarray((at // block)[:, None], jnp.int32)
    col = jnp.asarray(np.stack([at // block, at % part_ch, at // part_ch]), jnp.int32)
    code = true_all[:, None] * part_in + jnp.arange(part_in, dtype=jnp.int32)[None, :]
    none = jnp.full_like(code, -1)
    code = jnp.stack(
        [
            jnp.concatenate([code, none], axis=1).reshape(-1),
            jnp.concatenate([none, code], axis=1).reshape(-1),
        ]
    )
    whole = lambda x: pl.BlockSpec(x.shape, lambda i: (0, 0))
    args = (row_code, row_head, code, col, place_hot)
    return pl.pallas_call(
        functools.partial(prepare_kernel, count, gates, part_ch, taps, cols),
        grid=(1,),
        in_specs=[pl.BlockSpec((part_rows, channels), lambda i: (0, 0)) for _ in parts] + [whole(a) for a in args],
        out_specs=[
            pl.BlockSpec((channels, 2 * channels), lambda i: (0, 0)),
            pl.BlockSpec((taps + 4, channels), lambda i: (0, 0)),
        ],
        out_shape=[
            jax.ShapeDtypeStruct((channels, 2 * channels), BF16),
            jax.ShapeDtypeStruct((taps + 4, channels), F32),
        ],
        scratch_shapes=[pltpu.VMEM((2 * count, channels), F32)],
        compiler_params=kernel_params(),
        cost_estimate=COST,
    )(*parts, *args)


def low_kernel(count, where, x_ref, low_ref, true_ref):
    true_ref[...] = x_ref[...].astype(BF16)
    for own, true in pieces_of(x_ref.shape[1], where, count):
        low_ref[:, own] = true_ref[:, true]


def summed(refs, own):
    return sum(ref[:, own].astype(F32) for ref in refs[1:]) + refs[0][:, own].astype(F32)


def norm_two_kernel(count, where, x_ref, a_ref, b_ref, c_ref, gain_ref, resid_ref, h_ref):
    width = x_ref.shape[1]
    square = 0.0
    for own, true in pieces_of(width, where, count):
        resid = x_ref[:, true] + summed((a_ref, b_ref, c_ref), own)
        resid_ref[:, own] = resid
        square = square + jnp.sum(resid * resid, axis=1, keepdims=True)
    rstd = lax.rsqrt(square * (1.0 / width) + NORM_EPS)
    h_ref[...] = (resid_ref[...] * rstd * gain_ref[...]).astype(BF16)


def norm_two_back_kernel(count, where, cot_ref, a_ref, b_ref, c_ref, gain_ref, resid_ref, d_resid_ref, low_ref):
    width = cot_ref.shape[1]
    resid = resid_ref[...]
    rstd = lax.rsqrt(jnp.sum(resid * resid, axis=1, keepdims=True) * (1.0 / width) + NORM_EPS)
    along = 0.0
    for own, _ in pieces_of(width, where, count):
        d_normed = summed((a_ref, b_ref, c_ref), own) * gain_ref[:, own]
        d_resid_ref[:, own] = d_normed
        along = along + jnp.sum(d_normed * resid_ref[:, own], axis=1, keepdims=True)
    along = along * rstd * (1.0 / width)
    for own, true in pieces_of(width, where, count):
        d_resid = cot_ref[:, true] + rstd * (d_resid_ref[:, own] - resid_ref[:, own] * rstd * along)
        d_resid_ref[:, own] = d_resid
        low_ref[:, own] = d_resid.astype(BF16)


def pick(where, mine_ref, other_ref, own, per):
    is_mine = (pl.program_id(0) // per) == where[where.shape[0] - 1]
    return jnp.where(is_mine, mine_ref[:, own], other_ref[:, own]).astype(F32)


def norm_one_whole_kernel(count, per, where, x_ref, mine_ref, other_ref, gain_ref, d_resid_ref, *refs):
    out_ref = refs[-1]
    width = x_ref.shape[1]
    x = x_ref[...]
    rstd = lax.rsqrt(jnp.sum(x * x, axis=1, keepdims=True) * (1.0 / width) + NORM_EPS)
    along = 0.0
    for own, true in pieces_of(width, where, count):
        d_normed = pick(where, mine_ref, other_ref, own, per) * gain_ref[:, own]
        along = along + jnp.sum(d_normed * x_ref[:, true], axis=1, keepdims=True)
    along = along * rstd * (1.0 / width)
    for own, true in pieces_of(width, where, count):
        d_normed = pick(where, mine_ref, other_ref, own, per) * gain_ref[:, own]
        out_ref[:, true] = d_resid_ref[:, own].astype(F32) + rstd * (d_normed - x_ref[:, true] * rstd * along)


def norm_call(kernel, count, where, x, gain, outputs=1, slots=False):
    tokens, width = x.shape
    rows = min(ROWS, tokens // 4)
    per = tokens // 4 // rows
    time = pl.BlockSpec((rows, width), lambda i, w: (i, 0))
    moved = pl.BlockSpec((rows, width), lambda i, w: (w[count + i // per] * per + i % per, 0))
    args = (x,) if gain is None else (x, gain)
    return pl.pallas_call(
        functools.partial(kernel, count),
        grid_spec=pltpu.PrefetchScalarGridSpec(
            num_scalar_prefetch=1,
            grid=(tokens // rows,),
            in_specs=[moved if slots else time] + [pl.BlockSpec(a.shape, lambda i, w: (0, 0)) for a in args[1:]],
            out_specs=[time] * outputs,
        ),
        out_shape=[jax.ShapeDtypeStruct((tokens, width), BF16)] * outputs,
        compiler_params=kernel_params(),
        cost_estimate=COST,
    )(where, *args)


def own_call(kernel, count, where, x, total, gain, extra, out_types, scratch=False):
    tokens, width = x.shape
    rows = min(64, tokens // 4)
    per = tokens // 4 // rows
    time = pl.BlockSpec((rows, width), lambda i, w: (i, 0))
    true = pl.BlockSpec((rows, width), lambda i, w: (w[count] * per + i, 0))
    args = (x, total.own, total.core, total.far, gain) + extra
    return pl.pallas_call(
        functools.partial(kernel, count),
        grid_spec=pltpu.PrefetchScalarGridSpec(
            num_scalar_prefetch=1,
            grid=(per,),
            in_specs=[true, time, time, time, pl.BlockSpec(gain.shape, lambda i, w: (0, 0))] + [time] * len(extra),
            out_specs=[time] * len(out_types),
            scratch_shapes=[pltpu.VMEM((rows, width), F32)] if scratch else [],
        ),
        out_shape=[jax.ShapeDtypeStruct((tokens // 4, width), t) for t in out_types],
        compiler_params=kernel_params(),
        cost_estimate=COST,
    )(where, *args)


def sum_call(kernel, count, where, summed, x, gain, extra, out_types):
    tokens, width = x.shape
    rows = min(ROWS, tokens // 4)
    per = tokens // 2 // rows
    last = where.shape[0] - 1
    time = pl.BlockSpec((rows, width), lambda i, w: (i, 0))
    each = tokens // 4 // rows
    slot = pl.BlockSpec((rows, width), lambda i, w: (w[count + 4 + i // each] * each + i % each, 0))
    mine = pl.BlockSpec((rows, width), lambda i, w: (jnp.clip(i - w[last] * per, 0, per - 1), 0))
    other = pl.BlockSpec((rows, width), lambda i, w: (jnp.clip(i - (1 - w[last]) * per, 0, per - 1), 0))
    args = (x, summed.mine, summed.other, gain) + extra
    gain_spec = pl.BlockSpec(gain.shape, lambda i, w: (0, 0))
    return pl.pallas_call(
        functools.partial(kernel, count, per),
        grid_spec=pltpu.PrefetchScalarGridSpec(
            num_scalar_prefetch=1,
            grid=(tokens // rows,),
            in_specs=[time, mine, other, gain_spec] + [slot] * len(extra),
            out_specs=[time] * len(out_types),
        ),
        out_shape=[jax.ShapeDtypeStruct((tokens, width), t) for t in out_types],
        compiler_params=kernel_params(),
        cost_estimate=COST,
    )(where, *args)


def weight_call(
    body, pieces, target, rows, inputs, fixed, outputs, scalars, scratch=(), steps=None, spots=None, earlier=()
):
    tokens = inputs[0].shape[0]
    steps = tokens // rows if steps is None else steps
    same = lambda i, s: i
    read, write = spots if spots else (None, same)
    read = read or [same] * len(inputs)
    count = len(pieces)

    def kernel(scalar_ref, *refs):
        shard_refs, refs = refs[:count], refs[count:]
        weight, sem = refs[-2:]

        @pl.when(pl.program_id(0) == 0)
        def _():
            copies = []
            for n, (ref, (_, place)) in enumerate(zip(shard_refs, pieces)):
                for m, (source, to) in enumerate(place(scalar_ref)):
                    copies.append(pltpu.make_async_copy(ref.at[source], weight.at[to], sem.at[n, m]))
            for copy in copies:
                copy.start()
            for copy in copies:
                copy.wait()

        skip = len(inputs) + len(fixed)
        body(scalar_ref, weight, *refs[:skip], *refs[skip + len(earlier) : -2])

    whole = lambda x: pl.BlockSpec(x.shape, lambda i, s: (0,) * x.ndim)
    in_specs = [pl.BlockSpec(memory_space=pl.ANY)] * count
    for x, at in zip(inputs, read):
        in_specs.append(pl.BlockSpec((rows, x.shape[1]), lambda i, s, at=at: (at(i, s), 0)))
    in_specs += [whole(x) for x in fixed] + [pl.BlockSpec(memory_space=pl.ANY)] * len(earlier)
    out_specs, out_shape = [], []
    for o in outputs:
        if len(o) == 2:
            out_specs.append(pl.BlockSpec((rows, o[0]), lambda i, s: (write(i, s), 0)))
            out_shape.append(jax.ShapeDtypeStruct((tokens, o[0]), o[1]))
        else:
            out_specs.append(pl.BlockSpec(o[:2], lambda i, s: (0, 0)))
            out_shape.append(jax.ShapeDtypeStruct(o[:2], o[2]))
    first = 1 + count + len(inputs) + len(fixed)
    return pl.pallas_call(
        kernel,
        grid_spec=pltpu.PrefetchScalarGridSpec(
            num_scalar_prefetch=1,
            grid=(steps,),
            in_specs=in_specs,
            out_specs=out_specs,
            scratch_shapes=list(scratch) + [pltpu.VMEM(target, BF16), pltpu.SemaphoreType.DMA((count, 16))],
        ),
        out_shape=out_shape,
        input_output_aliases={first + i: i for i in range(len(earlier))},
        compiler_params=kernel_params(60 if count > 12 else 48),
        cost_estimate=COST,
    )(scalars, *[array for array, _ in pieces], *inputs, *fixed, *earlier)


def row_pieces(ring_gather, cols, lane, skip=0):
    out = []
    for array, k, half in ring_gather.pieces():
        first = array.shape[0] if half == 1 else 0
        begin = max(skip - first, 0)
        size = array.shape[0] - begin
        if size > 0:
            place = lambda s, begin=begin, start=k * cols + first + begin - skip, size=size: [
                ((pl.ds(begin, size),), (pl.ds(start, size), lane(s)))
            ]
            out.append((array, place))
    return out


def col_pieces(ring_gather, cols):
    if cols % LANES:
        return [(jnp.concatenate(ring_gather.parts, axis=1), lambda s: [((slice(None),), (slice(None),))])]
    out = []
    for array, k, half in ring_gather.pieces():
        size = array.shape[0]
        start = size if half == 1 else 0
        out.append(
            (
                array,
                lambda s, start=start, size=size, k=k: [
                    ((slice(None),), (pl.ds(start, size), pl.ds(k * cols, cols)))
                ],
            )
        )
    return out


NT = (((1,), (1,)), ((), ()))


def product_body(where, weight, x_ref, out_ref):
    out_ref[...] = jnp.dot(x_ref[...], weight[...], preferred_element_type=F32).astype(BF16)


def to_quarter(slot, refs, value):
    for s, ref in enumerate(refs):

        @pl.when(slot == s)
        def _():
            ref[...] = value.astype(BF16)


def product_nt_body(where, weight, x_ref, *out_refs):
    part = lax.dot_general(x_ref[...], weight[...], NT, preferred_element_type=F32)
    to_quarter(pl.program_id(0), out_refs, part)


def output_body(count, where, weight, hidden_ref, *refs):
    attn_refs, out_ref, part = refs[:4], refs[4], refs[5]
    part[...] = jnp.dot(hidden_ref[...], weight[...], preferred_element_type=F32)
    width = part.shape[1]
    for slot, ref in enumerate(attn_refs):

        @pl.when(pl.program_id(0) == slot)
        def _():
            part[...] += ref[...].astype(F32)

    cols = width // count
    for k in range(count):
        own = slice(k * cols, (k + 1) * cols)
        to = pl.ds(pl.multiple_of(where[count + 8 + k] * cols, LANES), cols) if count > 1 else own
        out_ref[:, to] = part[:, own].astype(BF16)


def mixed_body(count, where, weight, z_ref, loc_ref, prod_ref, enter_ref, mixed_ref, *out_refs):
    channels = loc_ref.shape[1]
    act, _ = gelu_both(z_ref[:, :channels].astype(F32))
    mixed_ref[...] = (act * (loc_ref[...] + prod_ref[...] * enter_ref[...])).astype(BF16)
    part = jnp.dot(mixed_ref[...], weight[...], preferred_element_type=F32)
    to_quarter(where[count + 4 + pl.program_id(0)], out_refs, part)


def gate_up_body(where, weight, h_ref, hidden_ref, act_ref, slope_ref, both):
    units = hidden_ref.shape[1]
    both[...] = jnp.dot(h_ref[...], weight[...], preferred_element_type=F32)
    for lane in range(0, units, LANES):
        own = slice(lane, lane + LANES)
        act, slope = gelu_both(both[:, own])
        up = both[:, units + lane : units + lane + LANES]
        hidden_ref[:, own] = (act * up).astype(BF16)
        act_ref[:, own] = act.astype(BF16)
        slope_ref[:, own] = (slope * up).astype(BF16)


def d_hidden_body(where, weight, d_ref, act_ref, slope_ref, out_ref):
    units = act_ref.shape[1]
    d_hidden = lax.dot_general(d_ref[...], weight[...], NT, preferred_element_type=F32)
    out_ref[:, :units] = (d_hidden * slope_ref[...].astype(F32)).astype(BF16)
    out_ref[:, units:] = (d_hidden * act_ref[...].astype(F32)).astype(BF16)


def d_h_one_body(where, weight, dzg_ref, dzr_ref, out_ref):
    channels = dzg_ref.shape[1]
    gate = lax.dot_general(dzg_ref[...], weight[:, :channels], NT, preferred_element_type=F32)
    rec = lax.dot_general(dzr_ref[...], weight[:, channels:], NT, preferred_element_type=F32)
    out_ref[...] = (gate + rec).astype(BF16)


def per_device(
    inputs,
    lengths,
    norm_gain1,
    in_weight,
    conv_weight,
    conv_bias,
    gate_weight,
    gate_bias,
    decay_param,
    out_weight,
    norm_gain2,
    mlp_in,
    mlp_down,
    cotangent,
):
    tokens, width = inputs.shape
    count, index = lax.axis_size("seq"), lax.axis_index("seq")
    br, ch = lax.axis_index("br"), lax.axis_index("ch")
    place = ring_place(index, count)
    cols = width // count
    taps = conv_weight.shape[0]
    span = taps - 1
    part_ch = conv_weight.shape[3]
    channels = part_ch * count
    hidden_units = mlp_down.shape[0]
    heads, part_in, block = gate_weight.shape[3], gate_weight.shape[4], gate_weight.shape[5]
    ahead = (place + jnp.arange(count, dtype=jnp.int32)) % count
    true_all = jnp.where(ahead < count // 2, 2 * ahead, 2 * (count - 1 - ahead) + 1)
    ring_index = (ring_place(jnp.arange(count, dtype=jnp.int32), count) - place) % count
    true_of = [true_all[k] for k in range(count)]
    ring_of = [ring_index[k] for k in range(count)]
    aligned = cols % LANES == 0

    def move(x, at):
        return jnp.concatenate(
            [lax.dynamic_slice_in_dim(x, a * cols, cols, 1) for a in at], axis=1
        )

    quarter = tokens // 4
    me = ch * 2 + br
    quarters = me ^ jnp.asarray([0, 2, 1, 3], jnp.int32)
    slots = me ^ jnp.arange(4, dtype=jnp.int32)
    slots = (slots % 2) * 2 + slots // 2
    per_device_cols = count // 4
    to = true_all // per_device_cols
    dealt = (((to % 2) ^ ch) * 2 + ((to // 2) ^ br)) * per_device_cols + true_all % per_device_cols
    whole_inputs = inputs
    if aligned:
        n_pieces = count
        where = jnp.concatenate([true_all, quarters, slots, dealt, br[None], ch[None]]).astype(jnp.int32)
    else:
        n_pieces = 1
        zero = jnp.zeros((1,), jnp.int32)
        where = jnp.concatenate([zero, quarters, slots, zero, br[None], ch[None]]).astype(jnp.int32)
        inputs, cotangent = move(inputs, true_of), move(cotangent, true_of)

    ring = Ring(count)

    fold = 2 * block
    gate_rows = heads * part_in
    packed_gates = 2 * part_in

    def one_row(*arrays):
        row = jnp.concatenate([a.reshape(-1) for a in arrays])
        return jnp.pad(row, (0, channels - row.shape[0]))[None]

    packed = jnp.concatenate(
        [
            gate_weight[:, 0, 0].transpose(0, 2, 1, 3).reshape(packed_gates, channels),
            one_row(norm_gain1, norm_gain2, decay_param),
            one_row(conv_weight, conv_bias, gate_bias),
        ],
        axis=0,
    )
    packed_rows = -(-(cols + packed.shape[0]) // 32) * 32 - cols
    packed = pad_rows(packed, packed_rows)

    own_cols = lax.dynamic_slice_in_dim(in_weight[0], br * channels, channels, 1)
    far_cols = lax.ppermute(
        lax.dynamic_slice_in_dim(in_weight[0], (1 - br) * channels, channels, 1), "br", SWAP
    )
    own_and_packed = jnp.concatenate([packed, own_cols], axis=0)
    in_own, in_far = Gather(ring, own_and_packed), Gather(ring, far_cols)
    out_ring = Gather(ring, out_weight[0, 0])
    down_ring = Gather(ring, mlp_down)
    in_own.hop()
    in_far.hop()
    own_first, far_first = in_own.last, in_far.last
    in_own.hop()
    in_far.hop()
    own_second, far_second = in_own.last, in_far.last
    for _ in range(2):
        in_own.hop()
        in_far.hop()
    mlp_all = lax.all_gather(after(mlp_in, *in_own.last, *in_far.last), "seq", axis=1, tiled=True)
    out_ring.hop()

    doc_starts = jnp.cumsum(lengths) - lengths
    positions = jnp.arange(tokens + span, dtype=jnp.int32) + index * tokens - span
    doc_ext = jnp.sum((positions[:, None] >= doc_starts[None, 1:]).astype(jnp.int32), axis=1)
    lags = [
        (doc_ext[span - lag : span - lag + tokens] == doc_ext[span:]).astype(F32) for lag in range(taps)
    ]
    reset = jnp.any(positions[span:, None] == doc_starts[None, :], axis=1).astype(F32)
    mask = jnp.stack(lags + [reset], axis=1)

    place_hot = (ring_index[:, None] == jnp.arange(count)[None, :]).astype(BF16)
    row = jnp.arange(channels)
    row_head, row_in = row // block, row % block
    row_seq = row_in // part_in
    row_place = (jnp.where(row_seq % 2 == 0, row_seq // 2, count - 1 - row_seq // 2) - place) % count
    source = row_place * gate_rows + row_head * part_in + row_in % part_in
    row_hot = (source[:, None] == jnp.arange(channels)[None, :]).astype(BF16)
    wide_col = jnp.arange(2 * channels)
    wide_gate, wide_head, wide_out = (
        wide_col // channels,
        (wide_col % channels) // block,
        wide_col % block,
    )
    spread_hot = (jnp.arange(fold)[:, None] == (wide_gate * block + wide_out)[None, :]).astype(BF16)
    on_block = (row_head[:, None] == wide_head[None, :]).astype(BF16)
    scalars = where
    last_at = where.shape[0] - 2
    firsts = [in_own.last[0] if k == count // 2 else in_own.parts[k] for k in range(count)]
    if aligned:
        h_one, gains = first_norm_call(n_pieces, where, inputs, firsts, packed_rows, packed_gates)
        gain_one, gain_two = gains[0:1], gains[1:2]
    else:
        rows = jnp.stack([part[packed_gates] for part in firsts]).astype(F32)
        gain_one, gain_two = rows[:, :cols].reshape(1, width), rows[:, cols : 2 * cols].reshape(1, width)
        (h_one,) = norm_call(norm_one_kernel, n_pieces, where, inputs, gain_one)
    in_pieces = row_pieces(
        in_own, cols, lambda s: pl.ds(pl.multiple_of(s[last_at] * channels, LANES), channels), packed_rows
    )
    in_pieces += row_pieces(
        in_far, cols, lambda s: pl.ds(pl.multiple_of((1 - s[last_at]) * channels, LANES), channels)
    )
    in_shape = (width, 2 * channels)
    (z_last,) = weight_call(
        product_body, in_pieces, in_shape, 16, (h_one[tokens - 16 :],), (), [(2 * channels, BF16)], scalars
    )
    if aligned:
        wide, chan = prepare_call(
            [after(firsts[0], z_last)] + firsts[1:], true_all, place_hot, packed_rows, part_in, block, part_ch, taps, cols
        )
    else:
        rows = jnp.stack([part[packed_gates : packed_gates + 2] for part in firsts])
        chan = jnp.concatenate([rows[:, 1, : (taps + 3) * part_ch], rows[:, 0, 2 * cols : 2 * cols + part_ch]], axis=1)
        chan = jnp.dot(place_hot, chan, preferred_element_type=F32).reshape(count, taps + 4, part_ch)
        chan = chan.transpose(1, 0, 2).reshape(taps + 4, channels)
        every = jnp.stack([part[:packed_gates].reshape(-1) for part in firsts])
        every = jnp.dot(place_hot, every, preferred_element_type=F32).astype(BF16)
        every = every.reshape(count, 2, part_in, heads, block).transpose(3, 0, 2, 1, 4)
        wide = every[:, :, :, :, None, :] * jnp.eye(heads, dtype=BF16)[:, None, None, None, :, None]
        wide = wide.reshape(channels, 2 * channels)
    conv = chan[: taps + 1]
    gate_bias_all = chan[taps + 1 : taps + 3].reshape(1, 2 * channels)
    decay_rate = chan[taps + 3 : taps + 4]
    rate = -DECAY_SCALE * jax.nn.softplus(-decay_rate)
    forward_pairs = [(i, i + 1) for i in range(count - 1)]
    rim = lax.ppermute(z_last[8:, channels:], "seq", forward_pairs).astype(F32)
    (z,) = weight_call(
        product_body, in_pieces, in_shape, quarter, (after(h_one, z_last),), (), [(2 * channels, BF16)], scalars
    )
    ring.mark = (z, rim, wide)
    out_first = out_ring.last
    out_ring.hop()

    unit, gates, loc, prod, last, total = forward_local(
        after(z, *out_first), rim, mask, conv, wide, gate_bias_all, rate
    )
    ring.mark = (last,)
    out_second = out_ring.last
    out_ring.hop()
    enter = entering(after(last[:2], *out_second), False)[None]
    ring.mark = (enter,)
    out_third = out_ring.last
    out_ring.hop()
    down_ring.hop()

    to_slot = lambda i, s: s[n_pieces + 4 + i]
    from_slot = lambda i, s: s[n_pieces + i]
    out_pieces = col_pieces(out_ring, cols)
    out_shape = (channels, width)
    one_quarter = (quarter, width, BF16)
    mixed, *attn_parts = weight_call(
        functools.partial(mixed_body, n_pieces), out_pieces, out_shape, quarter, (z, loc, prod),
        (after(enter, *out_third),), [(channels, BF16)] + [one_quarter] * 4, scalars, spots=(None, to_slot),
    )
    attn = TokenSum()
    attn.second(*attn_parts[2:])
    attn.cross()
    attn.first(*attn_parts[:2])
    down_first = down_ring.last
    ring.mark = (attn.chip,)
    down_ring.hop()
    d_mlp, slot_cot = norm_call(low_kernel, n_pieces, where, after(cotangent, attn.chip), None, 2, slots=True)
    if not aligned:
        slot_cot = move(slot_cot, ring_of)

    resid, h_own = own_call(
        norm_two_kernel, n_pieces, where, inputs, attn, after(gain_two, d_mlp, *down_first), (), (F32, BF16)
    )
    h_two = TokenGather(h_own)
    down_second = down_ring.last
    ring.mark = (h_own,)
    down_ring.hop()
    h_two = after(jnp.concatenate(h_two.parts(), axis=0), *down_second)
    down_third = down_ring.last
    ring.mark = (h_two,)
    down_ring.hop()


    def mlp_place(s):
        out = []
        for k in range(count):
            rows = pl.ds(pl.multiple_of(s[k] * cols, 8), cols)
            for g in range(2):
                out.append(
                    ((g, rows), (pl.ds(k * cols, cols), pl.ds(g * hidden_units, hidden_units)))
                )
        return out

    if aligned:
        mlp_pieces = [(mlp_all, mlp_place)]
    else:
        moved = [lax.dynamic_slice_in_dim(mlp_all, a * cols, cols, 1) for a in true_of]
        mlp_pieces = [
            (
                jnp.concatenate(moved, axis=1),
                lambda s: [
                    ((g,), (slice(None), pl.ds(g * hidden_units, hidden_units))) for g in range(2)
                ],
            )
        ]
    mlp_shape = (width, 2 * hidden_units)
    hidden, act, slope = weight_call(
        gate_up_body, mlp_pieces, mlp_shape, quarter, (after(h_two, *down_third),), (),
        [(hidden_units, BF16)] * 3, scalars, scratch=(pltpu.VMEM((quarter, 2 * hidden_units), F32),),
    )

    def chunk(x, k):
        return x[:, k * cols : (k + 1) * cols]

    def outer(left, right):
        return lax.dot_general(left, right, (((0,), (0,)), ((), ())), preferred_element_type=F32)

    down_pieces = col_pieces(down_ring, cols)
    down_shape = (hidden_units, width)
    (d_gate_up,) = weight_call(
        d_hidden_body, down_pieces, down_shape, quarter, (after(d_mlp, hidden), act, slope), (),
        [(2 * hidden_units, BF16)], scalars,
    )
    ring.mark = (d_gate_up,)
    g_mlp = Scatter(ring, lambda k, *t: outer(chunk(h_two, k), after(d_gate_up, *t)))
    g_mlp.hop()
    mlp_hop = [g_mlp.last]
    upper, lower = lambda i, s: i + 2, lambda i, s: i
    part = weight_call(
        product_nt_body, mlp_pieces, mlp_shape, quarter, (d_gate_up,), (), [one_quarter] * 2, scalars,
        steps=2, spots=([upper], upper),
    )
    d_h_two = TokenSum()
    d_h_two.second(*part)
    d_h_two.cross()
    part = weight_call(
        product_nt_body, mlp_pieces, mlp_shape, quarter, (after(d_gate_up, d_h_two.chip),), (), [one_quarter] * 2,
        scalars, steps=2, spots=([lower], lower),
    )
    d_h_two.first(*part)
    ring.mark = (part[0],)
    g_mlp.hop()
    mlp_hop.append(g_mlp.last)
    d_resid, d_attn = own_call(
        norm_two_back_kernel, n_pieces, where, cotangent, d_h_two, gain_two, (resid,), (F32, BF16)
    )
    d_attn = TokenGather(d_attn)

    (o_part,) = weight_call(
        functools.partial(output_body, n_pieces), down_pieces, down_shape, quarter,
        (after(hidden, d_attn.own),), tuple(attn_parts), [(width, BF16)], scalars, spots=(None, from_slot),
        scratch=(pltpu.VMEM((quarter, width), F32),),
    )
    if not aligned:
        at = jnp.arange(count)
        o_part = move(o_part, [jnp.sum(jnp.where(dealt == k, at, 0)) for k in range(count)])
    o_cols = width // 4
    ring.mark = (d_attn.own,)
    mlp_first = mlp_hop[1]
    g_mlp.hop()
    mlp_hop.append(g_mlp.last)
    d_attn = jnp.concatenate(d_attn.parts(), axis=0)
    rows = min(ROWS, quarter)
    per = quarter // rows
    last_step = tokens // rows - 1
    back = lambda i, s: last_step - i
    back_slot = lambda i, s: s[n_pieces + 4 + (last_step - i) // per] * per + (last_step - i) % per
    adj, tail, d_z_gate, head = weight_call(
        adjoint_body, out_pieces, out_shape, rows, (d_attn, z, loc, prod, gates, mask), (enter, rate),
        [(channels, F32), (channels, F32), (channels, BF16), (8, channels, F32)], scalars,
        scratch=(pltpu.VMEM((rows, channels), F32), pltpu.VMEM((8, channels), F32)),
        spots=([back_slot] + [back] * 5, back),
    )
    swapped = lax.ppermute(after(o_part[:, 2 * o_cols :], head), "ch", SWAP).astype(F32)
    g_down_part = outer(after(hidden, head), slot_cot).astype(BF16)
    o_far = (o_part[:, o_cols : 2 * o_cols].astype(F32) + after(swapped, g_down_part)[:, o_cols:]).astype(BF16)
    ring.mark = (head,)
    g_out = Scatter(ring, lambda k, *t: outer(after(mixed, *t), chunk(d_attn, k)))
    g_out.hop()
    out_hop = [g_out.last]
    arrive = entering(after(head[:2], *mlp_hop[2], g_down_part, o_far), True)[None]
    g_down = lax.psum_scatter(after(g_down_part, arrive), "seq", scatter_dimension=1, tiled=True)
    o_far = lax.ppermute(after(o_far, arrive), "br", SWAP)
    o_inputs = lax.dynamic_slice_in_dim(whole_inputs, (br * 2 + ch) * o_cols, o_cols, 1)
    output = o_inputs + o_part[:, :o_cols].astype(F32) + swapped[:, :o_cols] + o_far.astype(F32)
    back_args = (loc, prod, enter, gates, unit, mask, z, rim, conv, wide, rate)
    edge = backward_local(adj, tail, arrive, *back_args, first_rows=16)[3]
    backward_pairs = [(i + 1, i) for i in range(count - 1)]
    from_next = lax.ppermute(edge[:8], "seq", backward_pairs)
    ring.mark = (from_next,)
    g_mlp.hop()
    mlp_hop.append(g_mlp.last)
    d_z_rec, g_wide, sums, edge = backward_local(
        adj, tail, after(arrive, from_next, *out_hop[0]), *back_args
    )
    edge = after(edge, o_far)
    ring.mark = (edge,)
    g_out.hop()
    out_hop.append(g_out.last)
    fixed = (edge[8:] + from_next).astype(BF16)
    d_z_rec = d_z_rec.at[tokens - 8 :].set(fixed)

    d_z = jnp.concatenate([d_z_gate, d_z_rec], axis=1)
    g_in_ring = Scatter(ring, lambda k, *t: outer(chunk(h_one, k), after(d_z, *t)))
    ring.mark = (d_z,)
    g_in_ring.hop()
    (d_h_part,) = weight_call(
        d_h_one_body, in_pieces, in_shape, quarter, (d_z_gate, d_z_rec), (), [(width, BF16)], scalars
    )
    d_h_one = GroupSum(d_h_part)
    ring.mark = (d_h_part,)
    in_hop = [g_in_ring.last]
    g_in_ring.hop()
    d_h_one.chip(*in_hop[0])
    d_h_one.cross()
    ring.mark = (d_h_one.chip_sum,)
    g_out.hop()

    g_compact = lax.dot_general(
        (after(g_wide, d_h_one.chip_sum) * on_block.astype(F32)).astype(BF16),
        spread_hot,
        (((1,), (1,)), ((), ())),
        preferred_element_type=F32,
    ).astype(BF16)
    g_gates = lax.dot_general(row_hot, g_compact, (((0,), (0,)), ((), ())), preferred_element_type=F32)
    g_decay = sums[0:1] * -DECAY_SCALE * -jax.nn.sigmoid(-decay_rate)
    g_chan = jnp.concatenate([sums[4 : 4 + taps], sums[3:4], sums[1:3], g_decay, total[0:1]], axis=0)
    g_chan = g_chan.reshape(taps + 5, count, part_ch).transpose(1, 0, 2).reshape(count, -1)
    g_small = lax.dot_general(
        place_hot.astype(F32), g_chan, (((0,), (0,)), ((), ())), precision=lax.Precision.HIGHEST
    )
    g_rows = -(-g_small.shape[1] // fold)
    g_small = jnp.pad(g_small, ((0, 0), (0, g_rows * fold - g_small.shape[1]))).reshape(count, g_rows, fold)
    g_packed = jnp.concatenate([g_gates.reshape(count, gate_rows, fold), g_small], axis=1)
    total_rows = -(-g_packed.shape[1] // 32) * 32
    g_packed = jnp.pad(g_packed, ((0, 0), (0, total_rows - g_packed.shape[1]), (0, 0)))
    g_packed_ring = Scatter(ring, lambda k, *t: g_packed[k], free=True)
    for _ in range(4):
        g_packed_ring.hop()
    in_hop.append(g_in_ring.last)
    g_in_ring.hop()
    in_hop.append(g_in_ring.last)
    d_h_one.total(*in_hop[1])
    g_out.hop()
    g_in_ring.hop()
    (inputs_grad,) = sum_call(
        functools.partial(norm_one_whole_kernel), n_pieces, where, d_h_one, inputs, after(gain_one, *in_hop[2]),
        (d_attn,), (F32,)
    )
    if not aligned:
        inputs_grad = move(inputs_grad, ring_of)

    g_in_own = g_in_ring.result()
    g_in_gate, g_in_rec = g_in_own[:, :channels], g_in_own[:, channels:]
    keep_half = jnp.where(br == 0, g_in_gate, g_in_rec)
    send_half = jnp.where(br == 0, g_in_rec, g_in_gate).astype(BF16)
    got_half = lax.ppermute(send_half, "br", SWAP).astype(F32)
    g_in = jnp.concatenate(
        [jnp.where(br == 0, keep_half, got_half), jnp.where(br == 0, got_half, keep_half)], axis=1
    )
    g_mlp_own = g_mlp.result()
    g_gate_own, g_up_own = g_mlp_own[:, :hidden_units], g_mlp_own[:, hidden_units:]
    w_gate = jnp.where(br == 0, own_cols, far_cols).astype(F32)
    w_rec = jnp.where(br == 0, far_cols, own_cols).astype(F32)
    gains = jnp.stack(
        [
            jnp.sum(g_in_gate * w_gate, axis=1) + jnp.sum(g_in_rec * w_rec, axis=1),
            jnp.sum(g_gate_own * mlp_in[0].astype(F32), axis=1)
            + jnp.sum(g_up_own * mlp_in[1].astype(F32), axis=1),
        ]
    )
    gains = tiny_group_sum(gains)
    g_own = g_packed_ring.result()
    g_gate_w = g_own[:gate_rows].reshape(heads, part_in, 2, block).transpose(2, 0, 1, 3)[:, None, None]
    g_flat = g_own[gate_rows : gate_rows + g_rows].reshape(-1)
    g_chan = g_flat[: (taps + 5) * part_ch].reshape(taps + 5, part_ch)
    return (
        output,
        inputs_grad,
        gains[0] / norm_gain1.astype(F32),
        g_in[None],
        g_chan[:taps][:, None, None],
        g_chan[taps][None, None],
        g_gate_w,
        g_chan[taps + 1 : taps + 3][:, None, None],
        g_chan[taps + 3][None, None],
        g_out.result()[None, None],
        gains[1] / norm_gain2.astype(F32),
        jnp.stack([g_gate_own, g_up_own]),
        g_down.astype(F32),
        g_chan[taps + 4][None, None] / (tokens * count),
    )


def solution(mesh):
    placed = (
        P("seq", None),
        P(),
        P("seq"),
        P("br", "seq", "ch"),
        P(None, "ch", "br", "seq"),
        P("ch", "br", "seq"),
        P(None, "ch", "br", None, "seq", None),
        P(None, "ch", "br", "seq"),
        P("ch", "br", "seq"),
        P("ch", "br", None, "seq"),
        P("seq"),
        P(None, "seq", ("br", "ch")),
        P(("br", "ch"), "seq"),
        P("seq", None),
    )
    return jax.shard_map(
        per_device,
        mesh=mesh,
        in_specs=placed,
        out_specs=(
            P("seq", ("br", "ch")),
            P("seq", None),
            P("seq"),
            P("br", "seq", "ch"),
            P(None, "ch", "br", "seq"),
            P("ch", "br", "seq"),
            P(None, "ch", "br", None, "seq", None),
            P(None, "ch", "br", "seq"),
            P("ch", "br", "seq"),
            P("ch", "br", None, "seq"),
            P("seq"),
            P(None, "seq", ("br", "ch")),
            P(("br", "ch"), "seq"),
            P("ch", "br", "seq"),
        ),
        check_vma=False,
    )
```

```python
import functools

import jax
import jax.numpy as jnp
import numpy as np
from jax import lax
from jax.experimental import pallas as pl
from jax.experimental.pallas import tpu as pltpu
from jax.sharding import PartitionSpec as P

NORM_EPS = 1e-06
DECAY_SCALE = 8.0
GELU_C = 0.7978845608028654
GELU_K = 0.044715
LANES = 128
ROWS = 128
SWAP = [(0, 1), (1, 0)]
F32 = jnp.float32
BF16 = jnp.bfloat16
COST = pl.CostEstimate(flops=0, bytes_accessed=0, transcendentals=0)


def after(x, *others):
    if not others:
        return x
    return lax.optimization_barrier((x,) + others)[0]


def ring_order(count):
    return list(range(0, count, 2)) + list(range(count - 1, 0, -2))


def ring_place(index, count):
    half = index // 2
    return jnp.where(index % 2 == 0, half, count - 1 - half)


class Ring:
    def __init__(self, count, depth=3):
        order = ring_order(count)
        self.count = count
        self.half = count // 2
        self.reps = max(1, self.half // 4)
        self.pairs = {
            1: [(order[i], order[(i + 1) % count]) for i in range(count)],
            -1: [(order[(i + 1) % count], order[i]) for i in range(count)],
        }
        self.done = {1: [], -1: []}
        self.depth = depth
        self.mark = ()

    def hop(self, x, way, free=False):
        if not free:
            held = self.done[way]
            others = self.mark + tuple(held[-self.depth :][:1] if len(held) >= self.depth else ())
            if others:
                x = after(x, *others)
        got = lax.ppermute(x, "seq", self.pairs[way])
        if not free:
            self.done[way].append(got)
        return got


class Gather:
    def __init__(self, ring, x, free=False):
        self.ring, self.free = ring, free
        self.parts = [None] * ring.count
        self.parts[0] = x
        self.last = (x, x)
        self.step = 0

    def pieces(self):
        far = self.ring.half
        every = [(part, k, None) for k, part in enumerate(self.parts) if k != far]
        return every + [(self.last[0], far, 0), (self.last[1], far, 1)]

    def hop(self):
        ring = self.ring
        for _ in range(ring.reps):
            self.step += 1
            ahead, behind = self.last
            if self.step < ring.half:
                self.last = (ring.hop(ahead, 1, self.free), ring.hop(behind, -1, self.free))
                self.parts[ring.count - self.step], self.parts[self.step] = self.last
            else:
                cut = ahead.shape[0] // 2
                self.last = (
                    ring.hop(ahead[:cut], 1, self.free),
                    ring.hop(behind[cut:], -1, self.free),
                )
                self.parts[ring.half] = jnp.concatenate(self.last, axis=0)


class Scatter:
    def __init__(self, ring, part, free=False):
        self.ring, self.part, self.free = ring, part, free
        self.last = None
        self.step = 0

    def hop(self):
        ring = self.ring
        for _ in range(ring.reps):
            self.step += 1
            mark = () if self.free else ring.mark
            if self.step == 1:
                far = self.part(ring.half, *mark)
                self.cut = cut = far.shape[0] // 2
                up, down = far[:cut], far[cut:]
            else:
                ahead, behind = (x.astype(F32) for x in self.last)
                cut, at = self.cut, self.step - 1
                up = self.part(ring.half - at, *mark, self.last[0])
                down = self.part(ring.half + at, *mark, self.last[1])
                if at == 1:
                    up = jnp.concatenate([up[:cut] + ahead, up[cut:]], axis=0)
                    down = jnp.concatenate([down[:cut], down[cut:] + behind], axis=0)
                else:
                    up, down = up + ahead, down + behind
            self.last = (
                ring.hop(up.astype(BF16), 1, self.free),
                ring.hop(down.astype(BF16), -1, self.free),
            )

    def result(self):
        return self.part(0, *self.last) + (self.last[0].astype(F32) + self.last[1].astype(F32))


class TokenSum:
    def second(self, mine, others):
        got = lax.ppermute(others, "ch", SWAP)
        self.chip = (mine.astype(F32) + got.astype(F32)).astype(BF16)

    def cross(self, *others):
        self.far = lax.ppermute(after(self.chip, *others), "br", SWAP)

    def first(self, mine, others):
        self.own = mine
        self.core = lax.ppermute(others, "ch", SWAP)


class GroupSum:
    def __init__(self, part):
        self.half = part.shape[0] // 2
        core = lax.axis_index("ch")
        self.own = lax.dynamic_slice_in_dim(part, core * self.half, self.half, 0)
        theirs = lax.dynamic_slice_in_dim(part, (1 - core) * self.half, self.half, 0)
        self.got = lax.ppermute(theirs, "ch", SWAP)

    def chip(self, *others):
        got = after(self.got, *others) if others else self.got
        self.chip_sum = (self.own.astype(F32) + got.astype(F32)).astype(BF16)
        return self.chip_sum

    def cross(self, *others):
        x = after(self.chip_sum, *others) if others else self.chip_sum
        self.far = lax.ppermute(x, "br", SWAP)

    def total(self, *others):
        far = after(self.far, *others) if others else self.far
        self.mine = (self.chip_sum.astype(F32) + far.astype(F32)).astype(BF16)
        self.other = lax.ppermute(self.mine, "ch", SWAP)
        return self.mine


class TokenGather:
    def __init__(self, own):
        self.own = own
        self.far = lax.ppermute(own, "br", SWAP)
        self.core = lax.ppermute(own, "ch", SWAP)
        self.far_core = lax.ppermute(self.far, "ch", SWAP)

    def parts(self):
        return [self.own, self.core, self.far, self.far_core]


def entering(pair, reverse):
    count, index = lax.axis_size("seq"), lax.axis_index("seq")
    spread = jnp.broadcast_to(pair[None], (count,) + pair.shape)
    every = lax.all_to_all(spread, "seq", 0, 0, tiled=True)
    value = jnp.zeros(pair.shape[1:], F32)
    for k in range(count):
        at = count - 1 - k if reverse else k
        new = every[at, 1] + every[at, 0] * value
        value = jnp.where((at > index) if reverse else (at < index), new, value)
    return value


def gelu_both(x):
    square = x * x
    bent = jnp.tanh(GELU_C * (x + GELU_K * (x * square)))
    half = 0.5 * (1.0 + bent)
    slope = half + 0.5 * x * (1.0 - bent * bent) * (GELU_C * (1.0 + 3.0 * GELU_K * square))
    return x * half, slope


def minus_expm1(x, exp_x):
    series = 1.0 + x * (1.0 / 6.0)
    for k in (5.0, 4.0, 3.0, 2.0):
        series = 1.0 + x * (1.0 / k) * series
    return jnp.where(x > -0.2, -x * series, 1.0 - exp_x)


def scan_rows(keep, add, reverse):
    rows = keep.shape[0]
    at = lax.broadcasted_iota(jnp.int32, keep.shape, 0)
    step = 1
    while step < rows:
        shift = rows - step if reverse else step
        inside = (at < rows - step) if reverse else (at >= step)
        far_add = jnp.where(inside, pltpu.roll(add, shift, 0), 0.0)
        add = add + keep * far_add
        keep = keep * jnp.where(inside, pltpu.roll(keep, shift, 0), 1.0)
        step *= 2
    return keep, add


def forward_kernel(
    z_ref, rim_ref, mask_ref, conv_ref, wide_ref, bias_ref, rate_ref,
    unit_ref, gate_ref, loc_ref, prod_ref, last_ref, total_ref, ext,
):
    block = pl.program_id(0)
    rows, channels = z_ref.shape
    span = conv_ref.shape[0] - 2

    @pl.when(block == 0)
    def _():
        ext[0:8] = rim_ref[...]
        last_ref[0:1] = jnp.ones((1, channels), F32)
        last_ref[1:8] = jnp.zeros((7, channels), F32)
        total_ref[...] = jnp.zeros_like(total_ref)

    @pl.when(block > 0)
    def _():
        ext[0:8] = ext[rows : rows + 8]

    ext[8 : rows + 8] = z_ref[...].astype(F32)
    conv = jnp.broadcast_to(conv_ref[span + 1 : span + 2], (rows, channels))
    for lag in range(span + 1):
        conv = conv + conv_ref[lag : lag + 1] * ext[8 - lag : 8 - lag + rows] * mask_ref[:, lag : lag + 1]
    unit_ref[...] = conv.astype(BF16)
    pre = jnp.dot(unit_ref[...], wide_ref[...], preferred_element_type=F32) + bias_ref[...]
    gate_ref[...] = jax.nn.sigmoid(pre)
    reset = mask_ref[:, span + 1 : span + 2] > 0.5
    for lane in range(0, channels, LANES):
        own = slice(lane, lane + LANES)
        in_gate = gate_ref[:, channels + lane : channels + lane + LANES]
        log_decay = gate_ref[:, own] * rate_ref[0:1, own]
        decay = jnp.exp(log_decay)
        scale = jnp.sqrt(minus_expm1(2.0 * log_decay, decay * decay))
        total_ref[0:1, own] += jnp.sum(decay, axis=0, keepdims=True)
        keep = jnp.where(reset, 0.0, decay)
        drive = jnp.where(reset, 1.0, scale) * in_gate * unit_ref[:, own].astype(F32)
        prod, loc = scan_rows(keep, drive, False)
        loc = loc + prod * last_ref[1:2, own]
        prod = prod * last_ref[0:1, own]
        loc_ref[:, own] = loc
        prod_ref[:, own] = prod
        last_ref[0:1, own] = prod[rows - 1 :]
        last_ref[1:2, own] = loc[rows - 1 :]


def adjoint_body(
    where, weight, d_ref, z_ref, loc_ref, prod_ref, gate_ref, mask_ref, enter_ref, rate_ref,
    adj_ref, tail_ref, dzg_ref, head_ref, dmix_ref, after,
):
    step = pl.program_id(0)
    rows, channels = loc_ref.shape
    dmix_ref[...] = lax.dot_general(d_ref[...], weight[...], NT, preferred_element_type=F32)

    @pl.when(step == 0)
    def _():
        head_ref[0:1] = jnp.ones((1, channels), F32)
        head_ref[1:8] = jnp.zeros((7, channels), F32)
        after[0:2] = jnp.ones((2, channels), F32)
        after[2:8] = jnp.zeros((6, channels), F32)

    reset = mask_ref[:, 4:5] > 0.5
    for lane in range(0, channels, LANES):
        own = slice(lane, lane + LANES)
        state = loc_ref[:, own] + prod_ref[:, own] * enter_ref[0:1, own]
        act, slope = gelu_both(z_ref[:, own].astype(F32))
        dmix = dmix_ref[:, own]
        dzg_ref[:, own] = (dmix * state * slope).astype(BF16)
        keep = jnp.where(reset, 0.0, jnp.exp(gate_ref[:, own] * rate_ref[0:1, own]))
        at = lax.broadcasted_iota(jnp.int32, keep.shape, 0)
        nxt = jnp.where(at == rows - 1, after[0:1, own], pltpu.roll(keep, rows - 1, 0))
        tail, adj = scan_rows(nxt, dmix * act, True)
        adj = adj + tail * after[2:3, own]
        tail = tail * after[1:2, own]
        adj_ref[:, own] = adj
        tail_ref[:, own] = tail
        after[0:1, own] = keep[0:1]
        after[1:2, own] = tail[0:1]
        after[2:3, own] = adj[0:1]
        head_ref[0:1, own] = keep[0:1] * tail[0:1]
        head_ref[1:2, own] = keep[0:1] * adj[0:1]


def backward_kernel(
    adj_ref, tail_ref, arrive_ref, loc_ref, prod_ref, loc0_ref, prod0_ref, enter_ref, gate_ref,
    unit_ref, mask_ref, z_ref, z0_ref, rim_ref, conv_ref, wide_ref, rate_ref,
    dz_ref, gw_ref, sums_ref, edge_ref, dpre, ddir, zext, moved,
):
    step = pl.program_id(0)
    block = pl.num_programs(0) - 1 - step
    rows, channels = z_ref.shape
    span = conv_ref.shape[0] - 2

    @pl.when(step == 0)
    def _():
        gw_ref[...] = jnp.zeros_like(gw_ref)
        sums_ref[...] = jnp.zeros_like(sums_ref)
        moved[...] = jnp.zeros_like(moved)

    @pl.when(step > 0)
    def _():
        for lag in range(1, span + 1):
            moved[lag - 1, rows : rows + 8] = moved[lag - 1, 0:8]

    zext[8 : rows + 8] = z_ref[...].astype(F32)

    @pl.when(block == 0)
    def _():
        zext[0:8] = rim_ref[...]

    @pl.when(block > 0)
    def _():
        zext[0:8] = z0_ref[8:16].astype(F32)

    reset = mask_ref[:, 4:5] > 0.5
    for lane in range(0, channels, LANES):
        own = slice(lane, lane + LANES)
        two = slice(channels + lane, channels + lane + LANES)
        enter = enter_ref[0:1, own]
        adj = adj_ref[:, own] + tail_ref[:, own] * arrive_ref[0:1, own]
        state = loc_ref[:, own] + prod_ref[:, own] * enter
        before = jnp.where(block == 0, enter, loc0_ref[7:8, own] + prod0_ref[7:8, own] * enter)
        at = lax.broadcasted_iota(jnp.int32, state.shape, 0)
        previous = jnp.where(at == 0, before, pltpu.roll(state, 1, 0))
        rec_gate, in_gate = gate_ref[:, own], gate_ref[:, two]
        unit = unit_ref[:, own].astype(F32)
        rate = rate_ref[0:1, own]
        log_decay = rec_gate * rate
        decay = jnp.exp(log_decay)
        scale = jnp.sqrt(minus_expm1(2.0 * log_decay, decay * decay))
        dlog = decay * (adj * previous - adj * in_gate * unit * (decay / scale))
        dlog = jnp.where(reset, 0.0, dlog)
        sums_ref[0:1, own] += jnp.sum(dlog * rec_gate, axis=0, keepdims=True)
        scale = jnp.where(reset, 1.0, scale)
        dpre[:, own] = (dlog * rate * (rec_gate * (1.0 - rec_gate))).astype(BF16)
        through = adj * scale
        dpre[:, two] = (through * unit * (in_gate * (1.0 - in_gate))).astype(BF16)
        ddir[:, own] = through * in_gate

    gw_ref[...] += lax.dot_general(
        unit_ref[...], dpre[...], (((0,), (0,)), ((), ())), preferred_element_type=F32
    )
    dconv_all = ddir[...] + lax.dot_general(
        dpre[...], wide_ref[...], (((1,), (1,)), ((), ())), preferred_element_type=F32
    )
    ddir[...] = dconv_all
    for lane in range(0, channels, LANES):
        own = slice(lane, lane + LANES)
        two = slice(channels + lane, channels + lane + LANES)
        dconv = ddir[:, own]
        sums_ref[1:2, own] += jnp.sum(dpre[:, own].astype(F32), axis=0, keepdims=True)
        sums_ref[2:3, own] += jnp.sum(dpre[:, two].astype(F32), axis=0, keepdims=True)
        sums_ref[3:4, own] += jnp.sum(dconv, axis=0, keepdims=True)
        sums_ref[4:5, own] += jnp.sum(dconv * zext[8 : 8 + rows, own], axis=0, keepdims=True)
        dz = dconv * conv_ref[0:1, own]
        edge = jnp.zeros((8, LANES), F32)
        at8 = lax.broadcasted_iota(jnp.int32, edge.shape, 0)
        for lag in range(1, span + 1):
            kept = dconv * mask_ref[:, lag : lag + 1]
            sums_ref[4 + lag : 5 + lag, own] += jnp.sum(
                kept * zext[8 - lag : 8 - lag + rows, own], axis=0, keepdims=True
            )
            moved[lag - 1, 0:rows, own] = kept * conv_ref[lag : lag + 1, own]
            dz = dz + moved[lag - 1, lag : lag + rows, own]
            edge = edge + jnp.where(
                at8 >= 8 - lag, pltpu.roll(moved[lag - 1, 0:8, own], 8 - lag, 0), 0.0
            )
        dz_ref[:, own] = dz.astype(BF16)
        edge_ref[0:8, own] = edge

        @pl.when(step == 0)
        def _():
            edge_ref[8:16, own] = dz[rows - 8 :]


def kernel_params(mib=54):
    return pltpu.CompilerParams(dimension_semantics=("arbitrary",), vmem_limit_bytes=mib * 1024 * 1024)


def forward_local(z, rim, mask, conv, wide, bias, rate):
    tokens, channels = z.shape[0], rate.shape[1]
    rows = min(ROWS, tokens)
    spec = lambda shape, index: pl.BlockSpec(shape, index)
    whole = lambda x: pl.BlockSpec(x.shape, lambda i: (0,) * x.ndim)
    time = lambda width, at=0: pl.BlockSpec((rows, width), lambda i: (i, at))
    fixed = pl.BlockSpec((8, channels), lambda i: (0, 0))
    return pl.pallas_call(
        forward_kernel,
        grid=(tokens // rows,),
        in_specs=[time(channels, 1), whole(rim), time(mask.shape[1]), whole(conv), whole(wide), whole(bias), whole(rate)],
        out_specs=[time(channels), time(2 * channels), time(channels), time(channels), fixed, fixed],
        out_shape=[
            jax.ShapeDtypeStruct((tokens, channels), BF16),
            jax.ShapeDtypeStruct((tokens, 2 * channels), F32),
            jax.ShapeDtypeStruct((tokens, channels), F32),
            jax.ShapeDtypeStruct((tokens, channels), F32),
            jax.ShapeDtypeStruct((8, channels), F32),
            jax.ShapeDtypeStruct((8, channels), F32),
        ],
        scratch_shapes=[pltpu.VMEM((rows + 8, channels), F32)],
        compiler_params=kernel_params(),
        cost_estimate=COST,
    )(z, rim, mask, conv, wide, bias, rate)


def backward_local(adj, tail, arrive, loc, prod, enter, gate, unit, mask, z, rim, conv, wide, rate, first_rows=0):
    tokens, channels = loc.shape
    rows = first_rows or min(ROWS, tokens)
    tokens = first_rows or tokens
    last = tokens // rows - 1
    whole = lambda x: pl.BlockSpec(x.shape, lambda i: (0,) * x.ndim)
    time = lambda width, at=0: pl.BlockSpec((rows, width), lambda i: (last - i, at))
    ahead = lambda size, at=0: pl.BlockSpec(
        (size, channels), lambda i: (jnp.maximum((last - i) * (rows // size) - 1, 0), at)
    )
    fixed = lambda size, width: pl.BlockSpec((size, width), lambda i: (0, 0))
    span = conv.shape[0] - 2
    return pl.pallas_call(
        backward_kernel,
        grid=(tokens // rows,),
        in_specs=[
            time(channels), time(channels), whole(arrive), time(channels), time(channels), ahead(8), ahead(8),
            whole(enter), time(2 * channels), time(channels), time(mask.shape[1]), time(channels, 1), ahead(16, 1),
            whole(rim), whole(conv), whole(wide), whole(rate),
        ],
        out_specs=[time(channels), fixed(channels, 2 * channels), fixed(16, channels), fixed(16, channels)],
        out_shape=[
            jax.ShapeDtypeStruct((tokens, channels), BF16),
            jax.ShapeDtypeStruct((channels, 2 * channels), F32),
            jax.ShapeDtypeStruct((16, channels), F32),
            jax.ShapeDtypeStruct((16, channels), F32),
        ],
        scratch_shapes=[
            pltpu.VMEM((rows, 2 * channels), BF16),
            pltpu.VMEM((rows, channels), F32),
            pltpu.VMEM((rows + 8, channels), F32),
            pltpu.VMEM((span, rows + 8, channels), F32),
        ],
        compiler_params=kernel_params(),
        cost_estimate=COST,
    )(adj, tail, arrive, loc, prod, loc, prod, enter, gate, unit, mask, z, z, rim, conv, wide, rate)


def pad_rows(x, rows, before=False):
    extra = rows - x.shape[0]
    return jnp.pad(x, ((extra, 0) if before else (0, extra), (0, 0)))


def pieces_of(width, where, count):
    cols = width // count
    for k in range(count):
        true = pl.ds(pl.multiple_of(where[k] * cols, LANES), cols) if count > 1 else slice(0, width)
        yield slice(k * cols, (k + 1) * cols), true


def norm_one_kernel(count, where, x_ref, gain_ref, h_ref):
    width = x_ref.shape[1]
    x = x_ref[...]
    rstd = lax.rsqrt(jnp.sum(x * x, axis=1, keepdims=True) * (1.0 / width) + NORM_EPS)
    for own, true in pieces_of(width, where, count):
        h_ref[:, own] = (x_ref[:, true] * rstd * gain_ref[:, own]).astype(BF16)


def first_norm_kernel(count, row, where, x_ref, *refs):
    parts, h_ref, gain_ref = refs[:count], refs[count], refs[count + 1]
    width = x_ref.shape[1]
    cols = width // count
    x = x_ref[...]
    rstd = lax.rsqrt(jnp.sum(x * x, axis=1, keepdims=True) * (1.0 / width) + NORM_EPS)
    for part, (own, true) in zip(parts, pieces_of(width, where, count)):
        gain = part[row : row + 1, 0:cols].astype(F32)
        h_ref[:, own] = (x_ref[:, true] * rstd * gain).astype(BF16)
        gain_ref[0:1, own] = gain
        gain_ref[1:2, own] = part[row : row + 1, cols : 2 * cols].astype(F32)


def first_norm_call(count, where, x, parts, part_rows, row):
    tokens, width = x.shape
    rows = min(ROWS, tokens)
    time = pl.BlockSpec((rows, width), lambda i, w: (i, 0))
    fixed = lambda shape: pl.BlockSpec(shape, lambda i, w: (0, 0))
    return pl.pallas_call(
        functools.partial(first_norm_kernel, count, row),
        grid_spec=pltpu.PrefetchScalarGridSpec(
            num_scalar_prefetch=1,
            grid=(tokens // rows,),
            in_specs=[time] + [fixed((part_rows, p.shape[1])) for p in parts],
            out_specs=[time, fixed((8, width))],
        ),
        out_shape=[jax.ShapeDtypeStruct((tokens, width), BF16), jax.ShapeDtypeStruct((8, width), F32)],
        compiler_params=kernel_params(),
        cost_estimate=COST,
    )(where, x, *parts)


def prepare_kernel(count, gates, part_ch, taps, cols, *refs):
    parts, (row_ref, head_ref, code_ref, col_ref, hot_ref, wide_ref, chan_ref, small) = refs[:count], refs[count:]
    channels = wide_ref.shape[0]
    stacked = jnp.concatenate([p[0:gates].astype(F32) for p in parts], axis=0).astype(BF16)
    inside = head_ref[...] == col_ref[0:1]
    for g in range(2):
        hot = (row_ref[...] == code_ref[g : g + 1]).astype(F32).astype(BF16)
        placed = jnp.dot(hot, stacked, preferred_element_type=F32)
        wide_ref[:, g * channels : (g + 1) * channels] = jnp.where(inside, placed, 0.0).astype(BF16)
    for k, part in enumerate(parts):
        small[k : k + 1] = part[gates : gates + 1].astype(F32)
        small[count + k : count + k + 1] = part[gates + 1 : gates + 2].astype(F32)
    ordered = [
        jnp.dot(hot_ref[...], small[s * count : (s + 1) * count].astype(BF16), preferred_element_type=F32).astype(BF16)
        for s in range(2)
    ]
    lane = lax.broadcasted_iota(jnp.int32, (channels, channels), 0)
    seq = lax.broadcasted_iota(jnp.int32, (count, channels), 0)
    wanted = [(1, y * part_ch) for y in range(taps + 3)] + [(0, 2 * cols)]
    for y, (s, offset) in enumerate(wanted):
        hot = (lane == col_ref[1:2] + offset).astype(F32).astype(BF16)
        spread = jnp.dot(ordered[s], hot, preferred_element_type=F32)
        chan_ref[y : y + 1] = jnp.sum(jnp.where(seq == col_ref[2:3], spread, 0.0), axis=0, keepdims=True)


def prepare_call(parts, true_all, place_hot, part_rows, part_in, block, part_ch, taps, cols):
    count = len(parts)
    channels = parts[0].shape[1]
    gates = 2 * part_in
    at = np.arange(channels)
    row_code = jnp.asarray((at % block // part_in * part_in + at % part_in)[:, None], jnp.int32)
    row_head = jnp.asarray((at // block)[:, None], jnp.int32)
    col = jnp.asarray(np.stack([at // block, at % part_ch, at // part_ch]), jnp.int32)
    code = true_all[:, None] * part_in + jnp.arange(part_in, dtype=jnp.int32)[None, :]
    none = jnp.full_like(code, -1)
    code = jnp.stack(
        [
            jnp.concatenate([code, none], axis=1).reshape(-1),
            jnp.concatenate([none, code], axis=1).reshape(-1),
        ]
    )
    whole = lambda x: pl.BlockSpec(x.shape, lambda i: (0, 0))
    args = (row_code, row_head, code, col, place_hot)
    return pl.pallas_call(
        functools.partial(prepare_kernel, count, gates, part_ch, taps, cols),
        grid=(1,),
        in_specs=[pl.BlockSpec((part_rows, channels), lambda i: (0, 0)) for _ in parts] + [whole(a) for a in args],
        out_specs=[
            pl.BlockSpec((channels, 2 * channels), lambda i: (0, 0)),
            pl.BlockSpec((taps + 4, channels), lambda i: (0, 0)),
        ],
        out_shape=[
            jax.ShapeDtypeStruct((channels, 2 * channels), BF16),
            jax.ShapeDtypeStruct((taps + 4, channels), F32),
        ],
        scratch_shapes=[pltpu.VMEM((2 * count, channels), F32)],
        compiler_params=kernel_params(),
        cost_estimate=COST,
    )(*parts, *args)


def low_kernel(count, where, x_ref, low_ref, true_ref):
    true_ref[...] = x_ref[...].astype(BF16)
    for own, true in pieces_of(x_ref.shape[1], where, count):
        low_ref[:, own] = true_ref[:, true]


def summed(refs, own):
    return sum(ref[:, own].astype(F32) for ref in refs[1:]) + refs[0][:, own].astype(F32)


def norm_two_kernel(count, where, x_ref, a_ref, b_ref, c_ref, gain_ref, resid_ref, h_ref):
    width = x_ref.shape[1]
    square = 0.0
    for own, true in pieces_of(width, where, count):
        resid = x_ref[:, true] + summed((a_ref, b_ref, c_ref), own)
        resid_ref[:, own] = resid
        square = square + jnp.sum(resid * resid, axis=1, keepdims=True)
    rstd = lax.rsqrt(square * (1.0 / width) + NORM_EPS)
    h_ref[...] = (resid_ref[...] * rstd * gain_ref[...]).astype(BF16)


def norm_two_back_kernel(count, where, cot_ref, a_ref, b_ref, c_ref, gain_ref, resid_ref, d_resid_ref, low_ref):
    width = cot_ref.shape[1]
    resid = resid_ref[...]
    rstd = lax.rsqrt(jnp.sum(resid * resid, axis=1, keepdims=True) * (1.0 / width) + NORM_EPS)
    along = 0.0
    for own, _ in pieces_of(width, where, count):
        d_normed = summed((a_ref, b_ref, c_ref), own) * gain_ref[:, own]
        d_resid_ref[:, own] = d_normed
        along = along + jnp.sum(d_normed * resid_ref[:, own], axis=1, keepdims=True)
    along = along * rstd * (1.0 / width)
    for own, true in pieces_of(width, where, count):
        d_resid = cot_ref[:, true] + rstd * (d_resid_ref[:, own] - resid_ref[:, own] * rstd * along)
        d_resid_ref[:, own] = d_resid
        low_ref[:, own] = d_resid.astype(BF16)


def pick(where, mine_ref, other_ref, own, per):
    is_mine = (pl.program_id(0) // per) == where[where.shape[0] - 1]
    return jnp.where(is_mine, mine_ref[:, own], other_ref[:, own]).astype(F32)


def norm_one_whole_kernel(count, per, where, x_ref, mine_ref, other_ref, gain_ref, d_resid_ref, out_ref, kept):
    width = x_ref.shape[1]
    is_mine = (pl.program_id(0) // per) == where[where.shape[0] - 1]

    @pl.when(is_mine)
    def _():
        kept[...] = mine_ref[...].astype(F32) * gain_ref[...]

    @pl.when(jnp.logical_not(is_mine))
    def _():
        kept[...] = other_ref[...].astype(F32) * gain_ref[...]

    x = x_ref[...]
    rstd = lax.rsqrt(jnp.sum(x * x, axis=1, keepdims=True) * (1.0 / width) + NORM_EPS)
    along = 0.0
    for own, true in pieces_of(width, where, count):
        along = along + jnp.sum(kept[:, own] * x_ref[:, true], axis=1, keepdims=True)
    along = along * rstd * (1.0 / width)
    for own, true in pieces_of(width, where, count):
        out_ref[:, true] = d_resid_ref[:, own].astype(F32) + rstd * (kept[:, own] - x_ref[:, true] * rstd * along)


def norm_call(kernel, count, where, x, gain, outputs=1, slots=False):
    tokens, width = x.shape
    rows = min(ROWS, tokens // 4)
    per = tokens // 4 // rows
    time = pl.BlockSpec((rows, width), lambda i, w: (i, 0))
    moved = pl.BlockSpec((rows, width), lambda i, w: (w[count + i // per] * per + i % per, 0))
    args = (x,) if gain is None else (x, gain)
    return pl.pallas_call(
        functools.partial(kernel, count),
        grid_spec=pltpu.PrefetchScalarGridSpec(
            num_scalar_prefetch=1,
            grid=(tokens // rows,),
            in_specs=[moved if slots else time] + [pl.BlockSpec(a.shape, lambda i, w: (0, 0)) for a in args[1:]],
            out_specs=[time] * outputs,
        ),
        out_shape=[jax.ShapeDtypeStruct((tokens, width), BF16)] * outputs,
        compiler_params=kernel_params(),
        cost_estimate=COST,
    )(where, *args)


def own_call(kernel, count, where, x, total, gain, extra, out_types, scratch=False):
    tokens, width = x.shape
    rows = min(64, tokens // 4)
    per = tokens // 4 // rows
    time = pl.BlockSpec((rows, width), lambda i, w: (i, 0))
    true = pl.BlockSpec((rows, width), lambda i, w: (w[count] * per + i, 0))
    args = (x, total.own, total.core, total.far, gain) + extra
    return pl.pallas_call(
        functools.partial(kernel, count),
        grid_spec=pltpu.PrefetchScalarGridSpec(
            num_scalar_prefetch=1,
            grid=(per,),
            in_specs=[true, time, time, time, pl.BlockSpec(gain.shape, lambda i, w: (0, 0))] + [time] * len(extra),
            out_specs=[time] * len(out_types),
            scratch_shapes=[pltpu.VMEM((rows, width), F32)] if scratch else [],
        ),
        out_shape=[jax.ShapeDtypeStruct((tokens // 4, width), t) for t in out_types],
        compiler_params=kernel_params(),
        cost_estimate=COST,
    )(where, *args)


def sum_call(kernel, count, where, summed, x, gain, extra, out_types):
    tokens, width = x.shape
    rows = min(ROWS, tokens // 4)
    per = tokens // 2 // rows
    last = where.shape[0] - 1
    time = pl.BlockSpec((rows, width), lambda i, w: (i, 0))
    each = tokens // 4 // rows
    slot = pl.BlockSpec((rows, width), lambda i, w: (w[count + 4 + i // each] * each + i % each, 0))
    mine = pl.BlockSpec((rows, width), lambda i, w: (jnp.clip(i - w[last] * per, 0, per - 1), 0))
    other = pl.BlockSpec((rows, width), lambda i, w: (jnp.clip(i - (1 - w[last]) * per, 0, per - 1), 0))
    args = (x, summed.mine, summed.other, gain) + extra
    gain_spec = pl.BlockSpec(gain.shape, lambda i, w: (0, 0))
    return pl.pallas_call(
        functools.partial(kernel, count, per),
        grid_spec=pltpu.PrefetchScalarGridSpec(
            num_scalar_prefetch=1,
            grid=(tokens // rows,),
            in_specs=[time, mine, other, gain_spec] + [slot] * len(extra),
            out_specs=[time] * len(out_types),
            scratch_shapes=[pltpu.VMEM((rows, width), F32)],
        ),
        out_shape=[jax.ShapeDtypeStruct((tokens, width), t) for t in out_types],
        compiler_params=kernel_params(),
        cost_estimate=COST,
    )(where, *args)


def weight_call(
    body, pieces, target, rows, inputs, fixed, outputs, scalars, scratch=(), steps=None, spots=None, earlier=()
):
    tokens = inputs[0].shape[0]
    steps = tokens // rows if steps is None else steps
    same = lambda i, s: i
    read, write = spots if spots else (None, same)
    read = read or [same] * len(inputs)
    count = len(pieces)

    def kernel(scalar_ref, *refs):
        shard_refs, refs = refs[:count], refs[count:]
        weight, sem = refs[-2:]

        @pl.when(pl.program_id(0) == 0)
        def _():
            copies = []
            for n, (ref, (_, place)) in enumerate(zip(shard_refs, pieces)):
                for m, (source, to) in enumerate(place(scalar_ref)):
                    copies.append(pltpu.make_async_copy(ref.at[source], weight.at[to], sem.at[n, m]))
            for copy in copies:
                copy.start()
            for copy in copies:
                copy.wait()

        skip = len(inputs) + len(fixed)
        body(scalar_ref, weight, *refs[:skip], *refs[skip + len(earlier) : -2])

    whole = lambda x: pl.BlockSpec(x.shape, lambda i, s: (0,) * x.ndim)
    in_specs = [pl.BlockSpec(memory_space=pl.ANY)] * count
    for x, at in zip(inputs, read):
        in_specs.append(pl.BlockSpec((rows, x.shape[1]), lambda i, s, at=at: (at(i, s), 0)))
    in_specs += [whole(x) for x in fixed] + [pl.BlockSpec(memory_space=pl.ANY)] * len(earlier)
    out_specs, out_shape = [], []
    for o in outputs:
        if len(o) == 2:
            out_specs.append(pl.BlockSpec((rows, o[0]), lambda i, s: (write(i, s), 0)))
            out_shape.append(jax.ShapeDtypeStruct((tokens, o[0]), o[1]))
        else:
            out_specs.append(pl.BlockSpec(o[:2], lambda i, s: (0, 0)))
            out_shape.append(jax.ShapeDtypeStruct(o[:2], o[2]))
    first = 1 + count + len(inputs) + len(fixed)
    return pl.pallas_call(
        kernel,
        grid_spec=pltpu.PrefetchScalarGridSpec(
            num_scalar_prefetch=1,
            grid=(steps,),
            in_specs=in_specs,
            out_specs=out_specs,
            scratch_shapes=list(scratch) + [pltpu.VMEM(target, BF16), pltpu.SemaphoreType.DMA((count, 16))],
        ),
        out_shape=out_shape,
        input_output_aliases={first + i: i for i in range(len(earlier))},
        compiler_params=kernel_params(60 if count > 12 else 48),
        cost_estimate=COST,
    )(scalars, *[array for array, _ in pieces], *inputs, *fixed, *earlier)


def row_pieces(ring_gather, cols, lane, skip=0):
    out = []
    for array, k, half in ring_gather.pieces():
        first = array.shape[0] if half == 1 else 0
        begin = max(skip - first, 0)
        size = array.shape[0] - begin
        if size > 0:
            place = lambda s, begin=begin, start=k * cols + first + begin - skip, size=size: [
                ((pl.ds(begin, size),), (pl.ds(start, size), lane(s)))
            ]
            out.append((array, place))
    return out


def col_pieces(ring_gather, cols):
    if cols % LANES:
        return [(jnp.concatenate(ring_gather.parts, axis=1), lambda s: [((slice(None),), (slice(None),))])]
    out = []
    for array, k, half in ring_gather.pieces():
        size = array.shape[0]
        start = size if half == 1 else 0
        out.append(
            (
                array,
                lambda s, start=start, size=size, k=k: [
                    ((slice(None),), (pl.ds(start, size), pl.ds(k * cols, cols)))
                ],
            )
        )
    return out


NT = (((1,), (1,)), ((), ()))


def product_body(where, weight, x_ref, out_ref):
    out_ref[...] = jnp.dot(x_ref[...], weight[...], preferred_element_type=F32).astype(BF16)


def to_quarter(slot, refs, value):
    for s, ref in enumerate(refs):

        @pl.when(slot == s)
        def _():
            ref[...] = value.astype(BF16)


def product_nt_body(where, weight, x_ref, *out_refs):
    part = lax.dot_general(x_ref[...], weight[...], NT, preferred_element_type=F32)
    to_quarter(pl.program_id(0), out_refs, part)


def output_body(count, where, weight, hidden_ref, *refs):
    attn_refs, out_ref, part = refs[:4], refs[4], refs[5]
    part[...] = jnp.dot(hidden_ref[...], weight[...], preferred_element_type=F32)
    width = part.shape[1]
    for slot, ref in enumerate(attn_refs):

        @pl.when(pl.program_id(0) == slot)
        def _():
            part[...] += ref[...].astype(F32)

    cols = width // count
    for k in range(count):
        own = slice(k * cols, (k + 1) * cols)
        to = pl.ds(pl.multiple_of(where[count + 8 + k] * cols, LANES), cols) if count > 1 else own
        out_ref[:, to] = part[:, own].astype(BF16)


def mixed_body(count, where, weight, z_ref, loc_ref, prod_ref, enter_ref, mixed_ref, *out_refs):
    channels = loc_ref.shape[1]
    act, _ = gelu_both(z_ref[:, :channels].astype(F32))
    mixed_ref[...] = (act * (loc_ref[...] + prod_ref[...] * enter_ref[...])).astype(BF16)
    part = jnp.dot(mixed_ref[...], weight[...], preferred_element_type=F32)
    to_quarter(where[count + 4 + pl.program_id(0)], out_refs, part)


def gate_up_body(where, weight, h_ref, hidden_ref, act_ref, slope_ref, both):
    units = hidden_ref.shape[1]
    both[...] = jnp.dot(h_ref[...], weight[...], preferred_element_type=F32)
    for lane in range(0, units, LANES):
        own = slice(lane, lane + LANES)
        act, slope = gelu_both(both[:, own])
        up = both[:, units + lane : units + lane + LANES]
        hidden_ref[:, own] = (act * up).astype(BF16)
        act_ref[:, own] = act.astype(BF16)
        slope_ref[:, own] = (slope * up).astype(BF16)


def d_hidden_body(where, weight, d_ref, act_ref, slope_ref, out_ref):
    units = act_ref.shape[1]
    d_hidden = lax.dot_general(d_ref[...], weight[...], NT, preferred_element_type=F32)
    out_ref[:, :units] = (d_hidden * slope_ref[...].astype(F32)).astype(BF16)
    out_ref[:, units:] = (d_hidden * act_ref[...].astype(F32)).astype(BF16)


def d_h_one_body(where, weight, dzg_ref, dzr_ref, out_ref):
    channels = dzg_ref.shape[1]
    gate = lax.dot_general(dzg_ref[...], weight[:, :channels], NT, preferred_element_type=F32)
    rec = lax.dot_general(dzr_ref[...], weight[:, channels:], NT, preferred_element_type=F32)
    out_ref[...] = (gate + rec).astype(BF16)


def per_device(
    inputs,
    lengths,
    norm_gain1,
    in_weight,
    conv_weight,
    conv_bias,
    gate_weight,
    gate_bias,
    decay_param,
    out_weight,
    norm_gain2,
    mlp_in,
    mlp_down,
    cotangent,
):
    tokens, width = inputs.shape
    count, index = lax.axis_size("seq"), lax.axis_index("seq")
    br, ch = lax.axis_index("br"), lax.axis_index("ch")
    place = ring_place(index, count)
    cols = width // count
    taps = conv_weight.shape[0]
    span = taps - 1
    part_ch = conv_weight.shape[3]
    channels = part_ch * count
    hidden_units = mlp_down.shape[0]
    heads, part_in, block = gate_weight.shape[3], gate_weight.shape[4], gate_weight.shape[5]
    ahead = (place + jnp.arange(count, dtype=jnp.int32)) % count
    true_all = jnp.where(ahead < count // 2, 2 * ahead, 2 * (count - 1 - ahead) + 1)
    ring_index = (ring_place(jnp.arange(count, dtype=jnp.int32), count) - place) % count
    true_of = [true_all[k] for k in range(count)]
    ring_of = [ring_index[k] for k in range(count)]
    aligned = cols % LANES == 0

    def move(x, at):
        return jnp.concatenate(
            [lax.dynamic_slice_in_dim(x, a * cols, cols, 1) for a in at], axis=1
        )

    quarter = tokens // 4
    me = ch * 2 + br
    quarters = me ^ jnp.asarray([0, 2, 1, 3], jnp.int32)
    slots = me ^ jnp.arange(4, dtype=jnp.int32)
    slots = (slots % 2) * 2 + slots // 2
    per_device_cols = count // 4
    to = true_all // per_device_cols
    dealt = (((to % 2) ^ ch) * 2 + ((to // 2) ^ br)) * per_device_cols + true_all % per_device_cols
    whole_inputs = inputs
    if aligned:
        n_pieces = count
        where = jnp.concatenate([true_all, quarters, slots, dealt, br[None], ch[None]]).astype(jnp.int32)
    else:
        n_pieces = 1
        zero = jnp.zeros((1,), jnp.int32)
        where = jnp.concatenate([zero, quarters, slots, zero, br[None], ch[None]]).astype(jnp.int32)
        inputs, cotangent = move(inputs, true_of), move(cotangent, true_of)

    ring = Ring(count)

    fold = 2 * block
    gate_rows = heads * part_in
    packed_gates = 2 * part_in

    def one_row(*arrays):
        row = jnp.concatenate([a.reshape(-1) for a in arrays])
        return jnp.pad(row, (0, channels - row.shape[0]))[None]

    packed = jnp.concatenate(
        [
            gate_weight[:, 0, 0].transpose(0, 2, 1, 3).reshape(packed_gates, channels),
            one_row(norm_gain1, norm_gain2, decay_param),
            one_row(conv_weight, conv_bias, gate_bias),
        ],
        axis=0,
    )
    packed_rows = -(-(cols + packed.shape[0]) // 32) * 32 - cols
    packed = pad_rows(packed, packed_rows)

    own_cols = lax.dynamic_slice_in_dim(in_weight[0], br * channels, channels, 1)
    far_cols = lax.ppermute(
        lax.dynamic_slice_in_dim(in_weight[0], (1 - br) * channels, channels, 1), "br", SWAP
    )
    own_and_packed = jnp.concatenate([packed, own_cols], axis=0)
    in_own, in_far = Gather(ring, own_and_packed), Gather(ring, far_cols)
    out_ring = Gather(ring, out_weight[0, 0])
    down_ring = Gather(ring, mlp_down)
    in_own.hop()
    in_far.hop()
    own_first, far_first = in_own.last, in_far.last
    in_own.hop()
    in_far.hop()
    own_second, far_second = in_own.last, in_far.last
    for _ in range(2):
        in_own.hop()
        in_far.hop()
    mlp_all = lax.all_gather(after(mlp_in, *in_own.last, *in_far.last), "seq", axis=1, tiled=True)
    out_ring.hop()

    doc_starts = jnp.cumsum(lengths) - lengths
    positions = jnp.arange(tokens + span, dtype=jnp.int32) + index * tokens - span
    doc_ext = jnp.sum((positions[:, None] >= doc_starts[None, 1:]).astype(jnp.int32), axis=1)
    lags = [
        (doc_ext[span - lag : span - lag + tokens] == doc_ext[span:]).astype(F32) for lag in range(taps)
    ]
    reset = jnp.any(positions[span:, None] == doc_starts[None, :], axis=1).astype(F32)
    mask = jnp.stack(lags + [reset], axis=1)

    place_hot = (ring_index[:, None] == jnp.arange(count)[None, :]).astype(BF16)
    row = jnp.arange(channels)
    row_head, row_in = row // block, row % block
    row_seq = row_in // part_in
    row_place = (jnp.where(row_seq % 2 == 0, row_seq // 2, count - 1 - row_seq // 2) - place) % count
    source = row_place * gate_rows + row_head * part_in + row_in % part_in
    row_hot = (source[:, None] == jnp.arange(channels)[None, :]).astype(BF16)
    wide_col = jnp.arange(2 * channels)
    wide_gate, wide_head, wide_out = (
        wide_col // channels,
        (wide_col % channels) // block,
        wide_col % block,
    )
    spread_hot = (jnp.arange(fold)[:, None] == (wide_gate * block + wide_out)[None, :]).astype(BF16)
    on_block = (row_head[:, None] == wide_head[None, :]).astype(BF16)
    scalars = where
    last_at = where.shape[0] - 2
    firsts = [in_own.last[0] if k == count // 2 else in_own.parts[k] for k in range(count)]
    if aligned:
        h_one, gains = first_norm_call(n_pieces, where, inputs, firsts, packed_rows, packed_gates)
        gain_one, gain_two = gains[0:1], gains[1:2]
    else:
        rows = jnp.stack([part[packed_gates] for part in firsts]).astype(F32)
        gain_one, gain_two = rows[:, :cols].reshape(1, width), rows[:, cols : 2 * cols].reshape(1, width)
        (h_one,) = norm_call(norm_one_kernel, n_pieces, where, inputs, gain_one)
    in_pieces = row_pieces(
        in_own, cols, lambda s: pl.ds(pl.multiple_of(s[last_at] * channels, LANES), channels), packed_rows
    )
    in_pieces += row_pieces(
        in_far, cols, lambda s: pl.ds(pl.multiple_of((1 - s[last_at]) * channels, LANES), channels)
    )
    in_shape = (width, 2 * channels)
    (z_last,) = weight_call(
        product_body, in_pieces, in_shape, 16, (h_one[tokens - 16 :],), (), [(2 * channels, BF16)], scalars
    )
    if aligned:
        wide, chan = prepare_call(
            [after(firsts[0], z_last)] + firsts[1:], true_all, place_hot, packed_rows, part_in, block, part_ch, taps, cols
        )
    else:
        rows = jnp.stack([part[packed_gates : packed_gates + 2] for part in firsts])
        chan = jnp.concatenate([rows[:, 1, : (taps + 3) * part_ch], rows[:, 0, 2 * cols : 2 * cols + part_ch]], axis=1)
        chan = jnp.dot(place_hot, chan, preferred_element_type=F32).reshape(count, taps + 4, part_ch)
        chan = chan.transpose(1, 0, 2).reshape(taps + 4, channels)
        every = jnp.stack([part[:packed_gates].reshape(-1) for part in firsts])
        every = jnp.dot(place_hot, every, preferred_element_type=F32).astype(BF16)
        every = every.reshape(count, 2, part_in, heads, block).transpose(3, 0, 2, 1, 4)
        wide = every[:, :, :, :, None, :] * jnp.eye(heads, dtype=BF16)[:, None, None, None, :, None]
        wide = wide.reshape(channels, 2 * channels)
    conv = chan[: taps + 1]
    gate_bias_all = chan[taps + 1 : taps + 3].reshape(1, 2 * channels)
    decay_rate = chan[taps + 3 : taps + 4]
    rate = -DECAY_SCALE * jax.nn.softplus(-decay_rate)
    forward_pairs = [(i, i + 1) for i in range(count - 1)]
    rim = lax.ppermute(z_last[8:, channels:], "seq", forward_pairs).astype(F32)
    (z,) = weight_call(
        product_body, in_pieces, in_shape, quarter, (after(h_one, z_last),), (), [(2 * channels, BF16)], scalars
    )
    ring.mark = (z, rim, wide)
    out_first = out_ring.last
    out_ring.hop()

    unit, gates, loc, prod, last, total = forward_local(
        after(z, *out_first), rim, mask, conv, wide, gate_bias_all, rate
    )
    ring.mark = (last,)
    out_second = out_ring.last
    out_ring.hop()
    enter = entering(after(last[:2], *out_second), False)[None]
    ring.mark = (enter,)
    out_third = out_ring.last
    out_ring.hop()
    down_ring.hop()

    to_slot = lambda i, s: s[n_pieces + 4 + i]
    from_slot = lambda i, s: s[n_pieces + i]
    out_pieces = col_pieces(out_ring, cols)
    out_shape = (channels, width)
    one_quarter = (quarter, width, BF16)
    mixed, *attn_parts = weight_call(
        functools.partial(mixed_body, n_pieces), out_pieces, out_shape, quarter, (z, loc, prod),
        (after(enter, *out_third),), [(channels, BF16)] + [one_quarter] * 4, scalars, spots=(None, to_slot),
    )
    attn = TokenSum()
    attn.second(*attn_parts[2:])
    attn.cross()
    attn.first(*attn_parts[:2])
    down_first = down_ring.last
    ring.mark = (attn.chip,)
    down_ring.hop()
    d_mlp, slot_cot = norm_call(low_kernel, n_pieces, where, after(cotangent, attn.chip), None, 2, slots=True)
    if not aligned:
        slot_cot = move(slot_cot, ring_of)

    resid, h_own = own_call(
        norm_two_kernel, n_pieces, where, inputs, attn, after(gain_two, d_mlp, *down_first), (), (F32, BF16)
    )
    h_two = TokenGather(h_own)
    down_second = down_ring.last
    ring.mark = (h_own,)
    down_ring.hop()
    h_two = after(jnp.concatenate(h_two.parts(), axis=0), *down_second)
    down_third = down_ring.last
    ring.mark = (h_two,)
    down_ring.hop()


    def mlp_place(s):
        out = []
        for k in range(count):
            rows = pl.ds(pl.multiple_of(s[k] * cols, 8), cols)
            for g in range(2):
                out.append(
                    ((g, rows), (pl.ds(k * cols, cols), pl.ds(g * hidden_units, hidden_units)))
                )
        return out

    if aligned:
        mlp_pieces = [(mlp_all, mlp_place)]
    else:
        moved = [lax.dynamic_slice_in_dim(mlp_all, a * cols, cols, 1) for a in true_of]
        mlp_pieces = [
            (
                jnp.concatenate(moved, axis=1),
                lambda s: [
                    ((g,), (slice(None), pl.ds(g * hidden_units, hidden_units))) for g in range(2)
                ],
            )
        ]
    mlp_shape = (width, 2 * hidden_units)
    hidden, act, slope = weight_call(
        gate_up_body, mlp_pieces, mlp_shape, quarter, (after(h_two, *down_third),), (),
        [(hidden_units, BF16)] * 3, scalars, scratch=(pltpu.VMEM((quarter, 2 * hidden_units), F32),),
    )

    def chunk(x, k):
        return x[:, k * cols : (k + 1) * cols]

    def outer(left, right):
        return lax.dot_general(left, right, (((0,), (0,)), ((), ())), preferred_element_type=F32)

    down_pieces = col_pieces(down_ring, cols)
    down_shape = (hidden_units, width)
    (d_gate_up,) = weight_call(
        d_hidden_body, down_pieces, down_shape, quarter, (after(d_mlp, hidden), act, slope), (),
        [(2 * hidden_units, BF16)], scalars,
    )
    ring.mark = (d_gate_up,)
    g_mlp = Scatter(ring, lambda k, *t: outer(chunk(h_two, k), after(d_gate_up, *t)))
    g_mlp.hop()
    mlp_hop = [g_mlp.last]
    upper, lower = lambda i, s: i + 2, lambda i, s: i
    part = weight_call(
        product_nt_body, mlp_pieces, mlp_shape, quarter, (d_gate_up,), (), [one_quarter] * 2, scalars,
        steps=2, spots=([upper], upper),
    )
    d_h_two = TokenSum()
    d_h_two.second(*part)
    d_h_two.cross()
    part = weight_call(
        product_nt_body, mlp_pieces, mlp_shape, quarter, (after(d_gate_up, d_h_two.chip),), (), [one_quarter] * 2,
        scalars, steps=2, spots=([lower], lower),
    )
    d_h_two.first(*part)
    ring.mark = (part[0],)
    g_mlp.hop()
    mlp_hop.append(g_mlp.last)
    d_resid, d_attn = own_call(
        norm_two_back_kernel, n_pieces, where, cotangent, d_h_two, gain_two, (resid,), (F32, BF16)
    )
    d_attn = TokenGather(d_attn)

    (o_part,) = weight_call(
        functools.partial(output_body, n_pieces), down_pieces, down_shape, quarter,
        (after(hidden, d_attn.own),), tuple(attn_parts), [(width, BF16)], scalars, spots=(None, from_slot),
        scratch=(pltpu.VMEM((quarter, width), F32),),
    )
    if not aligned:
        at = jnp.arange(count)
        o_part = move(o_part, [jnp.sum(jnp.where(dealt == k, at, 0)) for k in range(count)])
    o_cols = width // 4
    ring.mark = (d_attn.own,)
    mlp_first = mlp_hop[1]
    g_mlp.hop()
    mlp_hop.append(g_mlp.last)
    d_attn = jnp.concatenate(d_attn.parts(), axis=0)
    rows = min(ROWS, quarter)
    per = quarter // rows
    last_step = tokens // rows - 1
    back = lambda i, s: last_step - i
    back_slot = lambda i, s: s[n_pieces + 4 + (last_step - i) // per] * per + (last_step - i) % per
    adj, tail, d_z_gate, head = weight_call(
        adjoint_body, out_pieces, out_shape, rows, (d_attn, z, loc, prod, gates, mask), (enter, rate),
        [(channels, F32), (channels, F32), (channels, BF16), (8, channels, F32)], scalars,
        scratch=(pltpu.VMEM((rows, channels), F32), pltpu.VMEM((8, channels), F32)),
        spots=([back_slot] + [back] * 5, back),
    )
    swapped = lax.ppermute(after(o_part[:, 2 * o_cols :], head), "ch", SWAP).astype(F32)
    g_down_part = outer(after(hidden, head), slot_cot).astype(BF16)
    o_far = (o_part[:, o_cols : 2 * o_cols].astype(F32) + after(swapped, g_down_part)[:, o_cols:]).astype(BF16)
    ring.mark = (head,)
    g_out = Scatter(ring, lambda k, *t: outer(after(mixed, *t), chunk(d_attn, k)))
    g_out.hop()
    out_hop = [g_out.last]
    arrive = entering(after(head[:2], *mlp_hop[2], g_down_part, o_far), True)[None]
    g_down = lax.psum_scatter(after(g_down_part, arrive), "seq", scatter_dimension=1, tiled=True)
    o_far = lax.ppermute(after(o_far, arrive), "br", SWAP)
    o_inputs = lax.dynamic_slice_in_dim(whole_inputs, (br * 2 + ch) * o_cols, o_cols, 1)
    output = o_inputs + o_part[:, :o_cols].astype(F32) + swapped[:, :o_cols] + o_far.astype(F32)
    back_args = (loc, prod, enter, gates, unit, mask, z, rim, conv, wide, rate)
    edge = backward_local(adj, tail, arrive, *back_args, first_rows=16)[3]
    backward_pairs = [(i + 1, i) for i in range(count - 1)]
    from_next = lax.ppermute(edge[:8], "seq", backward_pairs)
    ring.mark = (from_next,)
    g_mlp.hop()
    mlp_hop.append(g_mlp.last)
    d_z_rec, g_wide, sums, edge = backward_local(
        adj, tail, after(arrive, from_next, *out_hop[0]), *back_args
    )
    edge = after(edge, o_far)
    ring.mark = (edge,)
    g_out.hop()
    out_hop.append(g_out.last)
    fixed = (edge[8:] + from_next).astype(BF16)
    d_z_rec = d_z_rec.at[tokens - 8 :].set(fixed)

    d_z = jnp.concatenate([d_z_gate, d_z_rec], axis=1)
    g_in_ring = Scatter(ring, lambda k, *t: outer(chunk(h_one, k), after(d_z, *t)))
    ring.mark = (d_z,)
    g_in_ring.hop()
    (d_h_part,) = weight_call(
        d_h_one_body, in_pieces, in_shape, quarter, (d_z_gate, d_z_rec), (), [(width, BF16)], scalars
    )
    d_h_one = GroupSum(d_h_part)
    ring.mark = (d_h_part,)
    in_hop = [g_in_ring.last]
    g_in_ring.hop()
    d_h_one.chip(*in_hop[0])
    d_h_one.cross()
    ring.mark = (d_h_one.chip_sum,)
    g_out.hop()

    g_compact = lax.dot_general(
        (after(g_wide, d_h_one.chip_sum) * on_block.astype(F32)).astype(BF16),
        spread_hot,
        (((1,), (1,)), ((), ())),
        preferred_element_type=F32,
    ).astype(BF16)
    g_gates = lax.dot_general(row_hot, g_compact, (((0,), (0,)), ((), ())), preferred_element_type=F32)
    g_decay = sums[0:1] * -DECAY_SCALE * -jax.nn.sigmoid(-decay_rate)
    g_chan = jnp.concatenate([sums[4 : 4 + taps], sums[3:4], sums[1:3], g_decay, total[0:1]], axis=0)
    g_chan = g_chan.reshape(taps + 5, count, part_ch).transpose(1, 0, 2).reshape(count, -1)
    g_small = lax.dot_general(
        place_hot.astype(F32), g_chan, (((0,), (0,)), ((), ())), precision=lax.Precision.HIGHEST
    )
    g_rows = -(-g_small.shape[1] // fold)
    g_small = jnp.pad(g_small, ((0, 0), (0, g_rows * fold - g_small.shape[1]))).reshape(count, g_rows, fold)
    g_packed = jnp.concatenate([g_gates.reshape(count, gate_rows, fold), g_small], axis=1)
    total_rows = -(-g_packed.shape[1] // 32) * 32
    g_packed = jnp.pad(g_packed, ((0, 0), (0, total_rows - g_packed.shape[1]), (0, 0)))
    in_hop.append(g_in_ring.last)
    g_in_ring.hop()
    in_hop.append(g_in_ring.last)
    g_down = g_down.astype(F32)
    d_h_one.total(*in_hop[1], g_down)
    g_out.hop()
    g_in_ring.hop()
    g_packed_ring = Scatter(ring, lambda k, *t: after(g_packed, *in_hop[2])[k], free=True)
    for _ in range(4):
        g_packed_ring.hop()
    (inputs_grad,) = sum_call(
        functools.partial(norm_one_whole_kernel), n_pieces, where, d_h_one, inputs, after(gain_one, *in_hop[2]),
        (d_attn,), (F32,)
    )
    if not aligned:
        inputs_grad = move(inputs_grad, ring_of)

    g_in_own = g_in_ring.result()
    g_in_gate, g_in_rec = g_in_own[:, :channels], g_in_own[:, channels:]
    keep_half = jnp.where(br == 0, g_in_gate, g_in_rec)
    send_half = jnp.where(br == 0, g_in_rec, g_in_gate).astype(BF16)
    got_half = lax.ppermute(send_half, "br", SWAP).astype(F32)
    g_in = jnp.concatenate(
        [jnp.where(br == 0, keep_half, got_half), jnp.where(br == 0, got_half, keep_half)], axis=1
    )
    g_mlp_own = g_mlp.result()
    g_gate_own, g_up_own = g_mlp_own[:, :hidden_units], g_mlp_own[:, hidden_units:]
    w_gate = jnp.where(br == 0, own_cols, far_cols).astype(F32)
    w_rec = jnp.where(br == 0, far_cols, own_cols).astype(F32)
    gains = jnp.stack(
        [
            jnp.sum(g_in_gate * w_gate, axis=1) + jnp.sum(g_in_rec * w_rec, axis=1),
            jnp.sum(g_gate_own * mlp_in[0].astype(F32), axis=1)
            + jnp.sum(g_up_own * mlp_in[1].astype(F32), axis=1),
        ]
    )
    gains = gains + after(lax.ppermute(gains, "ch", SWAP), inputs_grad)
    gains = gains + lax.ppermute(gains, "br", SWAP)
    g_own = g_packed_ring.result()
    g_gate_w = g_own[:gate_rows].reshape(heads, part_in, 2, block).transpose(2, 0, 1, 3)[:, None, None]
    g_flat = g_own[gate_rows : gate_rows + g_rows].reshape(-1)
    g_chan = g_flat[: (taps + 5) * part_ch].reshape(taps + 5, part_ch)
    return (
        output,
        inputs_grad,
        gains[0] / norm_gain1.astype(F32),
        g_in[None],
        g_chan[:taps][:, None, None],
        g_chan[taps][None, None],
        g_gate_w,
        g_chan[taps + 1 : taps + 3][:, None, None],
        g_chan[taps + 3][None, None],
        g_out.result()[None, None],
        gains[1] / norm_gain2.astype(F32),
        jnp.stack([g_gate_own, g_up_own]),
        g_down.astype(F32),
        g_chan[taps + 4][None, None] / (tokens * count),
    )


def solution(mesh):
    placed = (
        P("seq", None),
        P(),
        P("seq"),
        P("br", "seq", "ch"),
        P(None, "ch", "br", "seq"),
        P("ch", "br", "seq"),
        P(None, "ch", "br", None, "seq", None),
        P(None, "ch", "br", "seq"),
        P("ch", "br", "seq"),
        P("ch", "br", None, "seq"),
        P("seq"),
        P(None, "seq", ("br", "ch")),
        P(("br", "ch"), "seq"),
        P("seq", None),
    )
    return jax.shard_map(
        per_device,
        mesh=mesh,
        in_specs=placed,
        out_specs=(
            P("seq", ("br", "ch")),
            P("seq", None),
            P("seq"),
            P("br", "seq", "ch"),
            P(None, "ch", "br", "seq"),
            P("ch", "br", "seq"),
            P(None, "ch", "br", None, "seq", None),
            P(None, "ch", "br", "seq"),
            P("ch", "br", "seq"),
            P("ch", "br", None, "seq"),
            P("seq"),
            P(None, "seq", ("br", "ch")),
            P(("br", "ch"), "seq"),
            P("ch", "br", "seq"),
        ),
        check_vma=False,
    )
```
